32 devices in a mesh: samp: 16 (over z, y, core), blk: 2 (over x).
Axes of the slice: x: 2, y: 2, z: 4, core: 2. Of those that a mesh axis runs over, the one named last changes fastest.
Arguments:
- genotypes: int32 [65536, 2048], P('samp', 'blk'), may hold values from 0 to 2
- traits: bfloat16 [65536, 64], P('samp'), may hold values from -6 to 6
- penalty_index: int32 [5], replicated, may hold values from 0 to 9
Outputs:
- level_gram: float32 [64, 10, 10], P('blk')
- level_cross: float32 [64, 10], P('blk')
The draws below stay inside these ranges and needn't reach their ends.
All inputs are finite; a program needn't handle non-finite values.
Results may differ from the reference program's by a relative error of at most 0.0004.
Values may be sent and summed in bfloat16 or wider, within the bound.
No kernel may reach another device: no remote copies, remote signals or barrier semaphores. Data moves between devices by JAX's collectives and lax.ppermute only.
A program may use at most 192 MiB of HBM per device.

```python
import jax
import jax.numpy as jnp
from jax import lax

BLOCK_VARS = 1024
TRAITS = 64
PEN = 5
BLOCKS = 2
VARIANTS = 2048
SAMPLES = 65536
STACK = 10


def draw_genotypes(key, part):
    key = jax.random.fold_in(key, 11)
    level_key, walk_key = jax.random.split(key)
    threshold = jax.random.randint(level_key, (VARIANTS,), 6, 59)
    haplos = 2 * SAMPLES

    def advance(latent, column):
        step_key = jax.random.fold_in(walk_key, column)
        fresh_key, copy_key = jax.random.split(step_key)
        fresh = jax.random.randint(fresh_key, (haplos,), 0, 64)
        keep_old = (jax.random.randint(copy_key, (haplos,), 0, 10) < 9) & (column > 0)
        latent = jnp.where(keep_old, latent, fresh)
        allele = (latent < threshold[column]).astype(jnp.int32)
        dosage = allele[:SAMPLES] + allele[SAMPLES:]
        return (latent, dosage)
    start = jnp.zeros((haplos,), jnp.int32)
    ignored, columns = lax.scan(advance, start, jnp.arange(VARIANTS, dtype=jnp.int32))
    return columns.T


def with_ends(result, key, least, high):
    place = [jax.random.randint(jax.random.fold_in(key, axis), (), 0, length) for axis, length in enumerate(result.shape)]
    widest = result.shape.index(max(result.shape))
    neighbour = place[:widest] + [(place[widest] + 1) % result.shape[widest]] + place[widest + 1:]
    return result.at[tuple(place)].set(least).at[tuple(neighbour)].set(high)


def levels(own_key, extent, shards, smallest, top_value):
    level = 1.0
    for axis_at, parts in shards:
        steps = jax.random.uniform(jax.random.fold_in(jax.random.fold_in(own_key, 6), axis_at), (parts,), jnp.float32, smallest / len(shards), top_value / len(shards))
        level = level * jnp.repeat(jnp.exp(steps), extent[axis_at] // parts).reshape((-1,) + (1,) * (len(extent) - 1 - axis_at))
    return level


def centred(key, shape, scale, limit, cuts=(), kind=jnp.bfloat16):
    entries = jax.random.normal(key, shape, jnp.float32) * scale
    if len(cuts) > 0:
        entries = levels(key, shape, cuts, -0.22, 0.18) * entries
    return jnp.clip(entries, min=-limit, max=limit).astype(kind)


def setup_inputs(seed: int = 0) -> dict:
    arg_keys = jax.random.split(jax.random.key(seed), 4)
    return {
        "genotypes": draw_genotypes(jax.random.fold_in(arg_keys[3], 71), 0),
        "traits": centred(arg_keys[1], (SAMPLES, TRAITS), 1.0, 6.0, ((0, 16),)),
        "penalty_index": with_ends(jax.random.randint(arg_keys[2], (PEN,), 0, 10), jax.random.fold_in(arg_keys[2], 1), 0, 9).astype(jnp.int32),
    }


def reference(genotypes, traits, penalty_index):
    hi = lax.Precision.HIGHEST
    total = jnp.float32(SAMPLES)
    lam = total * jnp.exp2((penalty_index.astype(jnp.float32) - 8.0) / 2.0)
    ysum = lax.optimization_barrier(jnp.sum(traits, axis=0, dtype=jnp.float32))
    preds = []
    for block in range(BLOCKS):
        dosage = genotypes[:, block * BLOCK_VARS:(block + 1) * BLOCK_VARS].astype(jnp.bfloat16)
        gram = jnp.dot(dosage.T.astype(jnp.float32), dosage.astype(jnp.float32), preferred_element_type=jnp.float32)
        xty = jnp.dot(dosage.T.astype(jnp.float32), traits.astype(jnp.float32), preferred_element_type=jnp.float32)
        colsum = lax.optimization_barrier(jnp.sum(dosage, axis=0, dtype=jnp.float32))
        mean = colsum / total
        spread = jnp.sqrt(jnp.diagonal(gram) / total - mean * mean + 1e-05)
        gstd = (gram - total * mean[:, None] * mean[None, :]) / (spread[:, None] * spread[None, :])
        rhs = (xty - mean[:, None] * ysum[None, :]) / spread[:, None]
        eye = jnp.eye(BLOCK_VARS, dtype=jnp.float32)
        betas = []
        for r in range(PEN):
            factor = jnp.linalg.cholesky(gstd + lam[r] * eye)
            betas.append(jax.scipy.linalg.cho_solve((factor, True), rhs))
        beta = jnp.stack(betas)
        coef = (beta / spread[None, :, None]).astype(jnp.bfloat16)
        offset = jnp.einsum('rmt,m->rt', coef.astype(jnp.float32), mean, precision=hi)
        pred = jnp.einsum('rmt,nm->trn', coef.astype(jnp.float32), dosage.astype(jnp.float32), precision=hi)
        preds.append((pred - offset.T[:, :, None]).astype(jnp.bfloat16))
    stacked = jnp.stack(preds).astype(jnp.float32)
    level_gram = jnp.einsum('btrn,ctsn->tbrcs', stacked, stacked, precision=hi)
    level_gram = level_gram.reshape(TRAITS, STACK, STACK) / BLOCK_VARS
    level_cross = jnp.einsum('btrn,nt->tbr', stacked, traits.astype(jnp.float32), precision=hi)
    level_cross = level_cross.reshape(TRAITS, STACK) / BLOCK_VARS
    return (level_gram, level_cross)
```

```python
import functools

import jax
import jax.numpy as jnp
from jax import lax
from jax.experimental import pallas as pl
from jax.experimental.pallas import tpu as pltpu
from jax.sharding import PartitionSpec as P

BLK = 128
SUB = 8
THIRD = 24
COPIES = 3
HI = lax.Precision.HIGHEST
NT = (((1,), (1,)), ((), ()))


def dot_hi(a, b):
    return jnp.dot(a, b, precision=HI, preferred_element_type=jnp.float32)


def dot_nt(a, b):
    return lax.dot_general(a, b, NT, precision=HI, preferred_element_type=jnp.float32)


def down(row):
    return jnp.transpose(jnp.broadcast_to(row, (BLK, BLK)))


def invert_tile(tile):
    strips = [tile[SUB * i:SUB * (i + 1), :] for i in range(BLK // SUB)]
    lane = lax.broadcasted_iota(jnp.int32, (SUB, BLK), 1)
    sub = lax.broadcasted_iota(jnp.int32, (SUB, BLK), 0)
    rows_at = [sub == j for j in range(SUB)]
    for k in range(BLK // SUB):
        at = SUB * k
        inside = (lane >= at) & (lane < at + SUB)
        eye = (lane - at == sub).astype(jnp.float32)
        cols = [jnp.broadcast_to(strips[k][:, at + j:at + j + 1], (SUB, BLK)) for j in range(SUB)]
        right = jnp.where(inside, eye, strips[k])
        for j in range(SUB):
            pivot = 1.0 / jnp.broadcast_to(cols[j][j:j + 1, :], (SUB, BLK))
            step = cols[j]

            def move(x):
                top = jnp.broadcast_to(x[j:j + 1, :], (SUB, BLK)) * pivot
                return jnp.where(rows_at[j], top, x - step * top)

            cols = cols[:j + 1] + [move(c) for c in cols[j + 1:]]
            right = move(right)
        tops = [jnp.broadcast_to(right[j:j + 1, :], (SUB, BLK)) for j in range(SUB)]
        fresh = []
        for i in range(BLK // SUB):
            if i == k:
                fresh.append(right)
                continue
            rest = jnp.where(inside, 0.0, strips[i])
            for j in range(SUB):
                rest = rest - jnp.broadcast_to(strips[i][:, at + j:at + j + 1], (SUB, BLK)) * tops[j]
            fresh.append(rest)
        strips = fresh
    return jnp.concatenate(strips, axis=0)


def solve_kernel(nsamp, ntraits, lam_ref, gram_ref, side_ref, coef_ref, aug, wide):
    nvars = gram_ref.shape[0]
    nblocks = nvars // BLK
    lam = lam_ref[0, 0]
    eye = lax.broadcasted_iota(jnp.int32, (BLK, BLK), 0) == lax.broadcasted_iota(jnp.int32, (BLK, BLK), 1)
    means, scales, means_down, scales_down = [], [], [], []
    for i in range(nblocks):
        span = slice(BLK * i, BLK * (i + 1))
        diag = jnp.sum(jnp.where(eye, gram_ref[span, span], 0.0), axis=0, keepdims=True)
        mean = side_ref[ntraits:ntraits + 1, span] / nsamp
        scale = 1.0 / jnp.sqrt(diag / nsamp - mean * mean + 1e-05)
        means.append(mean)
        scales.append(scale)
        means_down.append(down(mean))
        scales_down.append(down(scale))
    ysum = down(side_ref[ntraits + 1:ntraits + 2, 0:BLK])[0:ntraits, :]
    for j in range(nblocks):
        span = slice(BLK * j, BLK * (j + 1))
        for i in range(j, nblocks):
            rows = slice(BLK * i, BLK * (i + 1))
            value = gram_ref[rows, span] - nsamp * means_down[i] * means[j]
            value = value * (scales_down[i] * scales[j])
            if i == j:
                value = value + jnp.where(eye, lam, 0.0)
            aug[rows, span] = value
        aug[nvars:nvars + ntraits, span] = (side_ref[0:ntraits, span] - ysum * means[j]) * scales[j]
    end = nvars + ntraits

    def eliminate(k, carry):
        at = pl.multiple_of(k * BLK, BLK)
        inverse = invert_tile(aug[pl.ds(at, BLK), pl.ds(at, BLK)])
        for step in range(nblocks):
            @pl.when(k == step)
            def _(step=step):
                span = slice(BLK * step, BLK * (step + 1))
                low = BLK * (step + 1)
                panel = aug[low:end, span]
                mult = dot_hi(panel, inverse)
                wide[low:end, span] = mult
                for j in range(step + 1, nblocks):
                    top = BLK * j
                    aug[top:end, top:top + BLK] -= dot_nt(mult[top - low:, :], aug[top:top + BLK, span])
        return carry

    lax.fori_loop(0, nblocks, eliminate, 0)
    found = wide[nvars:end, nvars - BLK:nvars]
    solved = found
    parts = {nblocks - 1: found}
    for k in range(nblocks - 2, -1, -1):
        span = slice(BLK * k, BLK * (k + 1))
        found = wide[nvars:end, span] - dot_hi(solved, wide[BLK * (k + 1):nvars, span])
        parts[k] = found
        solved = jnp.concatenate([found, solved], axis=1)
    pad = coef_ref.shape[0] - ntraits
    for k in range(nblocks):
        span = slice(BLK * k, BLK * (k + 1))
        coef_ref[0:ntraits, span] = (parts[k] * scales[k]).astype(jnp.bfloat16)
        if pad > 0:
            coef_ref[ntraits:ntraits + pad, span] = jnp.zeros((pad, BLK), jnp.bfloat16)


def solve(gram, side, lam, nsamp, ntraits):
    nvars = gram.shape[0]
    return pl.pallas_call(
        functools.partial(solve_kernel, nsamp, ntraits),
        out_shape=jax.ShapeDtypeStruct((COPIES * THIRD, nvars), jnp.bfloat16),
        in_specs=[
            pl.BlockSpec(memory_space=pltpu.SMEM),
            pl.BlockSpec(memory_space=pltpu.VMEM),
            pl.BlockSpec(memory_space=pltpu.VMEM),
        ],
        out_specs=pl.BlockSpec(memory_space=pltpu.VMEM),
        scratch_shapes=[
            pltpu.VMEM((nvars + ntraits, nvars), jnp.float32),
            pltpu.VMEM((nvars + ntraits, nvars), jnp.float32),
        ],
        compiler_params=pltpu.CompilerParams(vmem_limit_bytes=48 * 1024 * 1024),
        cost_estimate=pl.CostEstimate(flops=100 * 10**9, bytes_accessed=200 * 10**6, transcendentals=0),
        name="ridge_solve",
    )(lam, gram, side)


def two_parts(value):
    first = value.astype(jnp.bfloat16)
    return first, (value - first.astype(jnp.float32)).astype(jnp.bfloat16)


def forms_kernel(nsamp, ntraits, npen, coef_ref, gram_ref, side_ref, cross_ref, out_ref, own, prod):
    nvars = gram_ref.shape[0]
    nblocks = nvars // BLK
    rank = lax.axis_index("blk")
    rows = COPIES * THIRD
    col_row = side_ref[ntraits:ntraits + 1, :]
    mean_own = col_row / nsamp
    mean_0 = cross_ref[nvars:nvars + 1, :] / nsamp
    mean_1 = cross_ref[nvars + 1:nvars + 2, :] / nsamp

    def at(r, q, b):
        return coef_ref[q * npen + r, b]

    def sheet(r, b):
        return jnp.concatenate([at(r, q, b) for q in range(COPIES)], axis=0)

    lane = lax.broadcasted_iota(jnp.int32, (rows, BLK), 1)
    acc = jnp.zeros((rows, BLK), jnp.float32)
    for r in range(npen):
        own[rows * r:rows * (r + 1), :] = jnp.concatenate([coef_ref[q * npen + r, rank] for q in range(COPIES)], axis=0).astype(jnp.float32)
    stack = own[...].astype(jnp.bfloat16)
    for j in range(0, nvars, 2 * BLK):
        span = slice(j, j + 2 * BLK)
        for i in range(0, nvars, 2 * BLK):
            tall = slice(i, i + 2 * BLK)
            down_mean = jnp.concatenate([down(mean_own[:, i:i + BLK]), down(mean_own[:, i + BLK:i + 2 * BLK])], axis=0)
            down_mean = jnp.concatenate([down_mean, down_mean], axis=1)
            value = gram_ref[tall, span] - nsamp * down_mean * mean_own[:, span]
            hi, lo = two_parts(value)
            part = jnp.dot(stack[:, tall], hi, preferred_element_type=jnp.float32)
            part = part + jnp.dot(stack[:, tall], lo, preferred_element_type=jnp.float32)
            if i == 0:
                prod[:, span] = part
            else:
                prod[:, span] += part
    place = 0
    for r in range(npen):
        for s in range(npen):
            if s < r:
                place += 1
                continue
            term = jnp.sum(prod[rows * r:rows * (r + 1), :] * own[rows * s:rows * (s + 1), :], axis=1, keepdims=True)
            acc = jnp.where((lane == place) | (lane == s * npen + r), term, acc)
            place += 1
    ysum = down(side_ref[ntraits + 1:ntraits + 2, 0:BLK])[0:ntraits, 0:1]
    target = side_ref[0:ntraits, :] - ysum * mean_own
    for r in range(npen):
        term = jnp.sum(own[rows * r:rows * r + ntraits, :] * target, axis=1, keepdims=True)
        term = jnp.concatenate([term, jnp.zeros((rows - ntraits, 1), jnp.float32)], axis=0)
        acc = jnp.where(lane == 2 * npen * npen + r, term, acc)
    for r in range(npen):
        own[rows * r:rows * (r + 1), :] = sheet(r, 1).astype(jnp.float32)
    stack = jnp.concatenate([sheet(r, 0) for r in range(npen)], axis=0)
    for j in range(0, nvars, 2 * BLK):
        span = slice(j, j + 2 * BLK)
        for i in range(0, nvars, 2 * BLK):
            tall = slice(i, i + 2 * BLK)
            down_mean = jnp.concatenate([down(mean_0[:, i:i + BLK]), down(mean_0[:, i + BLK:i + 2 * BLK])], axis=0)
            down_mean = jnp.concatenate([down_mean, down_mean], axis=1)
            value = cross_ref[tall, span] - nsamp * down_mean * mean_1[:, span]
            hi, lo = two_parts(value)
            part = jnp.dot(stack[:, tall], hi, preferred_element_type=jnp.float32)
            part = part + jnp.dot(stack[:, tall], lo, preferred_element_type=jnp.float32)
            if i == 0:
                prod[:, span] = part
            else:
                prod[:, span] += part
    place = npen * npen
    for r in range(npen):
        for s in range(npen):
            term = jnp.sum(prod[rows * r:rows * (r + 1), :] * own[rows * s:rows * (s + 1), :], axis=1, keepdims=True)
            acc = jnp.where(lane == place, term, acc)
            place += 1
    out_ref[...] = acc


def forms(coefs, gram, side, cross, nsamp, ntraits, npen):
    nvars = gram.shape[0]
    rows = COPIES * THIRD
    return pl.pallas_call(
        functools.partial(forms_kernel, nsamp, ntraits, npen),
        out_shape=jax.ShapeDtypeStruct((rows, BLK), jnp.float32),
        in_specs=[pl.BlockSpec(memory_space=pltpu.VMEM)] * 4,
        out_specs=pl.BlockSpec(memory_space=pltpu.VMEM),
        scratch_shapes=[
            pltpu.VMEM((npen * rows, nvars), jnp.float32),
            pltpu.VMEM((npen * rows, nvars), jnp.float32),
        ],
        compiler_params=pltpu.CompilerParams(vmem_limit_bytes=48 * 1024 * 1024),
        name="level_forms",
    )(coefs, gram, side, cross)


def sides(dosage, traits):
    ones = jnp.ones((traits.shape[0], 1), traits.dtype)
    pad = jnp.zeros((traits.shape[0], SUB - 1), traits.dtype)
    with_ones = jnp.concatenate([traits, ones, pad], axis=1)
    side = jnp.einsum("nt,nm->tm", with_ones, dosage, preferred_element_type=jnp.float32)
    ysum = jnp.sum(traits, axis=0, dtype=jnp.float32)
    ysum = jnp.pad(ysum, (0, dosage.shape[1] - ysum.shape[0]))
    return lax.dynamic_update_slice(side, ysum[None, :], (traits.shape[1] + 1, 0))


def gathered_order(coefs, npen, ntraits):
    coefs = coefs[:COPIES * npen].reshape(COPIES, npen, THIRD, coefs.shape[-1])
    coefs = coefs.transpose(1, 0, 2, 3).reshape(npen, COPIES * THIRD, coefs.shape[-1])
    return coefs[:, :ntraits]


def level_from_predictions(coefs, mean, dosage, traits, nvars):
    coef = coefs.transpose(0, 2, 1)
    ntraits = traits.shape[1]
    offset = jnp.einsum("rmt,m->rt", coef.astype(jnp.float32), mean, precision=HI)
    pred = jnp.einsum("rmt,nm->trn", coef, dosage, preferred_element_type=jnp.float32)
    pred = (pred - offset.T[:, :, None]).astype(jnp.bfloat16)
    local_traits = ntraits // lax.axis_size("blk")
    parts = lax.all_to_all(pred[None], "blk", split_axis=1, concat_axis=0, tiled=True)
    mine = lax.dynamic_slice_in_dim(traits, lax.axis_index("blk") * local_traits, local_traits, 1)
    gram = jnp.einsum("btrn,ctsn->tbrcs", parts, parts, preferred_element_type=jnp.float32)
    cross = jnp.einsum("btrn,nt->tbr", parts, mine, preferred_element_type=jnp.float32)
    count, stack = parts.shape[1], parts.shape[0] * parts.shape[2]
    gram, cross = lax.psum((gram.reshape(count, stack, stack), cross.reshape(count, stack)), "samp")
    return gram / nvars, cross / nvars


def local(genotypes, traits, penalty_index):
    dosage = genotypes.astype(jnp.bfloat16)
    count, nvars = dosage.shape
    ntraits = traits.shape[1]
    npen = penalty_index.shape[0]
    nblk = lax.axis_size("blk")
    nsamp = float(count * lax.axis_size("samp"))
    samp_rank = lax.axis_index("samp")
    blk_rank = lax.axis_index("blk")
    paired = nblk == 2
    if paired:
        half = count // 2
        sent = lax.dynamic_slice_in_dim(dosage, (1 - blk_rank) * half, half, 0)
        kept = lax.dynamic_slice_in_dim(dosage, blk_rank * half, half, 0)
        other = lax.ppermute(sent, "blk", [(0, 1), (1, 0)])
    gram = jnp.einsum("nm,nk->mk", dosage, dosage, preferred_element_type=jnp.float32)
    sums = lax.psum(jnp.concatenate([gram, sides(dosage, traits)], axis=0), "samp")
    gram, side = sums[:nvars], sums[nvars:]
    lam = nsamp * jnp.exp2((penalty_index.astype(jnp.float32) - 8.0) / 2.0)
    mine = lax.dynamic_index_in_dim(lam, samp_rank % npen, 0, keepdims=True).reshape(1, 1)
    coef = solve(gram, side, mine, nsamp, ntraits)
    third = lax.dynamic_slice_in_dim(coef, jnp.minimum(samp_rank // npen, COPIES - 1) * THIRD, THIRD, 0)
    if not paired:
        coefs = lax.all_gather(third, "samp")
        mean = side[ntraits] / nsamp
        return level_from_predictions(gathered_order(coefs, npen, ntraits), mean, dosage, traits, nvars)
    cross = jnp.einsum("nm,nk->mk", kept, other, preferred_element_type=jnp.float32)
    cross = jnp.where(blk_rank == 0, cross, cross.T)
    colsum = jnp.sum(dosage, axis=0, dtype=jnp.float32)
    tail = jnp.where(lax.broadcasted_iota(jnp.int32, (SUB, nvars), 0) == blk_rank, colsum[None, :], 0.0)
    cross = lax.psum(jnp.concatenate([cross, tail], axis=0), ("samp", "blk"))
    coefs = lax.all_gather(third, ("samp", "blk"))
    coefs = coefs.reshape(lax.axis_size("samp"), nblk, THIRD, nvars)
    found = forms(coefs, gram, side, cross, nsamp, ntraits, npen)[:ntraits] / nvars
    each = ntraits // nblk
    mixed = found[:, npen * npen:2 * npen * npen]
    mixed = lax.dynamic_slice_in_dim(mixed, blk_rank * each, each, 0).reshape(each, npen, npen)
    own = jnp.concatenate([found[:, :npen * npen], found[:, 2 * npen * npen:2 * npen * npen + npen]], axis=1)
    own = lax.all_to_all(own, "blk", split_axis=0, concat_axis=0, tiled=True)
    square = own[:, :npen * npen].reshape(nblk, each, npen, npen)
    upper = jnp.concatenate([square[0], mixed], axis=2)
    lower = jnp.concatenate([mixed.transpose(0, 2, 1), square[1]], axis=2)
    level_cross = own[:, npen * npen:].reshape(nblk, each, npen).transpose(1, 0, 2).reshape(each, nblk * npen)
    return jnp.concatenate([upper, lower], axis=1), level_cross


def solution(mesh):
    placed = (P("samp", "blk"), P("samp", None), P())
    return jax.shard_map(
        local,
        mesh=mesh,
        in_specs=placed,
        out_specs=(P("blk", None, None), P("blk", None)),
        check_vma=False,
    )
```

```python
import functools

import jax
import jax.numpy as jnp
from jax import lax
from jax.experimental import pallas as pl
from jax.experimental.pallas import tpu as pltpu
from jax.sharding import PartitionSpec as P

BLK = 128
SUB = 8
GROUP = 8
HI = lax.Precision.HIGHEST
NT = (((1,), (1,)), ((), ()))
TN = (((0,), (0,)), ((), ()))


def dot_hi(a, b):
    return jnp.dot(a, b, precision=HI, preferred_element_type=jnp.float32)


def dot_nt(a, b):
    return lax.dot_general(a, b, NT, precision=HI, preferred_element_type=jnp.float32)


def panel_rows(nvars):
    starts = [0]
    for j in range(nvars // BLK):
        starts.append(starts[-1] + nvars - BLK * j)
    return starts[:-1], starts[-1]


def side_rows(ntraits):
    return ntraits + SUB


def down(row):
    return jnp.transpose(jnp.broadcast_to(row, (BLK, BLK)))


def invert_tile(tile):
    strips = [tile[SUB * i:SUB * (i + 1), :] for i in range(BLK // SUB)]
    lane = lax.broadcasted_iota(jnp.int32, (SUB, BLK), 1)
    sub = lax.broadcasted_iota(jnp.int32, (SUB, BLK), 0)
    rows_at = [sub == j for j in range(SUB)]
    for k in range(BLK // SUB):
        at = SUB * k
        inside = (lane >= at) & (lane < at + SUB)
        eye = (lane - at == sub).astype(jnp.float32)
        cols = [jnp.broadcast_to(strips[k][:, at + j:at + j + 1], (SUB, BLK)) for j in range(SUB)]
        right = jnp.where(inside, eye, strips[k])
        for j in range(SUB):
            pivot = 1.0 / jnp.broadcast_to(cols[j][j:j + 1, :], (SUB, BLK))
            step = cols[j]

            def move(x):
                top = jnp.broadcast_to(x[j:j + 1, :], (SUB, BLK)) * pivot
                return jnp.where(rows_at[j], top, x - step * top)

            cols = cols[:j + 1] + [move(c) for c in cols[j + 1:]]
            right = move(right)
        tops = [jnp.broadcast_to(right[j:j + 1, :], (SUB, BLK)) for j in range(SUB)]
        fresh = []
        for i in range(BLK // SUB):
            if i == k:
                fresh.append(right)
                continue
            rest = jnp.where(inside, 0.0, strips[i])
            for j in range(SUB):
                rest = rest - jnp.broadcast_to(strips[i][:, at + j:at + j + 1], (SUB, BLK)) * tops[j]
            fresh.append(rest)
        strips = fresh
    return jnp.concatenate(strips, axis=0)


def gram_kernel(ntraits, rank_ref, geno_ref, traits_ref, packed_ref, sent_ref, kept_ref, side, *panels):
    nvars = geno_ref.shape[1]
    step = pl.program_id(0)
    half = pl.num_programs(0) // 2
    wide = 2 * BLK

    @pl.when(step == 0)
    def _():
        side[...] = jnp.zeros_like(side)
        for panel in panels:
            panel[...] = jnp.zeros_like(panel)

    dosage = geno_ref[...].astype(jnp.float32).astype(jnp.bfloat16)

    @pl.when(step < half)
    def _():
        sent_ref[...] = dosage

    @pl.when(step >= half)
    def _():
        kept_ref[...] = dosage

    turned = jnp.transpose(dosage)
    for j, panel in enumerate(panels):
        panel[...] += jnp.dot(turned[wide * j:, :], dosage[:, wide * j:wide * (j + 1)], preferred_element_type=jnp.float32)
    traits = traits_ref[...]
    side[0:ntraits, :] += lax.dot_general(traits, dosage, TN, preferred_element_type=jnp.float32)
    ones = jnp.ones((SUB, dosage.shape[0]), jnp.bfloat16)
    sums = jnp.dot(ones, dosage, preferred_element_type=jnp.float32)
    ysum = jnp.dot(ones, traits, preferred_element_type=jnp.float32)
    ysum = jnp.concatenate([ysum, jnp.zeros((SUB, BLK - ntraits), jnp.float32)], axis=1)
    ysum = jnp.concatenate([ysum, jnp.zeros((SUB, nvars - BLK), jnp.float32)], axis=1)
    row = lax.broadcasted_iota(jnp.int32, (SUB, nvars), 0)
    side[ntraits:ntraits + SUB, :] += jnp.where(row == 0, sums, jnp.where(row == 1, ysum, 0.0))

    @pl.when(step == pl.num_programs(0) - 1)
    def _():
        starts, low = panel_rows(nvars)
        for j, start in enumerate(starts):
            panel = panels[j // 2]
            skip = BLK * (j % 2)
            packed_ref[start:start + nvars - BLK * j, :] = panel[skip:, skip:skip + BLK]
        tall = side_rows(ntraits)
        for j in range(nvars // BLK):
            packed_ref[low + tall * j:low + tall * (j + 1), :] = side[:, BLK * j:BLK * (j + 1)]


def gram(genotypes, traits, rank):
    count, nvars = genotypes.shape
    ntraits = traits.shape[1]
    steps = 8
    tile = count // steps
    half = steps // 2
    low = panel_rows(nvars)[1]
    total = low + side_rows(ntraits) * (nvars // BLK)

    def source(i, rank_ref):
        return (lax.rem(i + half * (1 - rank_ref[0]), steps), 0)

    halves = jax.ShapeDtypeStruct((count // 2, nvars), jnp.bfloat16)
    return pl.pallas_call(
        functools.partial(gram_kernel, ntraits),
        grid_spec=pltpu.PrefetchScalarGridSpec(
            num_scalar_prefetch=1,
            grid=(steps,),
            in_specs=[pl.BlockSpec((tile, nvars), source), pl.BlockSpec((tile, ntraits), source)],
            out_specs=[
                pl.BlockSpec((total, BLK), lambda i, rank_ref: (0, 0)),
                pl.BlockSpec((tile, nvars), lambda i, rank_ref: (jnp.minimum(i, half - 1), 0)),
                pl.BlockSpec((tile, nvars), lambda i, rank_ref: (jnp.maximum(i - half, 0), 0)),
            ],
            scratch_shapes=[pltpu.VMEM((side_rows(ntraits), nvars), jnp.float32)]
            + [pltpu.VMEM((nvars - 2 * BLK * j, 2 * BLK), jnp.float32) for j in range(nvars // (2 * BLK))],
        ),
        out_shape=[jax.ShapeDtypeStruct((total, BLK), jnp.float32), halves, halves],
        compiler_params=pltpu.CompilerParams(vmem_limit_bytes=48 * 1024 * 1024),
        name="gram_sums",
    )(rank.reshape(1), genotypes, traits)


def solve_kernel(nsamp, ntraits, lam_ref, packed_ref, coef_ref, aug, wide):
    nvars = coef_ref.shape[1]
    nblocks = nvars // BLK
    starts, low = panel_rows(nvars)
    tall = side_rows(ntraits)
    lam = lam_ref[0, 0]
    eye = lax.broadcasted_iota(jnp.int32, (BLK, BLK), 0) == lax.broadcasted_iota(jnp.int32, (BLK, BLK), 1)
    sides = [packed_ref[low + tall * j:low + tall * (j + 1), :] for j in range(nblocks)]
    means = [side[ntraits:ntraits + 1, :] / nsamp for side in sides]
    means_down = [down(mean) for mean in means]
    ysum = down(sides[0][ntraits + 1:ntraits + 2, :])[0:ntraits, :]
    for j in range(nblocks):
        span = slice(BLK * j, BLK * (j + 1))
        for i in range(j, nblocks):
            at = starts[j] + BLK * (i - j)
            value = packed_ref[at:at + BLK, :] - nsamp * means_down[i] * means[j]
            if i == j:
                value = value + jnp.where(eye, lam * (value / nsamp + 1e-05), 0.0)
            aug[BLK * i:BLK * (i + 1), span] = value
        aug[nvars:nvars + ntraits, span] = sides[j][0:ntraits, :] - ysum * means[j]
    end = nvars + ntraits

    def eliminate(k, carry):
        at = pl.multiple_of(k * BLK, BLK)
        inverse = invert_tile(aug[pl.ds(at, BLK), pl.ds(at, BLK)])
        for step in range(nblocks):
            @pl.when(k == step)
            def _(step=step):
                span = slice(BLK * step, BLK * (step + 1))
                first = BLK * (step + 1)
                mult = dot_hi(aug[first:end, span], inverse)
                wide[first:end, span] = mult
                for j in range(step + 1, nblocks):
                    top = BLK * j
                    aug[top:end, top:top + BLK] -= dot_nt(mult[top - first:, :], aug[top:top + BLK, span])
        return carry

    lax.fori_loop(0, nblocks, eliminate, 0)
    solved = wide[nvars:end, nvars - BLK:nvars]
    coef_ref[:, nvars - BLK:nvars] = solved.astype(jnp.bfloat16)
    for k in range(nblocks - 2, -1, -1):
        span = slice(BLK * k, BLK * (k + 1))
        found = wide[nvars:end, span] - dot_hi(solved, wide[BLK * (k + 1):nvars, span])
        coef_ref[:, span] = found.astype(jnp.bfloat16)
        solved = jnp.concatenate([found, solved], axis=1)


def solve(packed, lam, nsamp, nvars, ntraits):
    return pl.pallas_call(
        functools.partial(solve_kernel, nsamp, ntraits),
        out_shape=jax.ShapeDtypeStruct((ntraits, nvars), jnp.bfloat16),
        in_specs=[pl.BlockSpec(memory_space=pltpu.SMEM), pl.BlockSpec(memory_space=pltpu.VMEM)],
        out_specs=pl.BlockSpec(memory_space=pltpu.VMEM),
        scratch_shapes=[
            pltpu.VMEM((nvars + ntraits, nvars), jnp.float32),
            pltpu.VMEM((nvars + ntraits, nvars), jnp.float32),
        ],
        compiler_params=pltpu.CompilerParams(vmem_limit_bytes=48 * 1024 * 1024),
        cost_estimate=pl.CostEstimate(flops=50 * 10**9, bytes_accessed=20 * 10**6, transcendentals=0),
        name="ridge_solve",
    )(lam, packed)


def level_kernel(npen, own_ref, other_ref, coef_ref, mean_ref, traits_ref, out_ref, pred):
    rank = lax.axis_index("blk")
    ntraits = coef_ref.shape[2]
    nvars = own_ref.shape[1]
    count = own_ref.shape[0]
    stack = 2 * npen
    tile = 512
    for place in range(2):
        block = rank if place == 0 else 1 - rank
        source = own_ref if place == 0 else other_ref
        mean = mean_ref[pl.ds(block, 1), :]
        coef = jnp.concatenate([coef_ref[r, block] for r in range(npen)], axis=0)
        offset = jnp.sum(coef.astype(jnp.float32) * mean, axis=1, keepdims=True)
        low = pl.multiple_of(block * (npen * ntraits), npen * ntraits)
        for n in range(0, count, tile):
            value = lax.dot_general(coef, source[n:n + tile, :], NT, preferred_element_type=jnp.float32)
            pred[pl.ds(low, npen * ntraits), n:n + tile] = value - offset
    for n in range(0, count, tile):
        rows = traits_ref[n:n + tile, :].astype(jnp.float32)
        rows = jnp.concatenate([rows, jnp.zeros((tile, BLK - ntraits), jnp.float32)], axis=1)
        pred[stack * ntraits:(stack + 1) * ntraits, n:n + tile] = jnp.transpose(rows)[0:ntraits, :]
    lane = lax.broadcasted_iota(jnp.int32, (SUB, BLK), 1)
    for t in range(0, ntraits, SUB):
        acc = jnp.zeros((SUB, BLK), jnp.float32)
        for i in range(stack):
            left = pred[i * ntraits + t:i * ntraits + t + SUB, :]
            for j in range(i, stack + 1):
                term = jnp.sum(left * pred[j * ntraits + t:j * ntraits + t + SUB, :], axis=1, keepdims=True)
                if j < stack:
                    acc = jnp.where((lane == i * stack + j) | (lane == j * stack + i), term, acc)
                else:
                    acc = jnp.where(lane == stack * stack + i, term, acc)
        out_ref[t:t + SUB, :] = acc


def level_sums(own, other, coefs, means, traits, npen):
    ntraits = traits.shape[1]
    count = own.shape[0]
    return pl.pallas_call(
        functools.partial(level_kernel, npen),
        out_shape=jax.ShapeDtypeStruct((ntraits, BLK), jnp.float32),
        in_specs=[pl.BlockSpec(memory_space=pltpu.VMEM)] * 5,
        out_specs=pl.BlockSpec(memory_space=pltpu.VMEM),
        scratch_shapes=[pltpu.VMEM(((2 * npen + 1) * ntraits, count), jnp.float32)],
        compiler_params=pltpu.CompilerParams(vmem_limit_bytes=56 * 1024 * 1024),
        name="level_sums",
    )(own, other, coefs, means, traits)


def level_from_predictions(coefs, mean, dosage, traits, nvars):
    coef = coefs.transpose(0, 2, 1)
    ntraits = traits.shape[1]
    offset = jnp.einsum("rmt,m->rt", coef.astype(jnp.float32), mean, precision=HI)
    pred = jnp.einsum("rmt,nm->trn", coef, dosage, preferred_element_type=jnp.float32)
    pred = (pred - offset.T[:, :, None]).astype(jnp.bfloat16)
    local_traits = ntraits // lax.axis_size("blk")
    parts = lax.all_to_all(pred[None], "blk", split_axis=1, concat_axis=0, tiled=True)
    mine = lax.dynamic_slice_in_dim(traits, lax.axis_index("blk") * local_traits, local_traits, 1)
    gram = jnp.einsum("btrn,ctsn->tbrcs", parts, parts, preferred_element_type=jnp.float32)
    cross = jnp.einsum("btrn,nt->tbr", parts, mine, preferred_element_type=jnp.float32)
    count, stack = parts.shape[1], parts.shape[0] * parts.shape[2]
    gram, cross = lax.psum((gram.reshape(count, stack, stack), cross.reshape(count, stack)), "samp")
    return gram / nvars, cross / nvars


def local(genotypes, traits, penalty_index):
    count, nvars = genotypes.shape
    ntraits = traits.shape[1]
    npen = penalty_index.shape[0]
    nblk = lax.axis_size("blk")
    members = lax.axis_size("samp")
    nsamp = float(count * members)
    samp_rank = lax.axis_index("samp")
    blk_rank = lax.axis_index("blk")
    paired = nblk == 2
    packed, sent, kept = gram(genotypes, traits, blk_rank if paired else jnp.int32(0))
    if paired:
        other = lax.ppermute(sent, "blk", [(0, 1), (1, 0)])
    sums = lax.psum(packed, "samp")
    low = panel_rows(nvars)[1]
    tall = side_rows(ntraits)
    mean = jnp.concatenate([sums[low + tall * j + ntraits] for j in range(nvars // BLK)]) / nsamp
    lam = nsamp * jnp.exp2((penalty_index.astype(jnp.float32) - 8.0) / 2.0)
    mine = lax.dynamic_index_in_dim(lam, (samp_rank % GROUP) % npen, 0, keepdims=True).reshape(1, 1)
    coef = solve(sums, mine, nsamp, nvars, ntraits)
    groups = [list(range(g, g + GROUP)) for g in range(0, members, GROUP)]
    if not paired:
        coefs = lax.all_gather(coef, "samp", axis_index_groups=groups)[:npen]
        dosage = genotypes.astype(jnp.bfloat16)
        return level_from_predictions(coefs, mean, dosage, traits, nvars)
    mean_far = lax.ppermute(mean, "blk", [(0, 1), (1, 0)])
    coef_far = lax.ppermute(coef, "blk", [(0, 1), (1, 0)])
    first = blk_rank == 0
    means = jnp.stack([jnp.where(first, mean, mean_far), jnp.where(first, mean_far, mean)])
    both = jnp.stack([jnp.where(first, coef, coef_far), jnp.where(first, coef_far, coef)])
    coefs = lax.all_gather(both, "samp", axis_index_groups=groups)
    rows = lax.dynamic_slice_in_dim(traits, blk_rank * (count // 2), count // 2, 0)
    found = level_sums(kept, other, coefs, means, rows, npen)
    stack = nblk * npen
    found = lax.psum(found, ("samp", "blk")) / nvars
    each = ntraits // nblk
    found = lax.dynamic_slice_in_dim(found, blk_rank * each, each, 0)
    return found[:, :stack * stack].reshape(each, stack, stack), found[:, stack * stack:stack * stack + stack]


def solution(mesh):
    placed = (P("samp", "blk"), P("samp", None), P())
    return jax.shard_map(
        local,
        mesh=mesh,
        in_specs=placed,
        out_specs=(P("blk", None, None), P("blk", None)),
        check_vma=False,
    )
```

```python
import functools

import jax
import jax.numpy as jnp
from jax import lax
from jax.experimental import pallas as pl
from jax.experimental.pallas import tpu as pltpu
from jax.sharding import PartitionSpec as P

BLK = 128
SUB = 8
GROUP = 8
HI = lax.Precision.HIGHEST
NT = (((1,), (1,)), ((), ()))
TN = (((0,), (0,)), ((), ()))


def dot_hi(a, b):
    return jnp.dot(a, b, precision=HI, preferred_element_type=jnp.float32)


def dot_nt(a, b):
    return lax.dot_general(a, b, NT, precision=HI, preferred_element_type=jnp.float32)


def panel_rows(nvars):
    starts = [0]
    for j in range(nvars // BLK):
        starts.append(starts[-1] + nvars - BLK * j)
    return starts[:-1], starts[-1]


def side_rows(ntraits):
    return ntraits + SUB


def down(row):
    return jnp.transpose(jnp.broadcast_to(row, (BLK, BLK)))


def inverse_of(x):
    near = pl.reciprocal(x, approx=True)
    return near * (2.0 - x * near)


def split(x):
    first = x.astype(jnp.bfloat16)
    rest = x - first.astype(jnp.float32)
    second = rest.astype(jnp.bfloat16)
    return first, second, (rest - second.astype(jnp.float32)).astype(jnp.bfloat16)


def as_left(x):
    a, b, c = split(x)
    return jnp.concatenate([a, a, b, a, b, c], axis=1)


def as_right(x, axis):
    a, b, c = split(x)
    return jnp.concatenate([a, b, a, c, b, a], axis=axis)


def invert_tile(tile):
    strips = [tile[SUB * i:SUB * (i + 1), :] for i in range(BLK // SUB)]
    lane = lax.broadcasted_iota(jnp.int32, (SUB, BLK), 1)
    sub = lax.broadcasted_iota(jnp.int32, (SUB, BLK), 0)
    rows_at = [sub == j for j in range(SUB)]
    for k in range(BLK // SUB):
        at = SUB * k
        inside = (lane >= at) & (lane < at + SUB)
        eye = (lane - at == sub).astype(jnp.float32)
        cols = [jnp.broadcast_to(strips[k][:, at + j:at + j + 1], (SUB, BLK)) for j in range(SUB)]
        right = jnp.where(inside, eye, strips[k])
        for j in range(SUB):
            pivot = inverse_of(jnp.broadcast_to(cols[j][j:j + 1, :], (SUB, BLK)))
            step = jnp.where(rows_at[j], -1.0, cols[j])

            def move(x):
                return jnp.where(rows_at[j], 0.0, x) - (step * jnp.broadcast_to(x[j:j + 1, :], (SUB, BLK))) * pivot

            cols = cols[:j + 1] + [move(c) for c in cols[j + 1:]]
            right = move(right)
        tops = [jnp.broadcast_to(right[j:j + 1, :], (SUB, BLK)) for j in range(SUB)]
        fresh = []
        for i in range(BLK // SUB):
            if i == k:
                fresh.append(right)
                continue
            rest = jnp.where(inside, 0.0, strips[i])
            for j in range(SUB):
                rest = rest - jnp.broadcast_to(strips[i][:, at + j:at + j + 1], (SUB, BLK)) * tops[j]
            fresh.append(rest)
        strips = fresh
    return jnp.concatenate(strips, axis=0)


def gram_kernel(ntraits, rank_ref, geno_ref, traits_ref, packed_ref, sent_ref, kept_ref, side, *panels):
    nvars = geno_ref.shape[1]
    step = pl.program_id(0)
    half = pl.num_programs(0) // 2
    wide = 2 * BLK

    @pl.when(step == 0)
    def _():
        side[...] = jnp.zeros_like(side)
        for panel in panels:
            panel[...] = jnp.zeros_like(panel)

    dosage = geno_ref[...].astype(jnp.float32).astype(jnp.bfloat16)

    @pl.when(step < half)
    def _():
        sent_ref[...] = dosage

    @pl.when(step >= half)
    def _():
        kept_ref[...] = dosage

    for j, panel in enumerate(panels):
        left, right = dosage[:, wide * j:], dosage[:, wide * j:wide * (j + 1)]
        panel[...] += lax.dot_general(left, right, TN, preferred_element_type=jnp.float32)
    traits = traits_ref[...]
    side[0:ntraits, :] += lax.dot_general(traits, dosage, TN, preferred_element_type=jnp.float32)
    ones = jnp.ones((SUB, dosage.shape[0]), jnp.bfloat16)
    sums = jnp.dot(ones, dosage, preferred_element_type=jnp.float32)
    ysum = jnp.dot(ones, traits, preferred_element_type=jnp.float32)
    ysum = jnp.concatenate([ysum, jnp.zeros((SUB, BLK - ntraits), jnp.float32)], axis=1)
    ysum = jnp.concatenate([ysum, jnp.zeros((SUB, nvars - BLK), jnp.float32)], axis=1)
    row = lax.broadcasted_iota(jnp.int32, (SUB, nvars), 0)
    side[ntraits:ntraits + SUB, :] += jnp.where(row == 0, sums, jnp.where(row == 1, ysum, 0.0))

    @pl.when(step == pl.num_programs(0) - 1)
    def _():
        starts, low = panel_rows(nvars)
        for j, start in enumerate(starts):
            panel = panels[j // 2]
            skip = BLK * (j % 2)
            packed_ref[start:start + nvars - BLK * j, :] = panel[skip:, skip:skip + BLK]
        tall = side_rows(ntraits)
        for j in range(nvars // BLK):
            packed_ref[low + tall * j:low + tall * (j + 1), :] = side[:, BLK * j:BLK * (j + 1)]
        used = low + tall * (nvars // BLK)
        if used < packed_ref.shape[0]:
            packed_ref[used:, :] = jnp.zeros((packed_ref.shape[0] - used, BLK), jnp.float32)


def gram(genotypes, traits, rank, members):
    count, nvars = genotypes.shape
    ntraits = traits.shape[1]
    steps = 8
    tile = count // steps
    half = steps // 2
    low = panel_rows(nvars)[1]
    share = 2 * SUB * members
    total = -(-(low + side_rows(ntraits) * (nvars // BLK)) // share) * share

    def source(i, rank_ref):
        return (lax.rem(i + half * (1 - rank_ref[0]), steps), 0)

    halves = jax.ShapeDtypeStruct((count // 2, nvars), jnp.bfloat16)
    return pl.pallas_call(
        functools.partial(gram_kernel, ntraits),
        grid_spec=pltpu.PrefetchScalarGridSpec(
            num_scalar_prefetch=1,
            grid=(steps,),
            in_specs=[pl.BlockSpec((tile, nvars), source), pl.BlockSpec((tile, ntraits), source)],
            out_specs=[
                pl.BlockSpec((total, BLK), lambda i, rank_ref: (0, 0)),
                pl.BlockSpec((tile, nvars), lambda i, rank_ref: (jnp.minimum(i, half - 1), 0)),
                pl.BlockSpec((tile, nvars), lambda i, rank_ref: (jnp.maximum(i - half, 0), 0)),
            ],
            scratch_shapes=[pltpu.VMEM((side_rows(ntraits), nvars), jnp.float32)]
            + [pltpu.VMEM((nvars - 2 * BLK * j, 2 * BLK), jnp.float32) for j in range(nvars // (2 * BLK))],
        ),
        out_shape=[jax.ShapeDtypeStruct((total, BLK), jnp.float32), halves, halves],
        compiler_params=pltpu.CompilerParams(vmem_limit_bytes=48 * 1024 * 1024),
        name="gram_sums",
    )(rank.reshape(1), genotypes, traits)


def solve_kernel(nsamp, ntraits, lam_ref, near_a, near_b, far_a, far_b, coef_ref, mean_ref, aug, wide):
    nvars = coef_ref.shape[1]
    nblocks = nvars // BLK
    starts, low = panel_rows(nvars)
    tall = side_rows(ntraits)
    lam = lam_ref[0, 0]
    lower = lax.rem(lax.axis_index("samp"), 2) == 0
    quarter = near_a.shape[0]
    pairs = [(near_a, far_a), (near_b, far_b), (far_a, near_a), (far_b, near_b)]

    def read(row, count):
        found = []
        while count > 0:
            place, at = divmod(row, quarter)
            size = min(count, quarter - at)
            even, odd = pairs[place]
            found.append(jnp.where(lower, even[at:at + size, :], odd[at:at + size, :]))
            row, count = row + size, count - size
        return found[0] if len(found) == 1 else jnp.concatenate(found, axis=0)

    eye = lax.broadcasted_iota(jnp.int32, (BLK, BLK), 0) == lax.broadcasted_iota(jnp.int32, (BLK, BLK), 1)
    sides = [read(low + tall * j, tall) for j in range(nblocks)]
    means = [side[ntraits:ntraits + 1, :] / nsamp for side in sides]
    means_down = [down(mean) for mean in means]
    ysum = down(sides[0][ntraits + 1:ntraits + 2, :])[0:ntraits, :]
    for j in range(nblocks):
        span = slice(BLK * j, BLK * (j + 1))
        mean_ref[:, span] = jnp.broadcast_to(means[j], (SUB, BLK))
        for i in range(j, nblocks):
            value = read(starts[j] + BLK * (i - j), BLK) - nsamp * means_down[i] * means[j]
            if i == j:
                value = value + jnp.where(eye, lam * (value / nsamp + 1e-05), 0.0)
            aug[BLK * i:BLK * (i + 1), span] = value
        aug[nvars:nvars + ntraits, span] = sides[j][0:ntraits, :] - ysum * means[j]
    end = nvars + ntraits
    inverse = invert_tile(aug[0:BLK, 0:BLK])
    for k in range(nblocks):
        span = slice(BLK * k, BLK * (k + 1))
        first = BLK * (k + 1)
        panel = aug[first:end, span]
        mult = jnp.dot(as_left(panel), as_right(inverse, 0), preferred_element_type=jnp.float32)
        wide[first:end, span] = mult
        if k == nblocks - 1:
            break
        left, right = as_left(mult), as_right(panel, 1)
        j = k + 1
        while j < nblocks:
            top = BLK * j
            size = BLK if j == k + 1 or j == nblocks - 1 else 2 * BLK
            at = top - first
            aug[top:end, top:top + size] -= lax.dot_general(left[at:, :], right[at:at + size, :], NT, preferred_element_type=jnp.float32)
            if j == k + 1:
                inverse = invert_tile(aug[top:top + BLK, top:top + BLK])
            j += size // BLK
    solved = wide[nvars:end, nvars - BLK:nvars]
    coef_ref[:, nvars - BLK:nvars] = solved.astype(jnp.bfloat16)
    for k in range(nblocks - 2, -1, -1):
        span = slice(BLK * k, BLK * (k + 1))
        found = wide[nvars:end, span] - dot_hi(solved, wide[BLK * (k + 1):nvars, span])
        coef_ref[:, span] = found.astype(jnp.bfloat16)
        solved = jnp.concatenate([found, solved], axis=1)


def solve(pieces, lam, nsamp, nvars, ntraits):
    return pl.pallas_call(
        functools.partial(solve_kernel, nsamp, ntraits),
        out_shape=[jax.ShapeDtypeStruct((ntraits, nvars), jnp.bfloat16), jax.ShapeDtypeStruct((SUB, nvars), jnp.float32)],
        in_specs=[pl.BlockSpec(memory_space=pltpu.SMEM)] + [pl.BlockSpec(memory_space=pltpu.VMEM)] * 4,
        out_specs=[pl.BlockSpec(memory_space=pltpu.VMEM)] * 2,
        scratch_shapes=[
            pltpu.VMEM((nvars + ntraits, nvars), jnp.float32),
            pltpu.VMEM((nvars + ntraits, nvars), jnp.float32),
        ],
        compiler_params=pltpu.CompilerParams(vmem_limit_bytes=48 * 1024 * 1024),
        cost_estimate=pl.CostEstimate(flops=50 * 10**9, bytes_accessed=20 * 10**6, transcendentals=0),
        name="ridge_solve",
    )(lam, *pieces)


def level_kernel(npen, own_ref, other_ref, coef_ref, mean_ref, far_mean_ref, traits_ref, out_ref, pred):
    rank = lax.axis_index("blk")
    ntraits = coef_ref.shape[2]
    nvars = own_ref.shape[1]
    count = own_ref.shape[0]
    stack = 2 * npen
    tile = 512
    for place in range(2):
        block = rank if place == 0 else 1 - rank
        source = own_ref if place == 0 else other_ref
        mean = (mean_ref if place == 0 else far_mean_ref)[0:1, :]
        coef = jnp.concatenate([coef_ref[r, block] for r in range(npen)], axis=0)
        offset = jnp.sum(coef.astype(jnp.float32) * mean, axis=1, keepdims=True)
        low = pl.multiple_of(block * (npen * ntraits), npen * ntraits)
        for n in range(0, count, tile):
            value = lax.dot_general(coef, source[n:n + tile, :], NT, preferred_element_type=jnp.float32)
            pred[pl.ds(low, npen * ntraits), n:n + tile] = value - offset
    for n in range(0, count, tile):
        rows = traits_ref[n:n + tile, :].astype(jnp.float32)
        rows = jnp.concatenate([rows, jnp.zeros((tile, BLK - ntraits), jnp.float32)], axis=1)
        pred[stack * ntraits:(stack + 1) * ntraits, n:n + tile] = jnp.transpose(rows)[0:ntraits, :]
    lane = lax.broadcasted_iota(jnp.int32, (SUB, BLK), 1)
    for t in range(0, ntraits, SUB):
        acc = jnp.zeros((SUB, BLK), jnp.float32)
        for i in range(stack):
            left = pred[i * ntraits + t:i * ntraits + t + SUB, :]
            for j in range(i, stack + 1):
                term = jnp.sum(left * pred[j * ntraits + t:j * ntraits + t + SUB, :], axis=1, keepdims=True)
                if j < stack:
                    acc = jnp.where((lane == i * stack + j) | (lane == j * stack + i), term, acc)
                else:
                    acc = jnp.where(lane == stack * stack + i, term, acc)
        out_ref[t:t + SUB, :] = acc


def level_sums(own, other, coefs, mean, far_mean, traits, npen):
    ntraits = traits.shape[1]
    count = own.shape[0]
    return pl.pallas_call(
        functools.partial(level_kernel, npen),
        out_shape=jax.ShapeDtypeStruct((ntraits, BLK), jnp.float32),
        in_specs=[pl.BlockSpec(memory_space=pltpu.VMEM)] * 6,
        out_specs=pl.BlockSpec(memory_space=pltpu.VMEM),
        scratch_shapes=[pltpu.VMEM(((2 * npen + 1) * ntraits, count), jnp.float32)],
        compiler_params=pltpu.CompilerParams(vmem_limit_bytes=56 * 1024 * 1024),
        name="level_sums",
    )(own, other, coefs, mean, far_mean, traits)


def swapped(x, bit):
    return lax.ppermute(x, "samp", [(i, i ^ (1 << bit)) for i in range(lax.axis_size("samp"))])


def place_bit(bit):
    return lax.rem(lax.div(lax.axis_index("samp"), 1 << bit), 2)


def halved(x, bit):
    rows = x.shape[0] // 2
    mine = place_bit(bit)
    far = swapped(lax.dynamic_slice_in_dim(x, (1 - mine) * rows, rows, 0), bit)
    return lax.dynamic_slice_in_dim(x, mine * rows, rows, 0) + far


def doubled(x, bit):
    far = swapped(x, bit)
    even = place_bit(bit) == 0
    return jnp.concatenate([jnp.where(even, x, far), jnp.where(even, far, x)], axis=0)


def all_sums(x):
    bits = list(range(1, lax.axis_size("samp").bit_length() - 1))
    x = halved(x, 0)
    rows = x.shape[0] // 2
    near = []
    for part, order in ((x[:rows], bits), (x[rows:], bits[1:] + bits[:1])):
        for bit in order:
            part = halved(part, bit)
        for bit in reversed(order):
            part = doubled(part, bit)
        near.append(part)
    return near + [swapped(part, 0) for part in near]


def small_sum(x):
    for bit in range(lax.axis_size("samp").bit_length() - 1):
        x = x + swapped(x, bit)
    return x


def level_from_predictions(coefs, mean, dosage, traits, nvars):
    coef = coefs.transpose(0, 2, 1)
    ntraits = traits.shape[1]
    offset = jnp.einsum("rmt,m->rt", coef.astype(jnp.float32), mean, precision=HI)
    pred = jnp.einsum("rmt,nm->trn", coef, dosage, preferred_element_type=jnp.float32)
    pred = (pred - offset.T[:, :, None]).astype(jnp.bfloat16)
    local_traits = ntraits // lax.axis_size("blk")
    parts = lax.all_to_all(pred[None], "blk", split_axis=1, concat_axis=0, tiled=True)
    mine = lax.dynamic_slice_in_dim(traits, lax.axis_index("blk") * local_traits, local_traits, 1)
    gram = jnp.einsum("btrn,ctsn->tbrcs", parts, parts, preferred_element_type=jnp.float32)
    cross = jnp.einsum("btrn,nt->tbr", parts, mine, preferred_element_type=jnp.float32)
    count, stack = parts.shape[1], parts.shape[0] * parts.shape[2]
    gram, cross = lax.psum((gram.reshape(count, stack, stack), cross.reshape(count, stack)), "samp")
    return gram / nvars, cross / nvars


def local(genotypes, traits, penalty_index):
    count, nvars = genotypes.shape
    ntraits = traits.shape[1]
    npen = penalty_index.shape[0]
    nblk = lax.axis_size("blk")
    members = lax.axis_size("samp")
    nsamp = float(count * members)
    samp_rank = lax.axis_index("samp")
    blk_rank = lax.axis_index("blk")
    paired = nblk == 2
    packed, sent, kept = gram(genotypes, traits, blk_rank if paired else jnp.int32(0), members)
    if paired:
        other = lax.ppermute(sent, "blk", [(0, 1), (1, 0)])
    pieces = all_sums(packed)
    lam = nsamp * jnp.exp2((penalty_index.astype(jnp.float32) - 8.0) / 2.0)
    mine = lax.dynamic_index_in_dim(lam, (samp_rank % GROUP) % npen, 0, keepdims=True).reshape(1, 1)
    coef, mean = solve(pieces, mine, nsamp, nvars, ntraits)
    groups = [list(range(g, g + GROUP)) for g in range(0, members, GROUP)]
    if not paired:
        coefs = lax.all_gather(coef, "samp", axis_index_groups=groups)[:npen]
        dosage = genotypes.astype(jnp.bfloat16)
        return level_from_predictions(coefs, mean[0], dosage, traits, nvars)
    coef_far = lax.ppermute(coef, "blk", [(0, 1), (1, 0)])
    mean_far = lax.ppermute(mean, "blk", [(0, 1), (1, 0)])
    first = blk_rank == 0
    both = jnp.stack([jnp.where(first, coef, coef_far), jnp.where(first, coef_far, coef)])
    coefs = lax.all_gather(both, "samp", axis_index_groups=groups)
    rows = lax.dynamic_slice_in_dim(traits, blk_rank * (count // 2), count // 2, 0)
    found = level_sums(kept, other, coefs, mean, mean_far, rows, npen)
    stack = nblk * npen
    each = ntraits // nblk
    far = lax.ppermute(lax.dynamic_slice_in_dim(found, (1 - blk_rank) * each, each, 0), "blk", [(0, 1), (1, 0)])
    found = small_sum(lax.dynamic_slice_in_dim(found, blk_rank * each, each, 0) + far) / nvars
    return found[:, :stack * stack].reshape(each, stack, stack), found[:, stack * stack:stack * stack + stack]


def solution(mesh):
    placed = (P("samp", "blk"), P("samp", None), P())
    return jax.shard_map(
        local,
        mesh=mesh,
        in_specs=placed,
        out_specs=(P("blk", None, None), P("blk", None)),
        check_vma=False,
    )
```

```python
import functools

import jax
import jax.numpy as jnp
from jax import lax
from jax.experimental import pallas as pl
from jax.experimental.pallas import tpu as pltpu
from jax.sharding import PartitionSpec as P

BLK = 128
SUB = 8
GROUP = 8
HI = lax.Precision.HIGHEST
NT = (((1,), (1,)), ((), ()))
TN = (((0,), (0,)), ((), ()))


def dot_hi(a, b):
    return jnp.dot(a, b, precision=HI, preferred_element_type=jnp.float32)


def dot_nt(a, b):
    return lax.dot_general(a, b, NT, precision=HI, preferred_element_type=jnp.float32)


def panel_rows(nvars):
    starts = [0]
    for j in range(nvars // BLK):
        starts.append(starts[-1] + nvars - BLK * j)
    return starts[:-1], starts[-1]


def side_rows(ntraits):
    return ntraits + SUB


def down(row):
    return jnp.transpose(jnp.broadcast_to(row, (BLK, BLK)))


def inverse_of(x):
    near = pl.reciprocal(x, approx=True)
    return near * (2.0 - x * near)


def split(x):
    first = x.astype(jnp.bfloat16)
    rest = x - first.astype(jnp.float32)
    second = rest.astype(jnp.bfloat16)
    return first, second, (rest - second.astype(jnp.float32)).astype(jnp.bfloat16)


def as_left(x):
    a, b, c = split(x)
    return jnp.concatenate([a, a, b, a, b, c], axis=1)


def as_right(x, axis):
    a, b, c = split(x)
    return jnp.concatenate([a, b, a, c, b, a], axis=axis)


def spread(x, lane):
    return jnp.broadcast_to(x[:, lane:lane + 1], (SUB, BLK))


def drop(x, row):
    return jnp.broadcast_to(x[row:row + 1, :], (SUB, BLK))


def total_of(terms):
    while len(terms) > 1:
        terms = [sum(terms[i:i + 2][1:], terms[i]) for i in range(0, len(terms), 2)]
    return terms[0]


def invert_pivots(cols, rows_at):
    for j in range(0, SUB, 2):
        a, b = drop(cols[j], j), drop(cols[j + 1], j)
        c, d = drop(cols[j], j + 1), drop(cols[j + 1], j + 1)
        scale = inverse_of(a * d - b * c)
        both = rows_at[j] | rows_at[j + 1]
        even = jnp.where(rows_at[j], -1.0, jnp.where(rows_at[j + 1], 0.0, cols[j]))
        odd = jnp.where(rows_at[j + 1], -1.0, jnp.where(rows_at[j], 0.0, cols[j + 1]))
        moved = []
        for i, x in enumerate(cols):
            if i == j:
                moved.append((odd * c - even * d) * scale)
            elif i == j + 1:
                moved.append((even * b - odd * a) * scale)
            else:
                above, below = drop(x, j), drop(x, j + 1)
                change = even * (d * above - b * below) + odd * (a * below - c * above)
                moved.append(jnp.where(both, 0.0, x) - change * scale)
        cols = moved
    return cols


def invert_tile(tile):
    count = BLK // SUB
    strips = [tile[SUB * i:SUB * (i + 1), :] for i in range(count)]
    lane = lax.broadcasted_iota(jnp.int32, (SUB, BLK), 1)
    sub = lax.broadcasted_iota(jnp.int32, (SUB, BLK), 0)
    rows_at = [sub == j for j in range(SUB)]
    cols = [spread(strips[0], j) for j in range(SUB)]
    for k in range(count):
        at = SUB * k
        inside = (lane >= at) & (lane < at + SUB)
        eye = (lane - at == sub).astype(jnp.float32)
        pivots = invert_pivots(cols, rows_at)
        own = jnp.where(inside, eye, strips[k])
        right = total_of([pivots[j] * drop(own, j) for j in range(SUB)])
        if k < count - 1:
            beside = [spread(strips[k + 1], at + j) for j in range(SUB)]
            mult = [total_of([beside[j] * drop(pivots[i], j) for j in range(SUB)]) for i in range(SUB)]
            after = []
            for j in range(SUB):
                above = spread(strips[k], at + SUB + j)
                below = spread(strips[k + 1], at + SUB + j)
                after.append(below - total_of([mult[i] * drop(above, i) for i in range(SUB)]))
            cols = after
        tops = [drop(right, j) for j in range(SUB)]
        fresh = []
        for i in range(count):
            if i == k:
                fresh.append(right)
                continue
            rest = jnp.where(inside, 0.0, strips[i])
            for j in range(SUB):
                rest = rest - spread(strips[i], at + j) * tops[j]
            fresh.append(rest)
        strips = fresh
    return jnp.concatenate(strips, axis=0)


def gram_kernel(ntraits, rank_ref, geno_ref, traits_ref, near_ref, away_ref, sent_ref, kept_ref, side, *panels):
    nvars = geno_ref.shape[1]
    step = pl.program_id(0)
    half = pl.num_programs(0) // 2
    wide = 2 * BLK

    @pl.when(step == 0)
    def _():
        side[...] = jnp.zeros_like(side)
        for panel in panels:
            panel[...] = jnp.zeros_like(panel)

    dosage = geno_ref[...].astype(jnp.float32).astype(jnp.bfloat16)

    @pl.when(step < half)
    def _():
        sent_ref[...] = dosage

    @pl.when(step >= half)
    def _():
        kept_ref[...] = dosage

    for j, panel in enumerate(panels):
        left, right = dosage[:, wide * j:], dosage[:, wide * j:wide * (j + 1)]
        panel[...] += lax.dot_general(left, right, TN, preferred_element_type=jnp.float32)
    traits = traits_ref[...]
    side[0:ntraits, :] += lax.dot_general(traits, dosage, TN, preferred_element_type=jnp.float32)
    ones = jnp.ones((SUB, dosage.shape[0]), jnp.bfloat16)
    sums = jnp.dot(ones, dosage, preferred_element_type=jnp.float32)
    ysum = jnp.dot(ones, traits, preferred_element_type=jnp.float32)
    ysum = jnp.concatenate([ysum, jnp.zeros((SUB, BLK - ntraits), jnp.float32)], axis=1)
    ysum = jnp.concatenate([ysum, jnp.zeros((SUB, nvars - BLK), jnp.float32)], axis=1)
    row = lax.broadcasted_iota(jnp.int32, (SUB, nvars), 0)
    side[ntraits:ntraits + SUB, :] += jnp.where(row == 0, sums, jnp.where(row == 1, ysum, 0.0))

    def hand_out(even, odd):
        rows = even.shape[0]

        def store(row, value):
            while value.shape[0] > 0:
                place, at = divmod(row, rows)
                size = min(value.shape[0], rows - at)
                (odd if place else even)[at:at + size, :] = value[:size, :]
                row, value = row + size, value[size:, :]

        starts, low = panel_rows(nvars)
        for j, start in enumerate(starts):
            skip = BLK * (j % 2)
            store(start, panels[j // 2][skip:, skip:skip + BLK])
        tall = side_rows(ntraits)
        for j in range(nvars // BLK):
            store(low + tall * j, side[:, BLK * j:BLK * (j + 1)])
        used = low + tall * (nvars // BLK)
        if used < 2 * rows:
            store(used, jnp.zeros((2 * rows - used, BLK), jnp.float32))

    last = step == pl.num_programs(0) - 1

    @pl.when(last & (rank_ref[1] == 0))
    def _():
        hand_out(near_ref, away_ref)

    @pl.when(last & (rank_ref[1] == 1))
    def _():
        hand_out(away_ref, near_ref)


def gram(genotypes, traits, place, members):
    count, nvars = genotypes.shape
    ntraits = traits.shape[1]
    steps = 4
    tile = count // steps
    half = steps // 2
    low = panel_rows(nvars)[1]
    share = 2 * SUB * members
    total = -(-(low + side_rows(ntraits) * (nvars // BLK)) // share) * share

    def source(i, place_ref):
        return (lax.rem(i + half * (1 - place_ref[0]), steps), 0)

    halves = jax.ShapeDtypeStruct((count // 2, nvars), jnp.bfloat16)
    return pl.pallas_call(
        functools.partial(gram_kernel, ntraits),
        grid_spec=pltpu.PrefetchScalarGridSpec(
            num_scalar_prefetch=1,
            grid=(steps,),
            in_specs=[pl.BlockSpec((tile, nvars), source), pl.BlockSpec((tile, ntraits), source)],
            out_specs=[
                pl.BlockSpec((total // 2, BLK), lambda i, rank_ref: (0, 0)),
                pl.BlockSpec((total // 2, BLK), lambda i, rank_ref: (0, 0)),
                pl.BlockSpec((tile, nvars), lambda i, rank_ref: (jnp.minimum(i, half - 1), 0)),
                pl.BlockSpec((tile, nvars), lambda i, rank_ref: (jnp.maximum(i - half, 0), 0)),
            ],
            scratch_shapes=[pltpu.VMEM((side_rows(ntraits), nvars), jnp.float32)]
            + [pltpu.VMEM((nvars - 2 * BLK * j, 2 * BLK), jnp.float32) for j in range(nvars // (2 * BLK))],
        ),
        out_shape=[jax.ShapeDtypeStruct((total // 2, BLK), jnp.float32)] * 2 + [halves, halves],
        compiler_params=pltpu.CompilerParams(vmem_limit_bytes=48 * 1024 * 1024),
        name="gram_sums",
    )(place, genotypes, traits)


def solve_kernel(nsamp, ntraits, lam_ref, near_a, near_b, far_a, far_b, coef_ref, mean_ref, aug, wide):
    nvars = coef_ref.shape[1]
    nblocks = nvars // BLK
    starts, low = panel_rows(nvars)
    tall = side_rows(ntraits)
    lam = lam_ref[0, 0]
    lower = lax.rem(lax.axis_index("samp"), 2) == 0
    quarter = near_a.shape[0]
    pairs = [(near_a, far_a), (near_b, far_b), (far_a, near_a), (far_b, near_b)]

    def read(row, count):
        found = []
        while count > 0:
            place, at = divmod(row, quarter)
            size = min(count, quarter - at)
            even, odd = pairs[place]
            found.append(jnp.where(lower, even[at:at + size, :], odd[at:at + size, :]))
            row, count = row + size, count - size
        return found[0] if len(found) == 1 else jnp.concatenate(found, axis=0)

    eye = lax.broadcasted_iota(jnp.int32, (BLK, BLK), 0) == lax.broadcasted_iota(jnp.int32, (BLK, BLK), 1)
    sides = [read(low + tall * j, tall) for j in range(nblocks)]
    means = [side[ntraits:ntraits + 1, :] / nsamp for side in sides]
    means_down = [down(mean) for mean in means]
    ysum = down(sides[0][ntraits + 1:ntraits + 2, :])[0:ntraits, :]
    for j in range(nblocks):
        span = slice(BLK * j, BLK * (j + 1))
        mean_ref[:, span] = jnp.broadcast_to(means[j], (SUB, BLK))
        for i in range(j, nblocks):
            value = read(starts[j] + BLK * (i - j), BLK) - nsamp * means_down[i] * means[j]
            if i == j:
                value = value + jnp.where(eye, lam * (value / nsamp + 1e-05), 0.0)
            aug[BLK * i:BLK * (i + 1), span] = value
        aug[nvars:nvars + ntraits, span] = sides[j][0:ntraits, :] - ysum * means[j]
    end = nvars + ntraits
    inverse = invert_tile(aug[0:BLK, 0:BLK])
    for k in range(nblocks):
        span = slice(BLK * k, BLK * (k + 1))
        first = BLK * (k + 1)
        panel = aug[first:end, span]
        mult = jnp.dot(as_left(panel), as_right(inverse, 0), preferred_element_type=jnp.float32)
        wide[first:end, span] = mult
        if k == nblocks - 1:
            break
        left, right = as_left(mult), as_right(panel, 1)
        j = k + 1
        while j < nblocks:
            top = BLK * j
            size = BLK if j == k + 1 or j == nblocks - 1 else 2 * BLK
            at = top - first
            aug[top:end, top:top + size] -= lax.dot_general(left[at:, :], right[at:at + size, :], NT, preferred_element_type=jnp.float32)
            if j == k + 1:
                inverse = invert_tile(aug[top:top + BLK, top:top + BLK])
            j += size // BLK
    solved = wide[nvars:end, nvars - BLK:nvars]
    coef_ref[:, nvars - BLK:nvars] = solved.astype(jnp.bfloat16)
    for k in range(nblocks - 2, -1, -1):
        span = slice(BLK * k, BLK * (k + 1))
        found = wide[nvars:end, span] - dot_hi(solved, wide[BLK * (k + 1):nvars, span])
        coef_ref[:, span] = found.astype(jnp.bfloat16)
        solved = jnp.concatenate([found, solved], axis=1)


def solve(pieces, lam, nsamp, nvars, ntraits):
    return pl.pallas_call(
        functools.partial(solve_kernel, nsamp, ntraits),
        out_shape=[jax.ShapeDtypeStruct((ntraits, nvars), jnp.bfloat16), jax.ShapeDtypeStruct((SUB, nvars), jnp.float32)],
        in_specs=[pl.BlockSpec(memory_space=pltpu.SMEM)] + [pl.BlockSpec(memory_space=pltpu.VMEM)] * 4,
        out_specs=[pl.BlockSpec(memory_space=pltpu.VMEM)] * 2,
        scratch_shapes=[
            pltpu.VMEM((nvars + ntraits, nvars), jnp.float32),
            pltpu.VMEM((nvars + ntraits, nvars), jnp.float32),
        ],
        compiler_params=pltpu.CompilerParams(vmem_limit_bytes=48 * 1024 * 1024),
        cost_estimate=pl.CostEstimate(flops=10**6, bytes_accessed=10**6, transcendentals=0),
        name="ridge_solve",
    )(lam, *pieces)


def level_kernel(npen, own_ref, other_ref, coef_ref, mean_ref, far_mean_ref, traits_ref, out_ref, pred):
    rank = lax.axis_index("blk")
    ntraits = coef_ref.shape[2]
    nvars = own_ref.shape[1]
    count = own_ref.shape[0]
    stack = 2 * npen
    tile = 512
    for place in range(2):
        block = rank if place == 0 else 1 - rank
        source = own_ref if place == 0 else other_ref
        mean = (mean_ref if place == 0 else far_mean_ref)[0:1, :]
        coef = jnp.concatenate([coef_ref[r, block] for r in range(npen)], axis=0)
        offset = jnp.sum(coef.astype(jnp.float32) * mean, axis=1, keepdims=True)
        low = pl.multiple_of(block * (npen * ntraits), npen * ntraits)
        for n in range(0, count, tile):
            value = lax.dot_general(coef, source[n:n + tile, :], NT, preferred_element_type=jnp.float32)
            pred[pl.ds(low, npen * ntraits), n:n + tile] = value - offset
    for n in range(0, count, tile):
        rows = traits_ref[n:n + tile, :].astype(jnp.float32)
        rows = jnp.concatenate([rows, jnp.zeros((tile, BLK - ntraits), jnp.float32)], axis=1)
        pred[stack * ntraits:(stack + 1) * ntraits, n:n + tile] = jnp.transpose(rows)[0:ntraits, :]
    lane = lax.broadcasted_iota(jnp.int32, (SUB, BLK), 1)
    for t in range(0, ntraits, SUB):
        acc = jnp.zeros((SUB, BLK), jnp.float32)
        for i in range(stack):
            left = pred[i * ntraits + t:i * ntraits + t + SUB, :]
            for j in range(i, stack + 1):
                term = jnp.sum(left * pred[j * ntraits + t:j * ntraits + t + SUB, :], axis=1, keepdims=True)
                if j < stack:
                    acc = jnp.where((lane == i * stack + j) | (lane == j * stack + i), term, acc)
                else:
                    acc = jnp.where(lane == stack * stack + i, term, acc)
        out_ref[t:t + SUB, :] = acc


def level_sums(own, other, coefs, mean, far_mean, traits, npen):
    ntraits = traits.shape[1]
    count = own.shape[0]
    return pl.pallas_call(
        functools.partial(level_kernel, npen),
        out_shape=jax.ShapeDtypeStruct((ntraits, BLK), jnp.float32),
        in_specs=[pl.BlockSpec(memory_space=pltpu.VMEM)] * 6,
        out_specs=pl.BlockSpec(memory_space=pltpu.VMEM),
        scratch_shapes=[pltpu.VMEM(((2 * npen + 1) * ntraits, count), jnp.float32)],
        compiler_params=pltpu.CompilerParams(vmem_limit_bytes=56 * 1024 * 1024),
        name="level_sums",
    )(own, other, coefs, mean, far_mean, traits)


def swapped(x, bit):
    return lax.ppermute(x, "samp", [(i, i ^ (1 << bit)) for i in range(lax.axis_size("samp"))])


def place_bit(bit):
    return lax.rem(lax.div(lax.axis_index("samp"), 1 << bit), 2)


def halved(x, bit):
    rows = x.shape[0] // 2
    mine = place_bit(bit)
    far = swapped(lax.dynamic_slice_in_dim(x, (1 - mine) * rows, rows, 0), bit)
    return lax.dynamic_slice_in_dim(x, mine * rows, rows, 0) + far


def doubled(x, bit):
    far = swapped(x, bit)
    even = place_bit(bit) == 0
    return jnp.concatenate([jnp.where(even, x, far), jnp.where(even, far, x)], axis=0)


def all_sums(x, away):
    bits = list(range(1, lax.axis_size("samp").bit_length() - 1))
    x = x + swapped(away, 0)
    rows = x.shape[0] // 2
    near = []
    for part, order in ((x[:rows], bits), (x[rows:], bits[1:] + bits[:1])):
        for bit in order:
            part = halved(part, bit)
        for bit in reversed(order):
            part = doubled(part, bit)
        near.append(part)
    return near + [swapped(part, 0) for part in near]


def small_sum(x):
    for bit in range(lax.axis_size("samp").bit_length() - 1):
        x = x + swapped(x, bit)
    return x


def level_from_predictions(coefs, mean, dosage, traits, nvars):
    coef = coefs.transpose(0, 2, 1)
    ntraits = traits.shape[1]
    offset = jnp.einsum("rmt,m->rt", coef.astype(jnp.float32), mean, precision=HI)
    pred = jnp.einsum("rmt,nm->trn", coef, dosage, preferred_element_type=jnp.float32)
    pred = (pred - offset.T[:, :, None]).astype(jnp.bfloat16)
    local_traits = ntraits // lax.axis_size("blk")
    parts = lax.all_to_all(pred[None], "blk", split_axis=1, concat_axis=0, tiled=True)
    mine = lax.dynamic_slice_in_dim(traits, lax.axis_index("blk") * local_traits, local_traits, 1)
    gram = jnp.einsum("btrn,ctsn->tbrcs", parts, parts, preferred_element_type=jnp.float32)
    cross = jnp.einsum("btrn,nt->tbr", parts, mine, preferred_element_type=jnp.float32)
    count, stack = parts.shape[1], parts.shape[0] * parts.shape[2]
    gram, cross = lax.psum((gram.reshape(count, stack, stack), cross.reshape(count, stack)), "samp")
    return gram / nvars, cross / nvars


def local(genotypes, traits, penalty_index):
    count, nvars = genotypes.shape
    ntraits = traits.shape[1]
    npen = penalty_index.shape[0]
    nblk = lax.axis_size("blk")
    members = lax.axis_size("samp")
    nsamp = float(count * members)
    samp_rank = lax.axis_index("samp")
    blk_rank = lax.axis_index("blk")
    paired = nblk == 2
    place = jnp.stack([blk_rank if paired else jnp.int32(0), place_bit(0)])
    near, away, sent, kept = gram(genotypes, traits, place, members)
    if paired:
        other = lax.ppermute(sent, "blk", [(0, 1), (1, 0)])
    pieces = all_sums(near, away)
    lam = nsamp * jnp.exp2((penalty_index.astype(jnp.float32) - 8.0) / 2.0)
    mine = lax.dynamic_index_in_dim(lam, (samp_rank % GROUP) % npen, 0, keepdims=True).reshape(1, 1)
    coef, mean = solve(pieces, mine, nsamp, nvars, ntraits)
    groups = [list(range(g, g + GROUP)) for g in range(0, members, GROUP)]
    if not paired:
        coefs = lax.all_gather(coef, "samp", axis_index_groups=groups)[:npen]
        dosage = genotypes.astype(jnp.bfloat16)
        return level_from_predictions(coefs, mean[0], dosage, traits, nvars)
    coef_far = lax.ppermute(coef, "blk", [(0, 1), (1, 0)])
    mean_far = lax.ppermute(mean, "blk", [(0, 1), (1, 0)])
    first = blk_rank == 0
    both = jnp.stack([jnp.where(first, coef, coef_far), jnp.where(first, coef_far, coef)])
    coefs = lax.all_gather(both, "samp", axis_index_groups=groups)
    rows = lax.dynamic_slice_in_dim(traits, blk_rank * (count // 2), count // 2, 0)
    found = level_sums(kept, other, coefs, mean, mean_far, rows, npen)
    stack = nblk * npen
    each = ntraits // nblk
    far = lax.ppermute(lax.dynamic_slice_in_dim(found, (1 - blk_rank) * each, each, 0), "blk", [(0, 1), (1, 0)])
    found = small_sum(lax.dynamic_slice_in_dim(found, blk_rank * each, each, 0) + far) / nvars
    return found[:, :stack * stack].reshape(each, stack, stack), found[:, stack * stack:stack * stack + stack]


def solution(mesh):
    placed = (P("samp", "blk"), P("samp", None), P())
    return jax.shard_map(
        local,
        mesh=mesh,
        in_specs=placed,
        out_specs=(P("blk", None, None), P("blk", None)),
        check_vma=False,
    )
```

```python
import functools

import jax
import jax.numpy as jnp
from jax import lax
from jax.experimental import pallas as pl
from jax.experimental.pallas import tpu as pltpu
from jax.sharding import PartitionSpec as P

BLK = 128
SUB = 8
GROUP = 8
HI = lax.Precision.HIGHEST
NT = (((1,), (1,)), ((), ()))
TN = (((0,), (0,)), ((), ()))


def dot_hi(a, b):
    return jnp.dot(a, b, precision=HI, preferred_element_type=jnp.float32)


def dot_nt(a, b):
    return lax.dot_general(a, b, NT, precision=HI, preferred_element_type=jnp.float32)


def panel_rows(nvars):
    starts = [0]
    for j in range(nvars // BLK):
        starts.append(starts[-1] + nvars - BLK * j)
    return starts[:-1], starts[-1]


def side_rows(ntraits):
    return ntraits + SUB


def down(row):
    return jnp.transpose(jnp.broadcast_to(row, (BLK, BLK)))


def inverse_of(x):
    near = pl.reciprocal(x, approx=True)
    return near * (2.0 - x * near)


def split(x):
    first = x.astype(jnp.bfloat16)
    rest = x - first.astype(jnp.float32)
    second = rest.astype(jnp.bfloat16)
    return first, second, (rest - second.astype(jnp.float32)).astype(jnp.bfloat16)


def as_left(x):
    a, b, c = split(x)
    return jnp.concatenate([a, a, b, a, b, c], axis=1)


def as_right(x, axis):
    a, b, c = split(x)
    return jnp.concatenate([a, b, a, c, b, a], axis=axis)


def spread(x, lane):
    return jnp.broadcast_to(x[:, lane:lane + 1], (SUB, BLK))


def drop(x, row):
    return jnp.broadcast_to(x[row:row + 1, :], (SUB, BLK))


def total_of(terms):
    while len(terms) > 1:
        terms = [sum(terms[i:i + 2][1:], terms[i]) for i in range(0, len(terms), 2)]
    return terms[0]


def solve_pivots(cols, right, rows_at):
    for j in range(0, SUB, 2):
        a, b = drop(cols[j], j), drop(cols[j + 1], j)
        c, d = drop(cols[j], j + 1), drop(cols[j + 1], j + 1)
        scale = inverse_of(a * d - b * c)
        both = rows_at[j] | rows_at[j + 1]
        even = jnp.where(rows_at[j], -1.0, jnp.where(rows_at[j + 1], 0.0, cols[j]))
        odd = jnp.where(rows_at[j + 1], -1.0, jnp.where(rows_at[j], 0.0, cols[j + 1]))
        above_by = even * d - odd * c
        below_by = odd * a - even * b

        def move(x):
            change = above_by * drop(x, j) + below_by * drop(x, j + 1)
            return jnp.where(both, 0.0, x) - change * scale

        cols = cols[:j + 2] + [move(x) for x in cols[j + 2:]]
        right = move(right)
    return right


def invert_tile(tile):
    count = BLK // SUB
    strips = [tile[SUB * i:SUB * (i + 1), :] for i in range(count)]
    lane = lax.broadcasted_iota(jnp.int32, (SUB, BLK), 1)
    sub = lax.broadcasted_iota(jnp.int32, (SUB, BLK), 0)
    rows_at = [sub == j for j in range(SUB)]
    for k in range(count):
        at = SUB * k
        inside = (lane >= at) & (lane < at + SUB)
        eye = (lane - at == sub).astype(jnp.float32)
        cols = [spread(strips[k], at + j) for j in range(SUB)]
        right = solve_pivots(cols, jnp.where(inside, eye, strips[k]), rows_at)
        tops = [drop(right, j) for j in range(SUB)]
        fresh = []
        for i in range(count):
            if i == k:
                fresh.append(right)
            else:
                change = total_of([spread(strips[i], at + j) * tops[j] for j in range(SUB)])
                fresh.append(jnp.where(inside, 0.0, strips[i]) - change)
        strips = fresh
    return jnp.concatenate(strips, axis=0)


def gram_kernel(ntraits, rank_ref, geno_ref, traits_ref, near_ref, away_ref, sent_ref, kept_ref, side, *panels):
    nvars = geno_ref.shape[1]
    step = pl.program_id(0)
    half = pl.num_programs(0) // 2
    wide = 2 * BLK

    @pl.when(step == 0)
    def _():
        side[...] = jnp.zeros_like(side)
        for panel in panels:
            panel[...] = jnp.zeros_like(panel)

    dosage = geno_ref[...].astype(jnp.float32).astype(jnp.bfloat16)

    @pl.when(step < half)
    def _():
        sent_ref[...] = dosage

    @pl.when(step >= half)
    def _():
        kept_ref[...] = dosage

    for j, panel in enumerate(panels):
        left, right = dosage[:, wide * j:], dosage[:, wide * j:wide * (j + 1)]
        panel[...] += lax.dot_general(left, right, TN, preferred_element_type=jnp.float32)
    traits = traits_ref[...]
    side[0:ntraits, :] += lax.dot_general(traits, dosage, TN, preferred_element_type=jnp.float32)
    ones = jnp.ones((SUB, dosage.shape[0]), jnp.bfloat16)
    sums = jnp.dot(ones, dosage, preferred_element_type=jnp.float32)
    ysum = jnp.dot(ones, traits, preferred_element_type=jnp.float32)
    ysum = jnp.concatenate([ysum, jnp.zeros((SUB, BLK - ntraits), jnp.float32)], axis=1)
    ysum = jnp.concatenate([ysum, jnp.zeros((SUB, nvars - BLK), jnp.float32)], axis=1)
    row = lax.broadcasted_iota(jnp.int32, (SUB, nvars), 0)
    side[ntraits:ntraits + SUB, :] += jnp.where(row == 0, sums, jnp.where(row == 1, ysum, 0.0))

    def hand_out(even, odd):
        rows = even.shape[0]

        def store(row, value):
            while value.shape[0] > 0:
                place, at = divmod(row, rows)
                size = min(value.shape[0], rows - at)
                (odd if place else even)[at:at + size, :] = value[:size, :]
                row, value = row + size, value[size:, :]

        starts, low = panel_rows(nvars)
        for j, start in enumerate(starts):
            skip = BLK * (j % 2)
            store(start, panels[j // 2][skip:, skip:skip + BLK])
        tall = side_rows(ntraits)
        for j in range(nvars // BLK):
            store(low + tall * j, side[:, BLK * j:BLK * (j + 1)])
        used = low + tall * (nvars // BLK)
        if used < 2 * rows:
            store(used, jnp.zeros((2 * rows - used, BLK), jnp.float32))

    last = step == pl.num_programs(0) - 1

    @pl.when(last & (rank_ref[1] == 0))
    def _():
        hand_out(near_ref, away_ref)

    @pl.when(last & (rank_ref[1] == 1))
    def _():
        hand_out(away_ref, near_ref)


def gram(genotypes, traits, place, members):
    count, nvars = genotypes.shape
    ntraits = traits.shape[1]
    steps = 4
    tile = count // steps
    half = steps // 2
    low = panel_rows(nvars)[1]
    share = 2 * SUB * members
    total = -(-(low + side_rows(ntraits) * (nvars // BLK)) // share) * share

    def source(i, place_ref):
        return (lax.rem(i + half * (1 - place_ref[0]), steps), 0)

    halves = jax.ShapeDtypeStruct((count // 2, nvars), jnp.bfloat16)
    return pl.pallas_call(
        functools.partial(gram_kernel, ntraits),
        grid_spec=pltpu.PrefetchScalarGridSpec(
            num_scalar_prefetch=1,
            grid=(steps,),
            in_specs=[pl.BlockSpec((tile, nvars), source), pl.BlockSpec((tile, ntraits), source)],
            out_specs=[
                pl.BlockSpec((total // 2, BLK), lambda i, rank_ref: (0, 0)),
                pl.BlockSpec((total // 2, BLK), lambda i, rank_ref: (0, 0)),
                pl.BlockSpec((tile, nvars), lambda i, rank_ref: (jnp.minimum(i, half - 1), 0)),
                pl.BlockSpec((tile, nvars), lambda i, rank_ref: (jnp.maximum(i - half, 0), 0)),
            ],
            scratch_shapes=[pltpu.VMEM((side_rows(ntraits), nvars), jnp.float32)]
            + [pltpu.VMEM((nvars - 2 * BLK * j, 2 * BLK), jnp.float32) for j in range(nvars // (2 * BLK))],
        ),
        out_shape=[jax.ShapeDtypeStruct((total // 2, BLK), jnp.float32)] * 2 + [halves, halves],
        compiler_params=pltpu.CompilerParams(vmem_limit_bytes=48 * 1024 * 1024),
        name="gram_sums",
    )(place, genotypes, traits)


def solve_kernel(nsamp, ntraits, lam_ref, near_a, near_b, far_a, far_b, coef_ref, mean_ref, aug, wide):
    nvars = coef_ref.shape[1]
    nblocks = nvars // BLK
    starts, low = panel_rows(nvars)
    tall = side_rows(ntraits)
    lam = lam_ref[0, 0]
    lower = lax.rem(lax.axis_index("samp"), 2) == 0
    quarter = near_a.shape[0]
    pairs = [(near_a, far_a), (near_b, far_b), (far_a, near_a), (far_b, near_b)]

    def read(row, count):
        found = []
        while count > 0:
            place, at = divmod(row, quarter)
            size = min(count, quarter - at)
            even, odd = pairs[place]
            found.append(jnp.where(lower, even[at:at + size, :], odd[at:at + size, :]))
            row, count = row + size, count - size
        return found[0] if len(found) == 1 else jnp.concatenate(found, axis=0)

    eye = lax.broadcasted_iota(jnp.int32, (BLK, BLK), 0) == lax.broadcasted_iota(jnp.int32, (BLK, BLK), 1)
    sides = [read(low + tall * j, tall) for j in range(nblocks)]
    means = [side[ntraits:ntraits + 1, :] / nsamp for side in sides]
    means_down = [down(mean) for mean in means]
    ysum = down(sides[0][ntraits + 1:ntraits + 2, :])[0:ntraits, :]
    for j in range(nblocks):
        span = slice(BLK * j, BLK * (j + 1))
        mean_ref[:, span] = jnp.broadcast_to(means[j], (SUB, BLK))
        for i in range(j, nblocks):
            value = read(starts[j] + BLK * (i - j), BLK) - nsamp * means_down[i] * means[j]
            if i == j:
                value = value + jnp.where(eye, lam * (value / nsamp + 1e-05), 0.0)
            aug[BLK * i:BLK * (i + 1), span] = value
        aug[nvars:nvars + ntraits, span] = sides[j][0:ntraits, :] - ysum * means[j]
    end = nvars + ntraits
    inverse = invert_tile(aug[0:BLK, 0:BLK])
    for k in range(nblocks):
        span = slice(BLK * k, BLK * (k + 1))
        first = BLK * (k + 1)
        panel = aug[first:end, span]
        mult = jnp.dot(as_left(panel), as_right(inverse, 0), preferred_element_type=jnp.float32)
        wide[first:end, span] = mult
        if k == nblocks - 1:
            break
        left, right = as_left(mult), as_right(panel, 1)
        j = k + 1
        while j < nblocks:
            top = BLK * j
            size = BLK if j == k + 1 or j == nblocks - 1 else 2 * BLK
            at = top - first
            aug[top:end, top:top + size] -= lax.dot_general(left[at:, :], right[at:at + size, :], NT, preferred_element_type=jnp.float32)
            if j == k + 1:
                inverse = invert_tile(aug[top:top + BLK, top:top + BLK])
            j += size // BLK
    solved = wide[nvars:end, nvars - BLK:nvars]
    coef_ref[:, nvars - BLK:nvars] = solved.astype(jnp.bfloat16)
    for k in range(nblocks - 2, -1, -1):
        span = slice(BLK * k, BLK * (k + 1))
        found = wide[nvars:end, span] - dot_hi(solved, wide[BLK * (k + 1):nvars, span])
        coef_ref[:, span] = found.astype(jnp.bfloat16)
        solved = jnp.concatenate([found, solved], axis=1)


def solve(pieces, lam, nsamp, nvars, ntraits):
    return pl.pallas_call(
        functools.partial(solve_kernel, nsamp, ntraits),
        out_shape=[jax.ShapeDtypeStruct((ntraits, nvars), jnp.bfloat16), jax.ShapeDtypeStruct((SUB, nvars), jnp.float32)],
        in_specs=[pl.BlockSpec(memory_space=pltpu.SMEM)] + [pl.BlockSpec(memory_space=pltpu.VMEM)] * 4,
        out_specs=[pl.BlockSpec(memory_space=pltpu.VMEM)] * 2,
        scratch_shapes=[
            pltpu.VMEM((nvars + ntraits, nvars), jnp.float32),
            pltpu.VMEM((nvars + ntraits, nvars), jnp.float32),
        ],
        compiler_params=pltpu.CompilerParams(vmem_limit_bytes=48 * 1024 * 1024),
        cost_estimate=pl.CostEstimate(flops=10**6, bytes_accessed=10**6, transcendentals=0),
        name="ridge_solve",
    )(lam, *pieces)


def level_kernel(npen, own_ref, halves_ref, coef_ref, mean_ref, far_mean_ref, traits_ref, out_ref, pred, other_ref, sem):
    rank = lax.axis_index("blk")
    ntraits = coef_ref.shape[2]
    nvars = own_ref.shape[1]
    count = own_ref.shape[0]
    stack = 2 * npen
    tile = 512
    fetch = pltpu.make_async_copy(halves_ref.at[1 - rank], other_ref, sem)
    fetch.start()
    for place in range(2):
        block = rank if place == 0 else 1 - rank
        if place == 1:
            fetch.wait()
        source = own_ref if place == 0 else other_ref
        mean = (mean_ref if place == 0 else far_mean_ref)[0:1, :]
        coef = jnp.concatenate([coef_ref[r, block] for r in range(npen)], axis=0)
        offset = jnp.sum(coef.astype(jnp.float32) * mean, axis=1, keepdims=True)
        low = pl.multiple_of(block * (npen * ntraits), npen * ntraits)
        for n in range(0, count, tile):
            value = lax.dot_general(coef, source[n:n + tile, :], NT, preferred_element_type=jnp.float32)
            pred[pl.ds(low, npen * ntraits), n:n + tile] = value - offset
    for n in range(0, count, tile):
        rows = traits_ref[n:n + tile, :].astype(jnp.float32)
        rows = jnp.concatenate([rows, jnp.zeros((tile, BLK - ntraits), jnp.float32)], axis=1)
        pred[stack * ntraits:(stack + 1) * ntraits, n:n + tile] = jnp.transpose(rows)[0:ntraits, :]
    lane = lax.broadcasted_iota(jnp.int32, (SUB, BLK), 1)
    for t in range(0, ntraits, SUB):
        acc = jnp.zeros((SUB, BLK), jnp.float32)
        for i in range(stack):
            left = pred[i * ntraits + t:i * ntraits + t + SUB, :]
            for j in range(i, stack + 1):
                term = jnp.sum(left * pred[j * ntraits + t:j * ntraits + t + SUB, :], axis=1, keepdims=True)
                if j < stack:
                    acc = jnp.where((lane == i * stack + j) | (lane == j * stack + i), term, acc)
                else:
                    acc = jnp.where(lane == stack * stack + i, term, acc)
        out_ref[t:t + SUB, :] = acc


def level_sums(own, halves, coefs, mean, far_mean, traits, npen):
    ntraits = traits.shape[1]
    count = own.shape[0]
    vmem = pl.BlockSpec(memory_space=pltpu.VMEM)
    return pl.pallas_call(
        functools.partial(level_kernel, npen),
        out_shape=jax.ShapeDtypeStruct((ntraits, BLK), jnp.float32),
        in_specs=[vmem, pl.BlockSpec(memory_space=pl.ANY)] + [vmem] * 4,
        out_specs=pl.BlockSpec(memory_space=pltpu.VMEM),
        scratch_shapes=[
            pltpu.VMEM(((2 * npen + 1) * ntraits, count), jnp.float32),
            pltpu.VMEM(own.shape, own.dtype),
            pltpu.SemaphoreType.DMA,
        ],
        compiler_params=pltpu.CompilerParams(vmem_limit_bytes=56 * 1024 * 1024),
        name="level_sums",
    )(own, halves, coefs, mean, far_mean, traits)


def swapped(x, bit):
    return lax.ppermute(x, "samp", [(i, i ^ (1 << bit)) for i in range(lax.axis_size("samp"))])


def place_bit(bit):
    return lax.rem(lax.div(lax.axis_index("samp"), 1 << bit), 2)


def halved(x, bit):
    rows = x.shape[0] // 2
    mine = place_bit(bit)
    far = swapped(lax.dynamic_slice_in_dim(x, (1 - mine) * rows, rows, 0), bit)
    return lax.dynamic_slice_in_dim(x, mine * rows, rows, 0) + far


def doubled(x, bit):
    far = swapped(x, bit)
    even = place_bit(bit) == 0
    return jnp.concatenate([jnp.where(even, x, far), jnp.where(even, far, x)], axis=0)


def all_sums(x, away):
    bits = list(range(1, lax.axis_size("samp").bit_length() - 1))
    x = x + swapped(away, 0)
    rows = x.shape[0] // 2
    near = []
    for part, order in ((x[:rows], bits), (x[rows:], bits[1:] + bits[:1])):
        for bit in order:
            part = halved(part, bit)
        for bit in reversed(order):
            part = doubled(part, bit)
        near.append(part)
    return near + [swapped(part, 0) for part in near]


def small_sum(x):
    for bit in range(lax.axis_size("samp").bit_length() - 1):
        x = x + swapped(x, bit)
    return x


def level_from_predictions(coefs, mean, dosage, traits, nvars):
    coef = coefs.transpose(0, 2, 1)
    ntraits = traits.shape[1]
    offset = jnp.einsum("rmt,m->rt", coef.astype(jnp.float32), mean, precision=HI)
    pred = jnp.einsum("rmt,nm->trn", coef, dosage, preferred_element_type=jnp.float32)
    pred = (pred - offset.T[:, :, None]).astype(jnp.bfloat16)
    local_traits = ntraits // lax.axis_size("blk")
    parts = lax.all_to_all(pred[None], "blk", split_axis=1, concat_axis=0, tiled=True)
    mine = lax.dynamic_slice_in_dim(traits, lax.axis_index("blk") * local_traits, local_traits, 1)
    gram = jnp.einsum("btrn,ctsn->tbrcs", parts, parts, preferred_element_type=jnp.float32)
    cross = jnp.einsum("btrn,nt->tbr", parts, mine, preferred_element_type=jnp.float32)
    count, stack = parts.shape[1], parts.shape[0] * parts.shape[2]
    gram, cross = lax.psum((gram.reshape(count, stack, stack), cross.reshape(count, stack)), "samp")
    return gram / nvars, cross / nvars


def local(genotypes, traits, penalty_index):
    count, nvars = genotypes.shape
    ntraits = traits.shape[1]
    npen = penalty_index.shape[0]
    nblk = lax.axis_size("blk")
    members = lax.axis_size("samp")
    nsamp = float(count * members)
    samp_rank = lax.axis_index("samp")
    blk_rank = lax.axis_index("blk")
    paired = nblk == 2
    place = jnp.stack([blk_rank if paired else jnp.int32(0), place_bit(0)])
    near, away, sent, kept = gram(genotypes, traits, place, members)
    if paired:
        halves = lax.all_gather(sent, "blk")
    pieces = all_sums(near, away)
    lam = nsamp * jnp.exp2((penalty_index.astype(jnp.float32) - 8.0) / 2.0)
    mine = lax.dynamic_index_in_dim(lam, (samp_rank % GROUP) % npen, 0, keepdims=True).reshape(1, 1)
    coef, mean = solve(pieces, mine, nsamp, nvars, ntraits)
    groups = [list(range(g, g + GROUP)) for g in range(0, members, GROUP)]
    if not paired:
        coefs = lax.all_gather(coef, "samp", axis_index_groups=groups)[:npen]
        dosage = genotypes.astype(jnp.bfloat16)
        return level_from_predictions(coefs, mean[0], dosage, traits, nvars)
    coef_far = lax.ppermute(coef, "blk", [(0, 1), (1, 0)])
    mean_far = lax.ppermute(mean, "blk", [(0, 1), (1, 0)])
    first = blk_rank == 0
    both = jnp.stack([jnp.where(first, coef, coef_far), jnp.where(first, coef_far, coef)])
    coefs = lax.all_gather(both, "samp", axis_index_groups=groups)
    rows = lax.dynamic_slice_in_dim(traits, blk_rank * (count // 2), count // 2, 0)
    found = level_sums(kept, halves, coefs, mean, mean_far, rows, npen)
    stack = nblk * npen
    each = ntraits // nblk
    far = lax.ppermute(lax.dynamic_slice_in_dim(found, (1 - blk_rank) * each, each, 0), "blk", [(0, 1), (1, 0)])
    found = small_sum(lax.dynamic_slice_in_dim(found, blk_rank * each, each, 0) + far) / nvars
    return found[:, :stack * stack].reshape(each, stack, stack), found[:, stack * stack:stack * stack + stack]


def solution(mesh):
    placed = (P("samp", "blk"), P("samp", None), P())
    return jax.shard_map(
        local,
        mesh=mesh,
        in_specs=placed,
        out_specs=(P("blk", None, None), P("blk", None)),
        check_vma=False,
    )
```

```python
import functools

import jax
import jax.numpy as jnp
from jax import lax
from jax.experimental import pallas as pl
from jax.experimental.pallas import tpu as pltpu
from jax.sharding import PartitionSpec as P

BLK = 128
SUB = 8
GROUP = 8
CHUNKS = 6
HI = lax.Precision.HIGHEST
NT = (((1,), (1,)), ((), ()))
TN = (((0,), (0,)), ((), ()))


def dot_hi(a, b):
    return jnp.dot(a, b, precision=HI, preferred_element_type=jnp.float32)


def dot_nt(a, b):
    return lax.dot_general(a, b, NT, precision=HI, preferred_element_type=jnp.float32)


def panel_rows(nvars):
    starts = [0]
    for j in range(nvars // BLK):
        starts.append(starts[-1] + nvars - BLK * j)
    return starts[:-1], starts[-1]


def side_rows(ntraits):
    return ntraits + SUB


def down(row):
    return jnp.transpose(jnp.broadcast_to(row, (BLK, BLK)))


def inverse_of(x):
    near = pl.reciprocal(x, approx=True)
    return near * (2.0 - x * near)


def split(x):
    first = x.astype(jnp.bfloat16)
    rest = x - first.astype(jnp.float32)
    second = rest.astype(jnp.bfloat16)
    return first, second, (rest - second.astype(jnp.float32)).astype(jnp.bfloat16)


def as_left(x):
    a, b, c = split(x)
    return jnp.concatenate([a, a, b, a, b, c], axis=1)


def as_right(x, axis):
    a, b, c = split(x)
    return jnp.concatenate([a, b, a, c, b, a], axis=axis)


def spread(x, lane):
    return jnp.broadcast_to(x[:, lane:lane + 1], (SUB, BLK))


def drop(x, row):
    return jnp.broadcast_to(x[row:row + 1, :], (SUB, BLK))


def solve_pivots(cols, right, rows_at):
    for j in range(0, SUB, 2):
        a, b = drop(cols[j], j), drop(cols[j + 1], j)
        c, d = drop(cols[j], j + 1), drop(cols[j + 1], j + 1)
        scale = inverse_of(a * d - b * c)
        both = rows_at[j] | rows_at[j + 1]
        even = jnp.where(rows_at[j], -1.0, jnp.where(rows_at[j + 1], 0.0, cols[j]))
        odd = jnp.where(rows_at[j + 1], -1.0, jnp.where(rows_at[j], 0.0, cols[j + 1]))
        above_by = even * d - odd * c
        below_by = odd * a - even * b

        def move(x):
            change = above_by * drop(x, j) + below_by * drop(x, j + 1)
            return jnp.where(both, 0.0, x) - change * scale

        cols = cols[:j + 2] + [move(x) for x in cols[j + 2:]]
        right = move(right)
    return right


def invert_tile(tile):
    count = BLK // SUB
    strips = [tile[SUB * i:SUB * (i + 1), :] for i in range(count)]
    lane = lax.broadcasted_iota(jnp.int32, (SUB, BLK), 1)
    sub = lax.broadcasted_iota(jnp.int32, (SUB, BLK), 0)
    rows_at = [sub == j for j in range(SUB)]
    for k in range(count):
        at = SUB * k
        inside = (lane >= at) & (lane < at + SUB)
        eye = (lane - at == sub).astype(jnp.float32)
        cols = [spread(strips[k], at + j) for j in range(SUB)]
        right = solve_pivots(cols, jnp.where(inside, eye, strips[k]), rows_at)
        tops = [drop(right, j) for j in range(SUB)]
        fresh = []
        for i in range(count):
            if i == k:
                fresh.append(right)
            else:
                rest = jnp.where(inside, 0.0, strips[i])
                for j in range(SUB):
                    rest = rest - spread(strips[i], at + j) * tops[j]
                fresh.append(rest)
        strips = fresh
    return jnp.concatenate(strips, axis=0)


def piece_starts(rows):
    each = rows * 7 // 64
    return [each * i for i in range(CHUNKS + 1)] + [rows]


def gram_kernel(ntraits, rank_ref, geno_ref, traits_ref, near_ref, away_ref, kept_ref, *refs):
    nvars = geno_ref.shape[1]
    step = pl.program_id(0)
    half = pl.num_programs(0) // 2
    wide = 2 * BLK
    pieces, side, panels = refs[:CHUNKS + 1], refs[CHUNKS + 1], refs[CHUNKS + 2:]

    @pl.when(step == 0)
    def _():
        side[...] = jnp.zeros_like(side)
        for panel in panels:
            panel[...] = jnp.zeros_like(panel)

    dosage = geno_ref[...].astype(jnp.float32).astype(jnp.bfloat16)

    count = dosage.shape[0]
    for tile in range(piece_starts(geno_ref.shape[0] * 2)[-1] // count):
        @pl.when(step == tile)
        def _(tile=tile):
            starts = piece_starts(count * 2)
            for piece, first, end in zip(pieces, starts, starts[1:]):
                low, high = max(first, tile * count), min(end, (tile + 1) * count)
                if low < high:
                    piece[low - first:high - first, :] = dosage[low - tile * count:high - tile * count, :]

    @pl.when(step >= half)
    def _():
        kept_ref[...] = dosage

    for j, panel in enumerate(panels):
        left, right = dosage[:, wide * j:], dosage[:, wide * j:wide * (j + 1)]
        panel[...] += lax.dot_general(left, right, TN, preferred_element_type=jnp.float32)
    traits = traits_ref[...]
    side[0:ntraits, :] += lax.dot_general(traits, dosage, TN, preferred_element_type=jnp.float32)
    ones = jnp.ones((SUB, dosage.shape[0]), jnp.bfloat16)
    sums = jnp.dot(ones, dosage, preferred_element_type=jnp.float32)
    ysum = jnp.dot(ones, traits, preferred_element_type=jnp.float32)
    ysum = jnp.concatenate([ysum, jnp.zeros((SUB, BLK - ntraits), jnp.float32)], axis=1)
    ysum = jnp.concatenate([ysum, jnp.zeros((SUB, nvars - BLK), jnp.float32)], axis=1)
    row = lax.broadcasted_iota(jnp.int32, (SUB, nvars), 0)
    side[ntraits:ntraits + SUB, :] += jnp.where(row == 0, sums, jnp.where(row == 1, ysum, 0.0))

    def hand_out(even, odd):
        rows = even.shape[0]

        def store(row, value):
            while value.shape[0] > 0:
                place, at = divmod(row, rows)
                size = min(value.shape[0], rows - at)
                (odd if place else even)[at:at + size, :] = value[:size, :]
                row, value = row + size, value[size:, :]

        starts, low = panel_rows(nvars)
        for j, start in enumerate(starts):
            skip = BLK * (j % 2)
            store(start, panels[j // 2][skip:, skip:skip + BLK])
        tall = side_rows(ntraits)
        for j in range(nvars // BLK):
            store(low + tall * j, side[:, BLK * j:BLK * (j + 1)])
        used = low + tall * (nvars // BLK)
        if used < 2 * rows:
            store(used, jnp.zeros((2 * rows - used, BLK), jnp.float32))

    last = step == pl.num_programs(0) - 1

    @pl.when(last & (rank_ref[1] == 0))
    def _():
        hand_out(near_ref, away_ref)

    @pl.when(last & (rank_ref[1] == 1))
    def _():
        hand_out(away_ref, near_ref)


def gram(genotypes, traits, place, members):
    count, nvars = genotypes.shape
    ntraits = traits.shape[1]
    steps = 4
    tile = count // steps
    half = steps // 2
    low = panel_rows(nvars)[1]
    share = 2 * SUB * members
    total = -(-(low + side_rows(ntraits) * (nvars // BLK)) // share) * share

    def source(i, place_ref):
        return (lax.rem(i + half * (1 - place_ref[0]), steps), 0)

    starts = piece_starts(count // 2)
    sizes = [end - first for first, end in zip(starts, starts[1:])]
    return pl.pallas_call(
        functools.partial(gram_kernel, ntraits),
        grid_spec=pltpu.PrefetchScalarGridSpec(
            num_scalar_prefetch=1,
            grid=(steps,),
            in_specs=[pl.BlockSpec((tile, nvars), source), pl.BlockSpec((tile, ntraits), source)],
            out_specs=[
                pl.BlockSpec((total // 2, BLK), lambda i, rank_ref: (0, 0)),
                pl.BlockSpec((total // 2, BLK), lambda i, rank_ref: (0, 0)),
                pl.BlockSpec((tile, nvars), lambda i, rank_ref: (jnp.maximum(i - half, 0), 0)),
            ]
            + [pl.BlockSpec((size, nvars), lambda i, rank_ref: (0, 0)) for size in sizes],
            scratch_shapes=[pltpu.VMEM((side_rows(ntraits), nvars), jnp.float32)]
            + [pltpu.VMEM((nvars - 2 * BLK * j, 2 * BLK), jnp.float32) for j in range(nvars // (2 * BLK))],
        ),
        out_shape=[jax.ShapeDtypeStruct((total // 2, BLK), jnp.float32)] * 2
        + [jax.ShapeDtypeStruct((size, nvars), jnp.bfloat16) for size in [count // 2] + sizes],
        compiler_params=pltpu.CompilerParams(vmem_limit_bytes=48 * 1024 * 1024),
        name="gram_sums",
    )(place, genotypes, traits)


def solve_kernel(nsamp, ntraits, lam_ref, near_a, near_b, far_a, far_b, coef_ref, mean_ref, aug, wide):
    nvars = coef_ref.shape[1]
    nblocks = nvars // BLK
    starts, low = panel_rows(nvars)
    tall = side_rows(ntraits)
    lam = lam_ref[0, 0]
    lower = lax.rem(lax.axis_index("samp"), 2) == 0
    quarter = near_a.shape[0]
    pairs = [(near_a, far_a), (near_b, far_b), (far_a, near_a), (far_b, near_b)]

    def read(row, count):
        found = []
        while count > 0:
            place, at = divmod(row, quarter)
            size = min(count, quarter - at)
            even, odd = pairs[place]
            found.append(jnp.where(lower, even[at:at + size, :], odd[at:at + size, :]))
            row, count = row + size, count - size
        return found[0] if len(found) == 1 else jnp.concatenate(found, axis=0)

    eye = lax.broadcasted_iota(jnp.int32, (BLK, BLK), 0) == lax.broadcasted_iota(jnp.int32, (BLK, BLK), 1)
    sides = [read(low + tall * j, tall) for j in range(nblocks)]
    means = [side[ntraits:ntraits + 1, :] / nsamp for side in sides]
    means_down = [down(mean) for mean in means]
    ysum = down(sides[0][ntraits + 1:ntraits + 2, :])[0:ntraits, :]
    for j in range(nblocks):
        span = slice(BLK * j, BLK * (j + 1))
        mean_ref[:, span] = jnp.broadcast_to(means[j], (SUB, BLK))
        for i in range(j, nblocks):
            value = read(starts[j] + BLK * (i - j), BLK) - nsamp * means_down[i] * means[j]
            if i == j:
                value = value + jnp.where(eye, lam * (value / nsamp + 1e-05), 0.0)
            aug[BLK * i:BLK * (i + 1), span] = value
        aug[nvars:nvars + ntraits, span] = sides[j][0:ntraits, :] - ysum * means[j]
    end = nvars + ntraits
    inverse = invert_tile(aug[0:BLK, 0:BLK])
    for k in range(nblocks):
        span = slice(BLK * k, BLK * (k + 1))
        first = BLK * (k + 1)
        panel = aug[first:end, span]
        mult = jnp.dot(as_left(panel), as_right(inverse, 0), preferred_element_type=jnp.float32)
        wide[first:end, span] = mult
        if k == nblocks - 1:
            break
        left, right = as_left(mult), as_right(panel, 1)
        j = k + 1
        while j < nblocks:
            top = BLK * j
            size = BLK if j == k + 1 or j == nblocks - 1 else 2 * BLK
            at = top - first
            aug[top:end, top:top + size] -= lax.dot_general(left[at:, :], right[at:at + size, :], NT, preferred_element_type=jnp.float32)
            if j == k + 1:
                inverse = invert_tile(aug[top:top + BLK, top:top + BLK])
            j += size // BLK
    solved = wide[nvars:end, nvars - BLK:nvars]
    coef_ref[:, nvars - BLK:nvars] = solved.astype(jnp.bfloat16)
    for k in range(nblocks - 2, -1, -1):
        span = slice(BLK * k, BLK * (k + 1))
        found = wide[nvars:end, span] - dot_hi(solved, wide[BLK * (k + 1):nvars, span])
        coef_ref[:, span] = found.astype(jnp.bfloat16)
        solved = jnp.concatenate([found, solved], axis=1)


def solve(pieces, lam, nsamp, nvars, ntraits):
    return pl.pallas_call(
        functools.partial(solve_kernel, nsamp, ntraits),
        out_shape=[jax.ShapeDtypeStruct((ntraits, nvars), jnp.bfloat16), jax.ShapeDtypeStruct((SUB, nvars), jnp.float32)],
        in_specs=[pl.BlockSpec(memory_space=pltpu.SMEM)] + [pl.BlockSpec(memory_space=pltpu.VMEM)] * 4,
        out_specs=[pl.BlockSpec(memory_space=pltpu.VMEM)] * 2,
        scratch_shapes=[
            pltpu.VMEM((nvars + ntraits, nvars), jnp.float32),
            pltpu.VMEM((nvars + ntraits, nvars), jnp.float32),
        ],
        compiler_params=pltpu.CompilerParams(vmem_limit_bytes=48 * 1024 * 1024),
        cost_estimate=pl.CostEstimate(flops=46 * 10**9, bytes_accessed=10**6, transcendentals=0),
        name="ridge_solve",
    )(lam, *pieces)


def level_kernel(npen, own_ref, coef_ref, mean_ref, far_mean_ref, traits_ref, *refs):
    rank = lax.axis_index("blk")
    ntraits = coef_ref.shape[2]
    nvars = own_ref.shape[1]
    count = own_ref.shape[0]
    stack = 2 * npen
    tile = 512
    pieces, (out_ref, pred, other_ref) = refs[:-3], refs[-3:]
    low = 0
    for piece in pieces:
        other_ref[low:low + piece.shape[0], :] = piece[...]
        low += piece.shape[0]
    for place in range(2):
        block = rank if place == 0 else 1 - rank
        source = own_ref if place == 0 else other_ref
        mean = (mean_ref if place == 0 else far_mean_ref)[0:1, :]
        coef = jnp.concatenate([coef_ref[r, block] for r in range(npen)], axis=0)
        offset = jnp.sum(coef.astype(jnp.float32) * mean, axis=1, keepdims=True)
        low = pl.multiple_of(block * (npen * ntraits), npen * ntraits)
        for n in range(0, count, tile):
            value = lax.dot_general(coef, source[n:n + tile, :], NT, preferred_element_type=jnp.float32)
            pred[pl.ds(low, npen * ntraits), n:n + tile] = value - offset
    for n in range(0, count, tile):
        rows = traits_ref[n:n + tile, :].astype(jnp.float32)
        rows = jnp.concatenate([rows, jnp.zeros((tile, BLK - ntraits), jnp.float32)], axis=1)
        pred[stack * ntraits:(stack + 1) * ntraits, n:n + tile] = jnp.transpose(rows)[0:ntraits, :]
    lane = lax.broadcasted_iota(jnp.int32, (SUB, BLK), 1)
    for t in range(0, ntraits, SUB):
        acc = jnp.zeros((SUB, BLK), jnp.float32)
        for i in range(stack):
            left = pred[i * ntraits + t:i * ntraits + t + SUB, :]
            for j in range(i, stack + 1):
                term = jnp.sum(left * pred[j * ntraits + t:j * ntraits + t + SUB, :], axis=1, keepdims=True)
                if j < stack:
                    acc = jnp.where((lane == i * stack + j) | (lane == j * stack + i), term, acc)
                else:
                    acc = jnp.where(lane == stack * stack + i, term, acc)
        out_ref[t:t + SUB, :] = acc


def level_sums(own, others, coefs, mean, far_mean, traits, npen):
    ntraits = traits.shape[1]
    count = own.shape[0]
    vmem = pl.BlockSpec(memory_space=pltpu.VMEM)
    return pl.pallas_call(
        functools.partial(level_kernel, npen),
        out_shape=jax.ShapeDtypeStruct((ntraits, BLK), jnp.float32),
        in_specs=[vmem] * (5 + len(others)),
        out_specs=pl.BlockSpec(memory_space=pltpu.VMEM),
        scratch_shapes=[
            pltpu.VMEM(((2 * npen + 1) * ntraits, count), jnp.float32),
            pltpu.VMEM(own.shape, own.dtype),
        ],
        compiler_params=pltpu.CompilerParams(vmem_limit_bytes=56 * 1024 * 1024),
        name="level_sums",
    )(own, coefs, mean, far_mean, traits, *others)


def swapped(x, bit):
    return lax.ppermute(x, "samp", [(i, i ^ (1 << bit)) for i in range(lax.axis_size("samp"))])


def place_bit(bit):
    return lax.rem(lax.div(lax.axis_index("samp"), 1 << bit), 2)


def add_kernel(near_a, far_a, near_b, far_b, *refs):
    out_a, out_b = refs[-2:]
    out_a[...] = near_a[...] + far_a[...]
    out_b[...] = near_b[...] + far_b[...]


def join_kernel(bits, near_a, far_a, near_b, far_b, *refs):
    rank = lax.axis_index("samp")
    for bit, near, far, out in zip(bits, (near_a, near_b), (far_a, far_b), refs[-2:]):
        rows = near.shape[0]
        mine = lax.rem(lax.div(rank, 1 << bit), 2)
        out[pl.ds(pl.multiple_of(mine * rows, SUB), rows), :] = near[...]
        out[pl.ds(pl.multiple_of((1 - mine) * rows, SUB), rows), :] = far[...]


def step_call(kernel, near, far, arrived, grow, name):
    operands = [near[0], far[0], near[1], far[1]] + arrived
    return pl.pallas_call(
        kernel,
        out_shape=[jax.ShapeDtypeStruct((grow * x.shape[0], x.shape[1]), x.dtype) for x in near],
        in_specs=[pl.BlockSpec(memory_space=pltpu.VMEM)] * 4 + [pl.BlockSpec(memory_space=pl.ANY)] * len(arrived),
        out_specs=[pl.BlockSpec(memory_space=pltpu.VMEM)] * 2,
        cost_estimate=pl.CostEstimate(flops=10**6, bytes_accessed=10**6, transcendentals=0),
        name=name,
    )(*operands)


def pass_kernel(coef_ref, piece_ref, out_ref):
    out_ref[...] = coef_ref[...]


def after(coef, piece):
    return pl.pallas_call(
        pass_kernel,
        out_shape=jax.ShapeDtypeStruct(coef.shape, coef.dtype),
        in_specs=[pl.BlockSpec(memory_space=pltpu.VMEM), pl.BlockSpec(memory_space=pl.ANY)],
        out_specs=pl.BlockSpec(memory_space=pltpu.VMEM),
        cost_estimate=pl.CostEstimate(flops=10**6, bytes_accessed=10**5, transcendentals=0),
        name="after_piece",
    )(coef, piece)


def cut(x, bit):
    rows = x.shape[0] // 2
    mine = place_bit(bit)
    return lax.dynamic_slice_in_dim(x, mine * rows, rows, 0), lax.dynamic_slice_in_dim(x, (1 - mine) * rows, rows, 0)


def all_sums(x, away, riders):
    bits = list(range(1, lax.axis_size("samp").bit_length() - 1))
    orders = (bits, bits[1:] + bits[:1])
    brought = []

    def ride():
        if len(brought) < len(riders):
            brought.append(riders[len(brought)]())
            return [brought[-1]]
        return []

    x = x + swapped(away, 0)
    rows = x.shape[0] // 2
    parts = [x[:rows], x[rows:]]
    for pair in zip(*orders):
        arrived = ride()
        kept, sent = zip(*[cut(part, bit) for part, bit in zip(parts, pair)])
        far = [swapped(part, bit) for part, bit in zip(sent, pair)]
        parts = step_call(add_kernel, kept, far, arrived, 1, "step_add")
    for pair in reversed(list(zip(*orders))):
        arrived = ride()
        far = [swapped(part, bit) for part, bit in zip(parts, pair)]
        parts = step_call(functools.partial(join_kernel, pair), parts, far, arrived, 2, "step_join")
    return list(parts) + [swapped(part, 0) for part in parts], brought


def small_sum(x):
    for bit in range(lax.axis_size("samp").bit_length() - 1):
        x = x + swapped(x, bit)
    return x


def level_from_predictions(coefs, mean, dosage, traits, nvars):
    coef = coefs.transpose(0, 2, 1)
    ntraits = traits.shape[1]
    offset = jnp.einsum("rmt,m->rt", coef.astype(jnp.float32), mean, precision=HI)
    pred = jnp.einsum("rmt,nm->trn", coef, dosage, preferred_element_type=jnp.float32)
    pred = (pred - offset.T[:, :, None]).astype(jnp.bfloat16)
    local_traits = ntraits // lax.axis_size("blk")
    parts = lax.all_to_all(pred[None], "blk", split_axis=1, concat_axis=0, tiled=True)
    mine = lax.dynamic_slice_in_dim(traits, lax.axis_index("blk") * local_traits, local_traits, 1)
    gram = jnp.einsum("btrn,ctsn->tbrcs", parts, parts, preferred_element_type=jnp.float32)
    cross = jnp.einsum("btrn,nt->tbr", parts, mine, preferred_element_type=jnp.float32)
    count, stack = parts.shape[1], parts.shape[0] * parts.shape[2]
    gram, cross = lax.psum((gram.reshape(count, stack, stack), cross.reshape(count, stack)), "samp")
    return gram / nvars, cross / nvars


def local(genotypes, traits, penalty_index):
    count, nvars = genotypes.shape
    ntraits = traits.shape[1]
    npen = penalty_index.shape[0]
    nblk = lax.axis_size("blk")
    members = lax.axis_size("samp")
    nsamp = float(count * members)
    samp_rank = lax.axis_index("samp")
    blk_rank = lax.axis_index("blk")
    paired = nblk == 2
    place = jnp.stack([blk_rank if paired else jnp.int32(0), place_bit(0)])
    near, away, kept, *sent = gram(genotypes, traits, place, members)
    riders = [functools.partial(lax.ppermute, piece, "blk", [(0, 1), (1, 0)]) for piece in sent] if paired else []
    pieces, others = all_sums(near, away, riders[:CHUNKS])
    others += [rider() for rider in riders[len(others):]]
    lam = nsamp * jnp.exp2((penalty_index.astype(jnp.float32) - 8.0) / 2.0)
    mine = lax.dynamic_index_in_dim(lam, (samp_rank % GROUP) % npen, 0, keepdims=True).reshape(1, 1)
    coef, mean = solve(pieces, mine, nsamp, nvars, ntraits)
    groups = [list(range(g, g + GROUP)) for g in range(0, members, GROUP)]
    if not paired:
        coefs = lax.all_gather(coef, "samp", axis_index_groups=groups)[:npen]
        dosage = genotypes.astype(jnp.bfloat16)
        return level_from_predictions(coefs, mean[0], dosage, traits, nvars)
    coef = after(coef, others[-1])
    coef_far = lax.ppermute(coef, "blk", [(0, 1), (1, 0)])
    mean_far = lax.ppermute(mean, "blk", [(0, 1), (1, 0)])
    first = blk_rank == 0
    both = jnp.stack([jnp.where(first, coef, coef_far), jnp.where(first, coef_far, coef)])
    coefs = lax.all_gather(both, "samp", axis_index_groups=groups)
    rows = lax.dynamic_slice_in_dim(traits, blk_rank * (count // 2), count // 2, 0)
    found = level_sums(kept, others, coefs, mean, mean_far, rows, npen)
    stack = nblk * npen
    each = ntraits // nblk
    far = lax.ppermute(lax.dynamic_slice_in_dim(found, (1 - blk_rank) * each, each, 0), "blk", [(0, 1), (1, 0)])
    found = small_sum(lax.dynamic_slice_in_dim(found, blk_rank * each, each, 0) + far) / nvars
    return found[:, :stack * stack].reshape(each, stack, stack), found[:, stack * stack:stack * stack + stack]


def solution(mesh):
    placed = (P("samp", "blk"), P("samp", None), P())
    return jax.shard_map(
        local,
        mesh=mesh,
        in_specs=placed,
        out_specs=(P("blk", None, None), P("blk", None)),
        check_vma=False,
    )
```

```python
import functools

import jax
import jax.numpy as jnp
from jax import lax
from jax.experimental import pallas as pl
from jax.experimental.pallas import tpu as pltpu
from jax.sharding import PartitionSpec as P

BLK = 128
SUB = 8
GROUP = 8
HI = lax.Precision.HIGHEST
NT = (((1,), (1,)), ((), ()))
TN = (((0,), (0,)), ((), ()))


def dot_hi(a, b):
    return jnp.dot(a, b, precision=HI, preferred_element_type=jnp.float32)


def dot_nt(a, b):
    return lax.dot_general(a, b, NT, precision=HI, preferred_element_type=jnp.float32)


def panel_rows(nvars):
    starts = [0]
    for j in range(nvars // BLK):
        starts.append(starts[-1] + nvars - BLK * j)
    return starts[:-1], starts[-1]


def side_rows(ntraits):
    return ntraits + SUB


def down(row):
    return jnp.transpose(jnp.broadcast_to(row, (BLK, BLK)))


def inverse_of(x):
    near = pl.reciprocal(x, approx=True)
    return near * (2.0 - x * near)


def split(x):
    first = x.astype(jnp.bfloat16)
    rest = x - first.astype(jnp.float32)
    second = rest.astype(jnp.bfloat16)
    return first, second, (rest - second.astype(jnp.float32)).astype(jnp.bfloat16)


def as_left(x):
    a, b, c = split(x)
    return jnp.concatenate([a, a, b, a, b, c], axis=1)


def as_right(x, axis):
    a, b, c = split(x)
    return jnp.concatenate([a, b, a, c, b, a], axis=axis)


def invert_tile(tile):
    strips = [tile[SUB * i:SUB * (i + 1), :] for i in range(BLK // SUB)]
    lane = lax.broadcasted_iota(jnp.int32, (SUB, BLK), 1)
    sub = lax.broadcasted_iota(jnp.int32, (SUB, BLK), 0)
    rows_at = [sub == j for j in range(SUB)]
    for k in range(BLK // SUB):
        at = SUB * k
        inside = (lane >= at) & (lane < at + SUB)
        eye = (lane - at == sub).astype(jnp.float32)
        cols = [jnp.broadcast_to(strips[k][:, at + j:at + j + 1], (SUB, BLK)) for j in range(SUB)]
        right = jnp.where(inside, eye, strips[k])
        for j in range(SUB):
            pivot = inverse_of(jnp.broadcast_to(cols[j][j:j + 1, :], (SUB, BLK)))
            step = jnp.where(rows_at[j], -1.0, cols[j])

            def move(x):
                return jnp.where(rows_at[j], 0.0, x) - (step * jnp.broadcast_to(x[j:j + 1, :], (SUB, BLK))) * pivot

            cols = cols[:j + 1] + [move(c) for c in cols[j + 1:]]
            right = move(right)
        tops = [jnp.broadcast_to(right[j:j + 1, :], (SUB, BLK)) for j in range(SUB)]
        fresh = []
        for i in range(BLK // SUB):
            if i == k:
                fresh.append(right)
                continue
            rest = jnp.where(inside, 0.0, strips[i])
            for j in range(SUB):
                rest = rest - jnp.broadcast_to(strips[i][:, at + j:at + j + 1], (SUB, BLK)) * tops[j]
            fresh.append(rest)
        strips = fresh
    return jnp.concatenate(strips, axis=0)


def piece_starts(rows):
    return [0, rows * 17 // 32, rows]


def gram_kernel(ntraits, rank_ref, geno_ref, traits_ref, near_ref, away_ref, kept_ref, *refs):
    nvars = geno_ref.shape[1]
    step = pl.program_id(0)
    half = pl.num_programs(0) // 2
    wide = 2 * BLK
    pieces, side, ysum, panels = refs[:2], refs[2], refs[3], refs[4:]

    @pl.when(step == 0)
    def _():
        side[...] = jnp.zeros_like(side)
        ysum[...] = jnp.zeros_like(ysum)
        for panel in panels:
            panel[...] = jnp.zeros_like(panel)

    dosage = geno_ref[...].astype(jnp.float32).astype(jnp.bfloat16)

    count = dosage.shape[0]
    for tile in range(piece_starts(geno_ref.shape[0] * 2)[-1] // count):
        @pl.when(step == tile)
        def _(tile=tile):
            starts = piece_starts(count * 2)
            for piece, first, end in zip(pieces, starts, starts[1:]):
                low, high = max(first, tile * count), min(end, (tile + 1) * count)
                if low < high:
                    piece[low - first:high - first, :] = dosage[low - tile * count:high - tile * count, :]

    @pl.when(step >= half)
    def _():
        kept_ref[...] = dosage

    for j, panel in enumerate(panels):
        left, right = dosage[:, wide * j:], dosage[:, wide * j:wide * (j + 1)]
        panel[...] += lax.dot_general(left, right, TN, preferred_element_type=jnp.float32)
    traits = traits_ref[...]
    rows = jnp.concatenate([traits, jnp.ones((2 * SUB, count), jnp.bfloat16)], axis=0)
    sums = jnp.dot(rows, dosage, preferred_element_type=jnp.float32)
    side[...] += sums[0:side.shape[0], :]
    ysum[...] += jnp.sum(traits.astype(jnp.float32), axis=1, keepdims=True)

    def hand_out(even, odd):
        rows = even.shape[0]

        def store(row, value):
            while value.shape[0] > 0:
                place, at = divmod(row, rows)
                size = min(value.shape[0], rows - at)
                (odd if place else even)[at:at + size, :] = value[:size, :]
                row, value = row + size, value[size:, :]

        starts, low = panel_rows(nvars)
        for j, start in enumerate(starts):
            skip = BLK * (j % 2)
            store(start, panels[j // 2][skip:, skip:skip + BLK])
        tall = side_rows(ntraits)
        for j in range(nvars // BLK):
            store(low + tall * j, side[:, BLK * j:BLK * (j + 1)])
        used = low + tall * (nvars // BLK) + ntraits
        store(used - ntraits, ysum[...])
        if used < 2 * rows:
            store(used, jnp.zeros((2 * rows - used, BLK), jnp.float32))

    last = step == pl.num_programs(0) - 1

    @pl.when(last & (rank_ref[1] == 0))
    def _():
        hand_out(near_ref, away_ref)

    @pl.when(last & (rank_ref[1] == 1))
    def _():
        hand_out(away_ref, near_ref)


def gram(genotypes, traits, place, members):
    count, nvars = genotypes.shape
    ntraits = traits.shape[0]
    steps = 4
    tile = count // steps
    half = steps // 2
    low = panel_rows(nvars)[1]
    share = 2 * SUB * members
    total = -(-(low + side_rows(ntraits) * (nvars // BLK) + ntraits) // share) * share

    def source(i, place_ref):
        return (lax.rem(i + half * (1 - place_ref[0]), steps), 0)

    def traits_source(i, place_ref):
        return (0, lax.rem(i + half * (1 - place_ref[0]), steps))

    starts = piece_starts(count // 2)
    sizes = [end - first for first, end in zip(starts, starts[1:])]
    return pl.pallas_call(
        functools.partial(gram_kernel, ntraits),
        grid_spec=pltpu.PrefetchScalarGridSpec(
            num_scalar_prefetch=1,
            grid=(steps,),
            in_specs=[pl.BlockSpec((tile, nvars), source), pl.BlockSpec((ntraits, tile), traits_source)],
            out_specs=[
                pl.BlockSpec((total // 2, BLK), lambda i, rank_ref: (0, 0)),
                pl.BlockSpec((total // 2, BLK), lambda i, rank_ref: (0, 0)),
                pl.BlockSpec((tile, nvars), lambda i, rank_ref: (jnp.maximum(i - half, 0), 0)),
            ]
            + [pl.BlockSpec((size, nvars), lambda i, rank_ref: (0, 0)) for size in sizes],
            scratch_shapes=[pltpu.VMEM((side_rows(ntraits), nvars), jnp.float32), pltpu.VMEM((ntraits, BLK), jnp.float32)]
            + [pltpu.VMEM((nvars - 2 * BLK * j, 2 * BLK), jnp.float32) for j in range(nvars // (2 * BLK))],
        ),
        out_shape=[jax.ShapeDtypeStruct((total // 2, BLK), jnp.float32)] * 2
        + [jax.ShapeDtypeStruct((size, nvars), jnp.bfloat16) for size in [count // 2] + sizes],
        compiler_params=pltpu.CompilerParams(vmem_limit_bytes=48 * 1024 * 1024),
        name="gram_sums",
    )(place, genotypes, traits)


def solve_kernel(nsamp, ntraits, lam_ref, near_a, near_b, far_a, far_b, *refs):
    coef_ref, mean_ref, aug, wide = refs[-4:]
    nvars = coef_ref.shape[1]
    nblocks = nvars // BLK
    starts, low = panel_rows(nvars)
    tall = side_rows(ntraits)
    lam = lam_ref[0, 0]
    lower = lax.rem(lax.axis_index("samp"), 2) == 0
    quarter = near_a.shape[0]
    pairs = [(near_a, far_a), (near_b, far_b), (far_a, near_a), (far_b, near_b)]

    def read(row, count):
        found = []
        while count > 0:
            place, at = divmod(row, quarter)
            size = min(count, quarter - at)
            even, odd = pairs[place]
            found.append(jnp.where(lower, even[at:at + size, :], odd[at:at + size, :]))
            row, count = row + size, count - size
        return found[0] if len(found) == 1 else jnp.concatenate(found, axis=0)

    eye = lax.broadcasted_iota(jnp.int32, (BLK, BLK), 0) == lax.broadcasted_iota(jnp.int32, (BLK, BLK), 1)
    sides = [read(low + tall * j, tall) for j in range(nblocks)]
    means = [side[ntraits:ntraits + 1, :] / nsamp for side in sides]
    means_down = [down(mean) for mean in means]
    ysum = read(low + tall * nblocks, ntraits)
    for j in range(nblocks):
        span = slice(BLK * j, BLK * (j + 1))
        mean_ref[:, span] = jnp.broadcast_to(means[j], (SUB, BLK))
        for i in range(j, nblocks):
            value = read(starts[j] + BLK * (i - j), BLK) - nsamp * means_down[i] * means[j]
            if i == j:
                value = value + jnp.where(eye, lam * (value / nsamp + 1e-05), 0.0)
            aug[BLK * i:BLK * (i + 1), span] = value
        aug[nvars:nvars + ntraits, span] = sides[j][0:ntraits, :] - ysum * means[j]
    end = nvars + ntraits
    inverse = invert_tile(aug[0:BLK, 0:BLK])
    for k in range(nblocks):
        span = slice(BLK * k, BLK * (k + 1))
        first = BLK * (k + 1)
        panel = aug[first:end, span]
        mult = jnp.dot(as_left(panel), as_right(inverse, 0), preferred_element_type=jnp.float32)
        wide[first:end, span] = mult
        if k == nblocks - 1:
            break
        left, right = as_left(mult), as_right(panel, 1)
        j = k + 1
        while j < nblocks:
            top = BLK * j
            size = BLK if j == k + 1 or j == nblocks - 1 else 2 * BLK
            at = top - first
            aug[top:end, top:top + size] -= lax.dot_general(left[at:, :], right[at:at + size, :], NT, preferred_element_type=jnp.float32)
            if j == k + 1:
                inverse = invert_tile(aug[top:top + BLK, top:top + BLK])
            j += size // BLK
    solved = wide[nvars:end, nvars - BLK:nvars]
    coef_ref[:, nvars - BLK:nvars] = solved.astype(jnp.bfloat16)
    for k in range(nblocks - 2, -1, -1):
        span = slice(BLK * k, BLK * (k + 1))
        found = wide[nvars:end, span] - dot_hi(solved, wide[BLK * (k + 1):nvars, span])
        coef_ref[:, span] = found.astype(jnp.bfloat16)
        solved = jnp.concatenate([found, solved], axis=1)


def solve(pieces, lam, arrived, nsamp, nvars, ntraits):
    return pl.pallas_call(
        functools.partial(solve_kernel, nsamp, ntraits),
        out_shape=[jax.ShapeDtypeStruct((ntraits, nvars), jnp.bfloat16), jax.ShapeDtypeStruct((SUB, nvars), jnp.float32)],
        in_specs=[pl.BlockSpec(memory_space=pltpu.SMEM)]
        + [pl.BlockSpec(memory_space=pltpu.VMEM)] * 4
        + [pl.BlockSpec(memory_space=pl.ANY)] * len(arrived),
        out_specs=[pl.BlockSpec(memory_space=pltpu.VMEM)] * 2,
        scratch_shapes=[
            pltpu.VMEM((nvars + ntraits, nvars), jnp.float32),
            pltpu.VMEM((nvars + ntraits, nvars), jnp.float32),
        ],
        compiler_params=pltpu.CompilerParams(vmem_limit_bytes=48 * 1024 * 1024),
        cost_estimate=pl.CostEstimate(flops=46 * 10**9, bytes_accessed=10**6, transcendentals=0),
        name="ridge_solve",
    )(lam, *pieces, *arrived)


def level_kernel(npen, own_ref, coef_ref, mean_ref, far_mean_ref, traits_ref, *refs):
    rank = lax.axis_index("blk")
    ntraits = coef_ref.shape[2]
    nvars = own_ref.shape[1]
    count = own_ref.shape[0]
    stack = 2 * npen
    tile = 512
    pieces, (out_ref, pred, other_ref) = refs[:-3], refs[-3:]
    low = 0
    for piece in pieces:
        other_ref[low:low + piece.shape[0], :] = piece[...]
        low += piece.shape[0]
    for place in range(2):
        block = rank if place == 0 else 1 - rank
        source = own_ref if place == 0 else other_ref
        mean = (mean_ref if place == 0 else far_mean_ref)[0:1, :]
        coef = jnp.concatenate([coef_ref[r, block] for r in range(npen)], axis=0)
        offset = jnp.sum(coef.astype(jnp.float32) * mean, axis=1, keepdims=True)
        low = pl.multiple_of(block * (npen * ntraits), npen * ntraits)
        for n in range(0, count, tile):
            value = lax.dot_general(coef, source[n:n + tile, :], NT, preferred_element_type=jnp.float32)
            pred[pl.ds(low, npen * ntraits), n:n + tile] = value - offset
    pred[stack * ntraits:(stack + 1) * ntraits, :] = traits_ref[...].astype(jnp.float32)
    lane = lax.broadcasted_iota(jnp.int32, (SUB, BLK), 1)
    for t in range(0, ntraits, SUB):
        acc = jnp.zeros((SUB, BLK), jnp.float32)
        for i in range(stack):
            left = pred[i * ntraits + t:i * ntraits + t + SUB, :]
            for j in range(i, stack + 1):
                term = jnp.sum(left * pred[j * ntraits + t:j * ntraits + t + SUB, :], axis=1, keepdims=True)
                if j < stack:
                    acc = jnp.where((lane == i * stack + j) | (lane == j * stack + i), term, acc)
                else:
                    acc = jnp.where(lane == stack * stack + i, term, acc)
        out_ref[t:t + SUB, :] = acc


def level_sums(own, others, coefs, mean, far_mean, traits, npen):
    ntraits = traits.shape[0]
    count = own.shape[0]
    vmem = pl.BlockSpec(memory_space=pltpu.VMEM)
    return pl.pallas_call(
        functools.partial(level_kernel, npen),
        out_shape=jax.ShapeDtypeStruct((ntraits, BLK), jnp.float32),
        in_specs=[vmem] * (5 + len(others)),
        out_specs=pl.BlockSpec(memory_space=pltpu.VMEM),
        scratch_shapes=[
            pltpu.VMEM(((2 * npen + 1) * ntraits, count), jnp.float32),
            pltpu.VMEM(own.shape, own.dtype),
        ],
        compiler_params=pltpu.CompilerParams(vmem_limit_bytes=56 * 1024 * 1024),
        name="level_sums",
    )(own, coefs, mean, far_mean, traits, *others)


def swapped(x, bit):
    return lax.ppermute(x, "samp", [(i, i ^ (1 << bit)) for i in range(lax.axis_size("samp"))])


def place_bit(bit):
    return lax.rem(lax.div(lax.axis_index("samp"), 1 << bit), 2)


def stack_kernel(near_ref, far_ref, piece_ref, out_ref):
    rank = lax.axis_index("blk")
    out_ref[rank] = near_ref[...]
    out_ref[1 - rank] = far_ref[...]


def stacked(near, far, piece):
    return pl.pallas_call(
        stack_kernel,
        out_shape=jax.ShapeDtypeStruct((2,) + near.shape, near.dtype),
        in_specs=[pl.BlockSpec(memory_space=pltpu.VMEM)] * 2 + [pl.BlockSpec(memory_space=pl.ANY)],
        out_specs=pl.BlockSpec(memory_space=pltpu.VMEM),
        cost_estimate=pl.CostEstimate(flops=10**6, bytes_accessed=10**5, transcendentals=0),
        name="stack_blocks",
    )(near, far, piece)


def halved(x, bit):
    rows = x.shape[0] // 2
    mine = place_bit(bit)
    far = swapped(lax.dynamic_slice_in_dim(x, (1 - mine) * rows, rows, 0), bit)
    return lax.dynamic_slice_in_dim(x, mine * rows, rows, 0) + far


def doubled(x, bit):
    far = swapped(x, bit)
    even = place_bit(bit) == 0
    return jnp.concatenate([jnp.where(even, x, far), jnp.where(even, far, x)], axis=0)


def all_sums(x, away):
    bits = list(range(1, lax.axis_size("samp").bit_length() - 1))
    x = x + swapped(away, 0)
    rows = x.shape[0] // 2
    near = []
    for part, order in ((x[:rows], bits), (x[rows:], bits[1:] + bits[:1])):
        for bit in order:
            part = halved(part, bit)
        for bit in reversed(order):
            part = doubled(part, bit)
        near.append(part)
    return near + [swapped(part, 0) for part in near]


def small_sum(x):
    for bit in range(lax.axis_size("samp").bit_length() - 1):
        x = x + swapped(x, bit)
    return x


def level_from_predictions(coefs, mean, dosage, traits, nvars):
    coef = coefs.transpose(0, 2, 1)
    ntraits = traits.shape[1]
    offset = jnp.einsum("rmt,m->rt", coef.astype(jnp.float32), mean, precision=HI)
    pred = jnp.einsum("rmt,nm->trn", coef, dosage, preferred_element_type=jnp.float32)
    pred = (pred - offset.T[:, :, None]).astype(jnp.bfloat16)
    local_traits = ntraits // lax.axis_size("blk")
    parts = lax.all_to_all(pred[None], "blk", split_axis=1, concat_axis=0, tiled=True)
    mine = lax.dynamic_slice_in_dim(traits, lax.axis_index("blk") * local_traits, local_traits, 1)
    gram = jnp.einsum("btrn,ctsn->tbrcs", parts, parts, preferred_element_type=jnp.float32)
    cross = jnp.einsum("btrn,nt->tbr", parts, mine, preferred_element_type=jnp.float32)
    count, stack = parts.shape[1], parts.shape[0] * parts.shape[2]
    gram, cross = lax.psum((gram.reshape(count, stack, stack), cross.reshape(count, stack)), "samp")
    return gram / nvars, cross / nvars


def local(genotypes, traits, penalty_index):
    count, nvars = genotypes.shape
    ntraits = traits.shape[1]
    npen = penalty_index.shape[0]
    nblk = lax.axis_size("blk")
    members = lax.axis_size("samp")
    nsamp = float(count * members)
    samp_rank = lax.axis_index("samp")
    blk_rank = lax.axis_index("blk")
    paired = nblk == 2
    place = jnp.stack([blk_rank if paired else jnp.int32(0), place_bit(0)])
    turned = traits.T
    near, away, kept, *sent = gram(genotypes, turned, place, members)
    others = [lax.ppermute(piece, "blk", [(0, 1), (1, 0)]) for piece in sent] if paired else []
    pieces = all_sums(near, away)
    lam = nsamp * jnp.exp2((penalty_index.astype(jnp.float32) - 8.0) / 2.0)
    mine = lax.dynamic_index_in_dim(lam, (samp_rank % GROUP) % npen, 0, keepdims=True).reshape(1, 1)
    coef, mean = solve(pieces, mine, others[:1], nsamp, nvars, ntraits)
    groups = [list(range(g, g + GROUP)) for g in range(0, members, GROUP)]
    if not paired:
        coefs = lax.all_gather(coef, "samp", axis_index_groups=groups)[:npen]
        dosage = genotypes.astype(jnp.bfloat16)
        return level_from_predictions(coefs, mean[0], dosage, traits, nvars)
    coef_far = lax.ppermute(coef, "blk", [(0, 1), (1, 0)])
    mean_far = lax.ppermute(mean, "blk", [(0, 1), (1, 0)])
    both = stacked(coef, coef_far, others[1])
    coefs = lax.all_gather(both, "samp", axis_index_groups=groups)
    rows = lax.dynamic_slice_in_dim(turned, blk_rank * (count // 2), count // 2, 1)
    found = level_sums(kept, others, coefs, mean, mean_far, rows, npen)
    stack = nblk * npen
    each = ntraits // nblk
    far = lax.ppermute(lax.dynamic_slice_in_dim(found, (1 - blk_rank) * each, each, 0), "blk", [(0, 1), (1, 0)])
    found = small_sum(lax.dynamic_slice_in_dim(found, blk_rank * each, each, 0) + far) / nvars
    return found[:, :stack * stack].reshape(each, stack, stack), found[:, stack * stack:stack * stack + stack]


def solution(mesh):
    placed = (P("samp", "blk"), P("samp", None), P())
    return jax.shard_map(
        local,
        mesh=mesh,
        in_specs=placed,
        out_specs=(P("blk", None, None), P("blk", None)),
        check_vma=False,
    )
```

```python
import functools

import jax
import jax.numpy as jnp
from jax import lax
from jax.experimental import pallas as pl
from jax.experimental.pallas import tpu as pltpu
from jax.sharding import PartitionSpec as P

BLK = 128
SUB = 8
GROUP = 8
HI = lax.Precision.HIGHEST
NT = (((1,), (1,)), ((), ()))
TN = (((0,), (0,)), ((), ()))


def dot_hi(a, b):
    return jnp.dot(a, b, precision=HI, preferred_element_type=jnp.float32)


def dot_nt(a, b):
    return lax.dot_general(a, b, NT, precision=HI, preferred_element_type=jnp.float32)


def panel_rows(nvars):
    starts = [0]
    for j in range(nvars // BLK):
        starts.append(starts[-1] + nvars - BLK * j)
    return starts[:-1], starts[-1]


def side_rows(ntraits):
    return ntraits + SUB


def down(row):
    return jnp.transpose(jnp.broadcast_to(row, (BLK, BLK)))


def inverse_of(x):
    near = pl.reciprocal(x, approx=True)
    return near * (2.0 - x * near)


def split(x):
    first = x.astype(jnp.bfloat16)
    rest = x - first.astype(jnp.float32)
    second = rest.astype(jnp.bfloat16)
    return first, second, (rest - second.astype(jnp.float32)).astype(jnp.bfloat16)


def as_left(x):
    a, b, c = split(x)
    return jnp.concatenate([a, a, b, a, b, c], axis=1)


def as_right(x, axis):
    a, b, c = split(x)
    return jnp.concatenate([a, b, a, c, b, a], axis=axis)


def stack_left(x):
    a, b, c = [part.astype(jnp.float32) for part in split(x)]
    return jnp.concatenate([a, a, b, a, b, c], axis=0).astype(jnp.bfloat16)


def stack_right(x):
    a, b, c = [part.astype(jnp.float32) for part in split(x)]
    return jnp.concatenate([a, b, a, c, b, a], axis=0).astype(jnp.bfloat16)


def invert_tile(tile):
    strips = [tile[SUB * i:SUB * (i + 1), :] for i in range(BLK // SUB)]
    lane = lax.broadcasted_iota(jnp.int32, (SUB, BLK), 1)
    sub = lax.broadcasted_iota(jnp.int32, (SUB, BLK), 0)
    rows_at = [sub == j for j in range(SUB)]
    for k in range(BLK // SUB):
        at = SUB * k
        inside = (lane >= at) & (lane < at + SUB)
        eye = (lane - at == sub).astype(jnp.float32)
        cols = [jnp.broadcast_to(strips[k][:, at + j:at + j + 1], (SUB, BLK)) for j in range(SUB)]
        right = jnp.where(inside, eye, strips[k])
        for j in range(SUB):
            pivot = inverse_of(jnp.broadcast_to(cols[j][j:j + 1, :], (SUB, BLK)))
            step = jnp.where(rows_at[j], -1.0, cols[j])

            def move(x):
                return jnp.where(rows_at[j], 0.0, x) - (step * jnp.broadcast_to(x[j:j + 1, :], (SUB, BLK))) * pivot

            cols = cols[:j + 1] + [move(c) for c in cols[j + 1:]]
            right = move(right)
        mirror = jnp.where(lane < at, -strips[k], jnp.where(inside, 0.0, strips[k]))
        change = lax.dot_general(stack_left(mirror), stack_right(right), TN, preferred_element_type=jnp.float32)
        fresh = []
        for i in range(BLK // SUB):
            rest = jnp.where(inside, 0.0, strips[i])
            if i == k:
                rest = right
            elif i == k + 1:
                for j in range(SUB):
                    factor = jnp.broadcast_to(strips[i][:, at + j:at + j + 1], (SUB, BLK))
                    rest = rest - factor * jnp.broadcast_to(right[j:j + 1, :], (SUB, BLK))
            else:
                rest = rest - change[SUB * i:SUB * (i + 1), :]
            fresh.append(rest)
        strips = fresh
    return jnp.concatenate(strips, axis=0)


def piece_starts(rows):
    return [0, rows * 17 // 32, rows]


def gram_kernel(ntraits, rank_ref, geno_ref, traits_ref, near_ref, away_ref, kept_ref, *refs):
    nvars = geno_ref.shape[1]
    step = pl.program_id(0)
    half = pl.num_programs(0) // 2
    wide = 2 * BLK
    pieces, side, ysum, panels = refs[:2], refs[2], refs[3], refs[4:]

    @pl.when(step == 0)
    def _():
        side[...] = jnp.zeros_like(side)
        ysum[...] = jnp.zeros_like(ysum)
        for panel in panels:
            panel[...] = jnp.zeros_like(panel)

    dosage = geno_ref[...].astype(jnp.float32).astype(jnp.bfloat16)

    count = dosage.shape[0]
    for j, panel in enumerate(panels):
        left, right = dosage[:, wide * j:], dosage[:, wide * j:wide * (j + 1)]
        panel[...] += lax.dot_general(left, right, TN, preferred_element_type=jnp.float32)
    traits = traits_ref[...]
    rows = jnp.concatenate([traits, jnp.ones((2 * SUB, count), jnp.bfloat16)], axis=0)
    sums = jnp.dot(rows, dosage, preferred_element_type=jnp.float32)
    side[...] += sums[0:side.shape[0], :]
    ysum[...] += jnp.sum(traits.astype(jnp.float32), axis=1, keepdims=True)

    for tile in range(piece_starts(geno_ref.shape[0] * 2)[-1] // count):
        @pl.when(step == tile)
        def _(tile=tile):
            starts = piece_starts(count * 2)
            for piece, first, end in zip(pieces, starts, starts[1:]):
                low, high = max(first, tile * count), min(end, (tile + 1) * count)
                if low < high:
                    piece[low - first:high - first, :] = dosage[low - tile * count:high - tile * count, :]

    @pl.when(step >= half)
    def _():
        kept_ref[...] = dosage

    def hand_out(even, odd):
        rows = even.shape[0]

        def store(row, value):
            while value.shape[0] > 0:
                place, at = divmod(row, rows)
                size = min(value.shape[0], rows - at)
                (odd if place else even)[at:at + size, :] = value[:size, :]
                row, value = row + size, value[size:, :]

        starts, low = panel_rows(nvars)
        for j, start in enumerate(starts):
            skip = BLK * (j % 2)
            store(start, panels[j // 2][skip:, skip:skip + BLK])
        tall = side_rows(ntraits)
        for j in range(nvars // BLK):
            store(low + tall * j, side[:, BLK * j:BLK * (j + 1)])
        used = low + tall * (nvars // BLK) + ntraits
        store(used - ntraits, ysum[...])
        if used < 2 * rows:
            store(used, jnp.zeros((2 * rows - used, BLK), jnp.float32))

    last = step == pl.num_programs(0) - 1

    @pl.when(last & (rank_ref[1] == 0))
    def _():
        hand_out(near_ref, away_ref)

    @pl.when(last & (rank_ref[1] == 1))
    def _():
        hand_out(away_ref, near_ref)


def gram(genotypes, traits, place, members):
    count, nvars = genotypes.shape
    ntraits = traits.shape[0]
    steps = 4
    tile = count // steps
    half = steps // 2
    low = panel_rows(nvars)[1]
    share = 2 * SUB * members
    total = -(-(low + side_rows(ntraits) * (nvars // BLK) + ntraits) // share) * share

    def source(i, place_ref):
        return (lax.rem(i + half * (1 - place_ref[0]), steps), 0)

    def traits_source(i, place_ref):
        return (0, lax.rem(i + half * (1 - place_ref[0]), steps))

    starts = piece_starts(count // 2)
    sizes = [end - first for first, end in zip(starts, starts[1:])]
    return pl.pallas_call(
        functools.partial(gram_kernel, ntraits),
        grid_spec=pltpu.PrefetchScalarGridSpec(
            num_scalar_prefetch=1,
            grid=(steps,),
            in_specs=[pl.BlockSpec((tile, nvars), source), pl.BlockSpec((ntraits, tile), traits_source)],
            out_specs=[
                pl.BlockSpec((total // 2, BLK), lambda i, rank_ref: (0, 0)),
                pl.BlockSpec((total // 2, BLK), lambda i, rank_ref: (0, 0)),
                pl.BlockSpec((tile, nvars), lambda i, rank_ref: (jnp.maximum(i - half, 0), 0)),
            ]
            + [pl.BlockSpec((size, nvars), lambda i, rank_ref: (0, 0)) for size in sizes],
            scratch_shapes=[pltpu.VMEM((side_rows(ntraits), nvars), jnp.float32), pltpu.VMEM((ntraits, BLK), jnp.float32)]
            + [pltpu.VMEM((nvars - 2 * BLK * j, 2 * BLK), jnp.float32) for j in range(nvars // (2 * BLK))],
        ),
        out_shape=[jax.ShapeDtypeStruct((total // 2, BLK), jnp.float32)] * 2
        + [jax.ShapeDtypeStruct((size, nvars), jnp.bfloat16) for size in [count // 2] + sizes],
        compiler_params=pltpu.CompilerParams(vmem_limit_bytes=48 * 1024 * 1024),
        name="gram_sums",
    )(place, genotypes, traits)


def solve_kernel(nsamp, ntraits, lam_ref, near_a, near_b, far_a, far_b, *refs):
    coef_ref, mean_ref, aug, wide = refs[-4:]
    nvars = coef_ref.shape[1]
    nblocks = nvars // BLK
    starts, low = panel_rows(nvars)
    tall = side_rows(ntraits)
    lam = lam_ref[0, 0]
    lower = lax.rem(lax.axis_index("samp"), 2) == 0
    quarter = near_a.shape[0]
    pairs = [(near_a, far_a), (near_b, far_b), (far_a, near_a), (far_b, near_b)]

    def read(row, count):
        found = []
        while count > 0:
            place, at = divmod(row, quarter)
            size = min(count, quarter - at)
            even, odd = pairs[place]
            found.append(jnp.where(lower, even[at:at + size, :], odd[at:at + size, :]))
            row, count = row + size, count - size
        return found[0] if len(found) == 1 else jnp.concatenate(found, axis=0)

    eye = lax.broadcasted_iota(jnp.int32, (BLK, BLK), 0) == lax.broadcasted_iota(jnp.int32, (BLK, BLK), 1)
    sides = [read(low + tall * j, tall) for j in range(nblocks)]
    means = [side[ntraits:ntraits + 1, :] / nsamp for side in sides]
    means_down = [down(mean) for mean in means]
    ysum = read(low + tall * nblocks, ntraits)
    for j in range(nblocks):
        span = slice(BLK * j, BLK * (j + 1))
        mean_ref[:, span] = jnp.broadcast_to(means[j], (SUB, BLK))
        for i in range(j, nblocks):
            value = read(starts[j] + BLK * (i - j), BLK) - nsamp * means_down[i] * means[j]
            if i == j:
                value = value + jnp.where(eye, lam * (value / nsamp + 1e-05), 0.0)
            aug[BLK * i:BLK * (i + 1), span] = value
        aug[nvars:nvars + ntraits, span] = sides[j][0:ntraits, :] - ysum * means[j]
    end = nvars + ntraits
    inverse = invert_tile(aug[0:BLK, 0:BLK])
    for k in range(nblocks):
        span = slice(BLK * k, BLK * (k + 1))
        first = BLK * (k + 1)
        panel = aug[first:end, span]
        mult = jnp.dot(as_left(panel), as_right(inverse, 0), preferred_element_type=jnp.float32)
        wide[first:end, span] = mult
        if k == nblocks - 1:
            break
        left, right = as_left(mult), as_right(panel, 1)
        j = k + 1
        while j < nblocks:
            top = BLK * j
            size = BLK if j == k + 1 or j == nblocks - 1 else 2 * BLK
            at = top - first
            aug[top:end, top:top + size] -= lax.dot_general(left[at:, :], right[at:at + size, :], NT, preferred_element_type=jnp.float32)
            if j == k + 1:
                inverse = invert_tile(aug[top:top + BLK, top:top + BLK])
            j += size // BLK
    solved = wide[nvars:end, nvars - BLK:nvars]
    coef_ref[:, nvars - BLK:nvars] = solved.astype(jnp.bfloat16)
    for k in range(nblocks - 2, -1, -1):
        span = slice(BLK * k, BLK * (k + 1))
        found = wide[nvars:end, span] - dot_hi(solved, wide[BLK * (k + 1):nvars, span])
        coef_ref[:, span] = found.astype(jnp.bfloat16)
        solved = jnp.concatenate([found, solved], axis=1)


def solve(pieces, lam, arrived, nsamp, nvars, ntraits):
    return pl.pallas_call(
        functools.partial(solve_kernel, nsamp, ntraits),
        out_shape=[jax.ShapeDtypeStruct((ntraits, nvars), jnp.bfloat16), jax.ShapeDtypeStruct((SUB, nvars), jnp.float32)],
        in_specs=[pl.BlockSpec(memory_space=pltpu.SMEM)]
        + [pl.BlockSpec(memory_space=pltpu.VMEM)] * 4
        + [pl.BlockSpec(memory_space=pl.ANY)] * len(arrived),
        out_specs=[pl.BlockSpec(memory_space=pltpu.VMEM)] * 2,
        scratch_shapes=[
            pltpu.VMEM((nvars + ntraits, nvars), jnp.float32),
            pltpu.VMEM((nvars + ntraits, nvars), jnp.float32),
        ],
        compiler_params=pltpu.CompilerParams(vmem_limit_bytes=48 * 1024 * 1024),
        cost_estimate=pl.CostEstimate(flops=46 * 10**9, bytes_accessed=10**6, transcendentals=0),
        name="ridge_solve",
    )(lam, *pieces, *arrived)


def level_kernel(npen, own_ref, coef_ref, mean_ref, far_mean_ref, traits_ref, *refs):
    rank = lax.axis_index("blk")
    ntraits = coef_ref.shape[2]
    nvars = own_ref.shape[1]
    count = own_ref.shape[0]
    stack = 2 * npen
    tile = 512
    pieces, (out_ref, pred, other_ref) = refs[:-3], refs[-3:]
    low = 0
    for piece in pieces:
        other_ref[low:low + piece.shape[0], :] = piece[...]
        low += piece.shape[0]
    for place in range(2):
        block = rank if place == 0 else 1 - rank
        source = own_ref if place == 0 else other_ref
        mean = (mean_ref if place == 0 else far_mean_ref)[0:1, :]
        coef = jnp.concatenate([coef_ref[r, block] for r in range(npen)], axis=0)
        offset = jnp.sum(coef.astype(jnp.float32) * mean, axis=1, keepdims=True)
        low = pl.multiple_of(block * (npen * ntraits), npen * ntraits)
        for n in range(0, count, tile):
            value = lax.dot_general(coef, source[n:n + tile, :], NT, preferred_element_type=jnp.float32)
            pred[pl.ds(low, npen * ntraits), n:n + tile] = value - offset
    pred[stack * ntraits:(stack + 1) * ntraits, :] = traits_ref[...].astype(jnp.float32)
    lane = lax.broadcasted_iota(jnp.int32, (SUB, BLK), 1)
    for t in range(0, ntraits, SUB):
        acc = jnp.zeros((SUB, BLK), jnp.float32)
        for i in range(stack):
            left = pred[i * ntraits + t:i * ntraits + t + SUB, :]
            for j in range(i, stack + 1):
                term = jnp.sum(left * pred[j * ntraits + t:j * ntraits + t + SUB, :], axis=1, keepdims=True)
                if j < stack:
                    acc = jnp.where((lane == i * stack + j) | (lane == j * stack + i), term, acc)
                else:
                    acc = jnp.where(lane == stack * stack + i, term, acc)
        out_ref[t:t + SUB, :] = acc


def level_sums(own, others, coefs, mean, far_mean, traits, npen):
    ntraits = traits.shape[0]
    count = own.shape[0]
    vmem = pl.BlockSpec(memory_space=pltpu.VMEM)
    return pl.pallas_call(
        functools.partial(level_kernel, npen),
        out_shape=jax.ShapeDtypeStruct((ntraits, BLK), jnp.float32),
        in_specs=[vmem] * (5 + len(others)),
        out_specs=pl.BlockSpec(memory_space=pltpu.VMEM),
        scratch_shapes=[
            pltpu.VMEM(((2 * npen + 1) * ntraits, count), jnp.float32),
            pltpu.VMEM(own.shape, own.dtype),
        ],
        compiler_params=pltpu.CompilerParams(vmem_limit_bytes=56 * 1024 * 1024),
        name="level_sums",
    )(own, coefs, mean, far_mean, traits, *others)


def swapped(x, bit):
    return lax.ppermute(x, "samp", [(i, i ^ (1 << bit)) for i in range(lax.axis_size("samp"))])


def place_bit(bit):
    return lax.rem(lax.div(lax.axis_index("samp"), 1 << bit), 2)


def stack_kernel(near_ref, far_ref, piece_ref, out_ref):
    rank = lax.axis_index("blk")
    out_ref[rank] = near_ref[...]
    out_ref[1 - rank] = far_ref[...]


def stacked(near, far, piece):
    return pl.pallas_call(
        stack_kernel,
        out_shape=jax.ShapeDtypeStruct((2,) + near.shape, near.dtype),
        in_specs=[pl.BlockSpec(memory_space=pltpu.VMEM)] * 2 + [pl.BlockSpec(memory_space=pl.ANY)],
        out_specs=pl.BlockSpec(memory_space=pltpu.VMEM),
        cost_estimate=pl.CostEstimate(flops=10**6, bytes_accessed=10**5, transcendentals=0),
        name="stack_blocks",
    )(near, far, piece)


def halved(x, bit):
    rows = x.shape[0] // 2
    mine = place_bit(bit)
    far = swapped(lax.dynamic_slice_in_dim(x, (1 - mine) * rows, rows, 0), bit)
    return lax.dynamic_slice_in_dim(x, mine * rows, rows, 0) + far


def doubled(x, bit):
    far = swapped(x, bit)
    even = place_bit(bit) == 0
    return jnp.concatenate([jnp.where(even, x, far), jnp.where(even, far, x)], axis=0)


def all_sums(x, away):
    bits = list(range(1, lax.axis_size("samp").bit_length() - 1))
    x = x + swapped(away, 0)
    rows = x.shape[0] // 2
    near = []
    for part, order in ((x[:rows], bits), (x[rows:], bits[1:] + bits[:1])):
        for bit in order:
            part = halved(part, bit)
        for bit in reversed(order):
            part = doubled(part, bit)
        near.append(part)
    return near + [swapped(part, 0) for part in near]


def small_sum(x):
    for bit in range(lax.axis_size("samp").bit_length() - 1):
        x = x + swapped(x, bit)
    return x


def level_from_predictions(coefs, mean, dosage, traits, nvars):
    coef = coefs.transpose(0, 2, 1)
    ntraits = traits.shape[1]
    offset = jnp.einsum("rmt,m->rt", coef.astype(jnp.float32), mean, precision=HI)
    pred = jnp.einsum("rmt,nm->trn", coef, dosage, preferred_element_type=jnp.float32)
    pred = (pred - offset.T[:, :, None]).astype(jnp.bfloat16)
    local_traits = ntraits // lax.axis_size("blk")
    parts = lax.all_to_all(pred[None], "blk", split_axis=1, concat_axis=0, tiled=True)
    mine = lax.dynamic_slice_in_dim(traits, lax.axis_index("blk") * local_traits, local_traits, 1)
    gram = jnp.einsum("btrn,ctsn->tbrcs", parts, parts, preferred_element_type=jnp.float32)
    cross = jnp.einsum("btrn,nt->tbr", parts, mine, preferred_element_type=jnp.float32)
    count, stack = parts.shape[1], parts.shape[0] * parts.shape[2]
    gram, cross = lax.psum((gram.reshape(count, stack, stack), cross.reshape(count, stack)), "samp")
    return gram / nvars, cross / nvars


def local(genotypes, traits, penalty_index):
    count, nvars = genotypes.shape
    ntraits = traits.shape[1]
    npen = penalty_index.shape[0]
    nblk = lax.axis_size("blk")
    members = lax.axis_size("samp")
    nsamp = float(count * members)
    samp_rank = lax.axis_index("samp")
    blk_rank = lax.axis_index("blk")
    paired = nblk == 2
    place = jnp.stack([blk_rank if paired else jnp.int32(0), place_bit(0)])
    turned = traits.T
    near, away, kept, *sent = gram(genotypes, turned, place, members)
    others = [lax.ppermute(piece, "blk", [(0, 1), (1, 0)]) for piece in sent] if paired else []
    pieces = all_sums(near, away)
    lam = nsamp * jnp.exp2((penalty_index.astype(jnp.float32) - 8.0) / 2.0)
    mine = lax.dynamic_index_in_dim(lam, (samp_rank % GROUP) % npen, 0, keepdims=True).reshape(1, 1)
    coef, mean = solve(pieces, mine, others[:1], nsamp, nvars, ntraits)
    groups = [list(range(g, g + GROUP)) for g in range(0, members, GROUP)]
    if not paired:
        coefs = lax.all_gather(coef, "samp", axis_index_groups=groups)[:npen]
        dosage = genotypes.astype(jnp.bfloat16)
        return level_from_predictions(coefs, mean[0], dosage, traits, nvars)
    coef_far = lax.ppermute(coef, "blk", [(0, 1), (1, 0)])
    mean_far = lax.ppermute(mean, "blk", [(0, 1), (1, 0)])
    both = stacked(coef, coef_far, others[1])
    coefs = lax.all_gather(both, "samp", axis_index_groups=groups)
    rows = lax.dynamic_slice_in_dim(turned, blk_rank * (count // 2), count // 2, 1)
    found = level_sums(kept, others, coefs, mean, mean_far, rows, npen)
    stack = nblk * npen
    each = ntraits // nblk
    found = small_sum(found + lax.ppermute(found, "blk", [(0, 1), (1, 0)]))
    found = lax.dynamic_slice_in_dim(found, blk_rank * each, each, 0) / nvars
    return found[:, :stack * stack].reshape(each, stack, stack), found[:, stack * stack:stack * stack + stack]


def solution(mesh):
    placed = (P("samp", "blk"), P("samp", None), P())
    return jax.shard_map(
        local,
        mesh=mesh,
        in_specs=placed,
        out_specs=(P("blk", None, None), P("blk", None)),
        check_vma=False,
    )
```

```python
import functools

import jax
import jax.numpy as jnp
from jax import lax
from jax.experimental import pallas as pl
from jax.experimental.pallas import tpu as pltpu
from jax.sharding import PartitionSpec as P

BLK = 128
SUB = 8
GROUP = 8
HI = lax.Precision.HIGHEST
NT = (((1,), (1,)), ((), ()))
TN = (((0,), (0,)), ((), ()))


def dot_hi(a, b):
    return jnp.dot(a, b, precision=HI, preferred_element_type=jnp.float32)


def dot_nt(a, b):
    return lax.dot_general(a, b, NT, precision=HI, preferred_element_type=jnp.float32)


def panel_rows(nvars):
    starts = [0]
    for j in range(nvars // BLK):
        starts.append(starts[-1] + nvars - BLK * j)
    return starts[:-1], starts[-1]


def side_rows(ntraits):
    return ntraits + SUB


def down(row):
    return jnp.transpose(jnp.broadcast_to(row, (BLK, BLK)))


def inverse_of(x):
    near = pl.reciprocal(x, approx=True)
    return near * (2.0 - x * near)


def split(x):
    first = x.astype(jnp.bfloat16)
    rest = x - first.astype(jnp.float32)
    second = rest.astype(jnp.bfloat16)
    return first, second, (rest - second.astype(jnp.float32)).astype(jnp.bfloat16)


def as_left(x):
    a, b, c = split(x)
    return jnp.concatenate([a, a, b, a, b, c], axis=1)


def as_right(x, axis):
    a, b, c = split(x)
    return jnp.concatenate([a, b, a, c, b, a], axis=axis)


def stack_left(x):
    a, b, c = [part.astype(jnp.float32) for part in split(x)]
    return jnp.concatenate([a, a, b, a, b, c], axis=0).astype(jnp.bfloat16)


def stack_right(x):
    a, b, c = [part.astype(jnp.float32) for part in split(x)]
    return jnp.concatenate([a, b, a, c, b, a], axis=0).astype(jnp.bfloat16)


def invert_tile(tile):
    strips = [tile[SUB * i:SUB * (i + 1), :] for i in range(BLK // SUB)]
    lane = lax.broadcasted_iota(jnp.int32, (SUB, BLK), 1)
    sub = lax.broadcasted_iota(jnp.int32, (SUB, BLK), 0)
    rows_at = [sub == j for j in range(SUB)]
    for k in range(BLK // SUB):
        at = SUB * k
        inside = (lane >= at) & (lane < at + SUB)
        eye = (lane - at == sub).astype(jnp.float32)
        cols = [jnp.broadcast_to(strips[k][:, at + j:at + j + 1], (SUB, BLK)) for j in range(SUB)]
        right = jnp.where(inside, eye, strips[k])
        for j in range(SUB):
            pivot = inverse_of(jnp.broadcast_to(cols[j][j:j + 1, :], (SUB, BLK)))
            step = jnp.where(rows_at[j], -1.0, cols[j])

            def move(x):
                return jnp.where(rows_at[j], 0.0, x) - (step * jnp.broadcast_to(x[j:j + 1, :], (SUB, BLK))) * pivot

            cols = cols[:j + 1] + [move(c) for c in cols[j + 1:]]
            right = move(right)
        mirror = jnp.where(lane < at, -strips[k], jnp.where(inside, 0.0, strips[k]))
        change = lax.dot_general(stack_left(mirror), stack_right(right), TN, preferred_element_type=jnp.float32)
        fresh = []
        for i in range(BLK // SUB):
            rest = jnp.where(inside, 0.0, strips[i])
            if i == k:
                rest = right
            elif i == k + 1:
                for j in range(SUB):
                    factor = jnp.broadcast_to(strips[i][:, at + j:at + j + 1], (SUB, BLK))
                    rest = rest - factor * jnp.broadcast_to(right[j:j + 1, :], (SUB, BLK))
            else:
                rest = rest - change[SUB * i:SUB * (i + 1), :]
            fresh.append(rest)
        strips = fresh
    return jnp.concatenate(strips, axis=0)


def piece_starts(rows):
    return [0, rows // 2, rows]


def gram_kernel(ntraits, rank_ref, geno_ref, traits_ref, near_ref, away_ref, kept_ref, *refs):
    nvars = geno_ref.shape[1]
    step = pl.program_id(0)
    half = pl.num_programs(0) // 2
    wide = 2 * BLK
    pieces, side, ysum, panels = refs[:2], refs[2], refs[3], refs[4:]

    @pl.when(step == 0)
    def _():
        side[...] = jnp.zeros_like(side)
        ysum[...] = jnp.zeros_like(ysum)
        for panel in panels:
            panel[...] = jnp.zeros_like(panel)

    dosage = geno_ref[...].astype(jnp.float32).astype(jnp.bfloat16)

    count = dosage.shape[0]
    for j, panel in enumerate(panels):
        left, right = dosage[:, wide * j:], dosage[:, wide * j:wide * (j + 1)]
        panel[...] += lax.dot_general(left, right, TN, preferred_element_type=jnp.float32)
    traits = traits_ref[...]
    rows = jnp.concatenate([traits, jnp.ones((2 * SUB, count), jnp.bfloat16)], axis=0)
    sums = jnp.dot(rows, dosage, preferred_element_type=jnp.float32)
    side[...] += sums[0:side.shape[0], :]
    ysum[...] += jnp.sum(traits.astype(jnp.float32), axis=1, keepdims=True)

    for tile in range(piece_starts(geno_ref.shape[0] * 2)[-1] // count):
        @pl.when(step == tile)
        def _(tile=tile):
            starts = piece_starts(count * 2)
            for piece, first, end in zip(pieces, starts, starts[1:]):
                low, high = max(first, tile * count), min(end, (tile + 1) * count)
                if low < high:
                    piece[low - first:high - first, :] = dosage[low - tile * count:high - tile * count, :]

    @pl.when(step >= half)
    def _():
        kept_ref[...] = dosage

    def hand_out(even, odd):
        rows = even.shape[0]

        def store(row, value):
            while value.shape[0] > 0:
                place, at = divmod(row, rows)
                size = min(value.shape[0], rows - at)
                (odd if place else even)[at:at + size, :] = value[:size, :]
                row, value = row + size, value[size:, :]

        starts, low = panel_rows(nvars)
        for j, start in enumerate(starts):
            skip = BLK * (j % 2)
            store(start, panels[j // 2][skip:, skip:skip + BLK])
        tall = side_rows(ntraits)
        for j in range(nvars // BLK):
            store(low + tall * j, side[:, BLK * j:BLK * (j + 1)])
        used = low + tall * (nvars // BLK) + ntraits
        store(used - ntraits, ysum[...])
        if used < 2 * rows:
            store(used, jnp.zeros((2 * rows - used, BLK), jnp.float32))

    last = step == pl.num_programs(0) - 1

    @pl.when(last & (rank_ref[1] == 0))
    def _():
        hand_out(near_ref, away_ref)

    @pl.when(last & (rank_ref[1] == 1))
    def _():
        hand_out(away_ref, near_ref)


def gram(genotypes, traits, place, members):
    count, nvars = genotypes.shape
    ntraits = traits.shape[0]
    steps = 4
    tile = count // steps
    half = steps // 2
    low = panel_rows(nvars)[1]
    share = SUB * members
    total = -(-(low + side_rows(ntraits) * (nvars // BLK) + ntraits) // share) * share

    def source(i, place_ref):
        return (lax.rem(i + half * (1 - place_ref[0]), steps), 0)

    def traits_source(i, place_ref):
        return (0, lax.rem(i + half * (1 - place_ref[0]), steps))

    starts = piece_starts(count // 2)
    sizes = [end - first for first, end in zip(starts, starts[1:])]
    return pl.pallas_call(
        functools.partial(gram_kernel, ntraits),
        grid_spec=pltpu.PrefetchScalarGridSpec(
            num_scalar_prefetch=1,
            grid=(steps,),
            in_specs=[pl.BlockSpec((tile, nvars), source), pl.BlockSpec((ntraits, tile), traits_source)],
            out_specs=[
                pl.BlockSpec((total // 2, BLK), lambda i, rank_ref: (0, 0)),
                pl.BlockSpec((total // 2, BLK), lambda i, rank_ref: (0, 0)),
                pl.BlockSpec((tile, nvars), lambda i, rank_ref: (jnp.maximum(i - half, 0), 0)),
            ]
            + [pl.BlockSpec((size, nvars), lambda i, rank_ref: (0, 0)) for size in sizes],
            scratch_shapes=[pltpu.VMEM((side_rows(ntraits), nvars), jnp.float32), pltpu.VMEM((ntraits, BLK), jnp.float32)]
            + [pltpu.VMEM((nvars - 2 * BLK * j, 2 * BLK), jnp.float32) for j in range(nvars // (2 * BLK))],
        ),
        out_shape=[jax.ShapeDtypeStruct((total // 2, BLK), jnp.float32)] * 2
        + [jax.ShapeDtypeStruct((size, nvars), jnp.bfloat16) for size in [count // 2] + sizes],
        compiler_params=pltpu.CompilerParams(vmem_limit_bytes=48 * 1024 * 1024),
        name="gram_sums",
    )(place, genotypes, traits)


def solve_kernel(nsamp, ntraits, lam_ref, near, far, *refs):
    coef_ref, mean_ref, aug, wide = refs[-4:]
    nvars = coef_ref.shape[1]
    nblocks = nvars // BLK
    starts, low = panel_rows(nvars)
    tall = side_rows(ntraits)
    lam = lam_ref[0, 0]
    lower = lax.rem(lax.axis_index("samp"), 2) == 0
    half = near.shape[0]
    pairs = [(near, far), (far, near)]

    def read(row, count):
        found = []
        while count > 0:
            place, at = divmod(row, half)
            size = min(count, half - at)
            even, odd = pairs[place]
            found.append(jnp.where(lower, even[at:at + size, :], odd[at:at + size, :]))
            row, count = row + size, count - size
        return found[0] if len(found) == 1 else jnp.concatenate(found, axis=0)

    eye = lax.broadcasted_iota(jnp.int32, (BLK, BLK), 0) == lax.broadcasted_iota(jnp.int32, (BLK, BLK), 1)
    sides = [read(low + tall * j, tall) for j in range(nblocks)]
    means = [side[ntraits:ntraits + 1, :] / nsamp for side in sides]
    means_down = [down(mean) for mean in means]
    ysum = read(low + tall * nblocks, ntraits)
    for j in range(nblocks):
        span = slice(BLK * j, BLK * (j + 1))
        mean_ref[:, span] = jnp.broadcast_to(means[j], (SUB, BLK))
        for i in range(j, nblocks):
            value = read(starts[j] + BLK * (i - j), BLK) - nsamp * means_down[i] * means[j]
            if i == j:
                value = value + jnp.where(eye, lam * (value / nsamp + 1e-05), 0.0)
            aug[BLK * i:BLK * (i + 1), span] = value
        aug[nvars:nvars + ntraits, span] = sides[j][0:ntraits, :] - ysum * means[j]
    end = nvars + ntraits
    inverse = invert_tile(aug[0:BLK, 0:BLK])
    for k in range(nblocks):
        span = slice(BLK * k, BLK * (k + 1))
        first = BLK * (k + 1)
        panel = aug[first:end, span]
        mult = jnp.dot(as_left(panel), as_right(inverse, 0), preferred_element_type=jnp.float32)
        wide[first:end, span] = mult
        if k == nblocks - 1:
            break
        left, right = as_left(mult), as_right(panel, 1)
        j = k + 1
        while j < nblocks:
            top = BLK * j
            size = BLK if j == k + 1 or j == nblocks - 1 else 2 * BLK
            at = top - first
            aug[top:end, top:top + size] -= lax.dot_general(left[at:, :], right[at:at + size, :], NT, preferred_element_type=jnp.float32)
            if j == k + 1:
                inverse = invert_tile(aug[top:top + BLK, top:top + BLK])
            j += size // BLK
    solved = wide[nvars:end, nvars - BLK:nvars]
    coef_ref[:, nvars - BLK:nvars] = solved.astype(jnp.bfloat16)
    for k in range(nblocks - 2, -1, -1):
        span = slice(BLK * k, BLK * (k + 1))
        found = wide[nvars:end, span] - dot_hi(solved, wide[BLK * (k + 1):nvars, span])
        coef_ref[:, span] = found.astype(jnp.bfloat16)
        solved = jnp.concatenate([found, solved], axis=1)


def solve(pieces, lam, arrived, nsamp, nvars, ntraits):
    return pl.pallas_call(
        functools.partial(solve_kernel, nsamp, ntraits),
        out_shape=[jax.ShapeDtypeStruct((ntraits, nvars), jnp.bfloat16), jax.ShapeDtypeStruct((SUB, nvars), jnp.float32)],
        in_specs=[pl.BlockSpec(memory_space=pltpu.SMEM)]
        + [pl.BlockSpec(memory_space=pltpu.VMEM)] * 2
        + [pl.BlockSpec(memory_space=pl.ANY)] * len(arrived),
        out_specs=[pl.BlockSpec(memory_space=pltpu.VMEM)] * 2,
        scratch_shapes=[
            pltpu.VMEM((nvars + ntraits, nvars), jnp.float32),
            pltpu.VMEM((nvars + ntraits, nvars), jnp.float32),
        ],
        compiler_params=pltpu.CompilerParams(vmem_limit_bytes=48 * 1024 * 1024),
        cost_estimate=pl.CostEstimate(flops=46 * 10**9, bytes_accessed=10**6, transcendentals=0),
        name="ridge_solve",
    )(lam, *pieces, *arrived)


def level_kernel(npen, own_ref, coef_ref, mean_ref, far_mean_ref, traits_ref, *refs):
    rank = lax.axis_index("blk")
    ntraits = coef_ref.shape[2]
    nvars = own_ref.shape[1]
    count = own_ref.shape[0]
    stack = 2 * npen
    tile = 512
    pieces, (out_ref, pred) = refs[:-2], refs[-2:]
    for place in range(2):
        block = rank if place == 0 else 1 - rank
        sources = [own_ref] if place == 0 else pieces
        mean = (mean_ref if place == 0 else far_mean_ref)[0:1, :]
        coef = jnp.concatenate([coef_ref[r, block] for r in range(npen)], axis=0)
        offset = jnp.sum(coef.astype(jnp.float32) * mean, axis=1, keepdims=True)
        low = pl.multiple_of(block * (npen * ntraits), npen * ntraits)
        n = 0
        for source in sources:
            for first in range(0, source.shape[0], tile):
                value = lax.dot_general(coef, source[first:first + tile, :], NT, preferred_element_type=jnp.float32)
                pred[pl.ds(low, npen * ntraits), n:n + tile] = value - offset
                n += tile
    pred[stack * ntraits:(stack + 1) * ntraits, :] = traits_ref[...].astype(jnp.float32)
    lane = lax.broadcasted_iota(jnp.int32, (SUB, BLK), 1)
    for t in range(0, ntraits, SUB):
        acc = jnp.zeros((SUB, BLK), jnp.float32)
        for i in range(stack):
            left = pred[i * ntraits + t:i * ntraits + t + SUB, :]
            for j in range(i, stack + 1):
                term = jnp.sum(left * pred[j * ntraits + t:j * ntraits + t + SUB, :], axis=1, keepdims=True)
                if j < stack:
                    acc = jnp.where((lane == i * stack + j) | (lane == j * stack + i), term, acc)
                else:
                    acc = jnp.where(lane == stack * stack + i, term, acc)
        out_ref[t:t + SUB, :] = acc


def level_sums(own, others, coefs, mean, far_mean, traits, npen):
    ntraits = traits.shape[0]
    count = own.shape[0]
    vmem = pl.BlockSpec(memory_space=pltpu.VMEM)
    return pl.pallas_call(
        functools.partial(level_kernel, npen),
        out_shape=jax.ShapeDtypeStruct((ntraits, BLK), jnp.float32),
        in_specs=[vmem] * (5 + len(others)),
        out_specs=pl.BlockSpec(memory_space=pltpu.VMEM),
        scratch_shapes=[
            pltpu.VMEM(((2 * npen + 1) * ntraits, count), jnp.float32),
        ],
        compiler_params=pltpu.CompilerParams(vmem_limit_bytes=56 * 1024 * 1024),
        name="level_sums",
    )(own, coefs, mean, far_mean, traits, *others)


def swapped(x, pair):
    return lax.ppermute(x, "samp", [(i, i ^ (1 << pair[i % 2])) for i in range(lax.axis_size("samp"))])


def place_bit(pair):
    rank = lax.axis_index("samp")
    unit = jnp.where(lax.rem(rank, 2) == 0, 1 << pair[0], 1 << pair[1])
    return lax.rem(lax.div(rank, unit.astype(rank.dtype)), 2)


def stack_kernel(near_ref, far_ref, piece_ref, out_ref):
    rank = lax.axis_index("blk")
    out_ref[rank] = near_ref[...]
    out_ref[1 - rank] = far_ref[...]


def stacked(near, far, piece):
    return pl.pallas_call(
        stack_kernel,
        out_shape=jax.ShapeDtypeStruct((2,) + near.shape, near.dtype),
        in_specs=[pl.BlockSpec(memory_space=pltpu.VMEM)] * 2 + [pl.BlockSpec(memory_space=pl.ANY)],
        out_specs=pl.BlockSpec(memory_space=pltpu.VMEM),
        cost_estimate=pl.CostEstimate(flops=10**6, bytes_accessed=10**5, transcendentals=0),
        name="stack_blocks",
    )(near, far, piece)


def halved(x, pair):
    rows = x.shape[0] // 2
    mine = place_bit(pair)
    far = swapped(lax.dynamic_slice_in_dim(x, (1 - mine) * rows, rows, 0), pair)
    return lax.dynamic_slice_in_dim(x, mine * rows, rows, 0) + far


def doubled(x, pair):
    far = swapped(x, pair)
    even = place_bit(pair) == 0
    return jnp.concatenate([jnp.where(even, x, far), jnp.where(even, far, x)], axis=0)


def all_sums(x, away):
    bits = list(range(1, lax.axis_size("samp").bit_length() - 1))
    pairs = list(zip(bits, bits[1:] + bits[:1]))
    x = x + swapped(away, (0, 0))
    for pair in pairs:
        x = halved(x, pair)
    for pair in reversed(pairs):
        x = doubled(x, pair)
    return [x, swapped(x, (0, 0))]


def small_sum(x):
    for bit in range(lax.axis_size("samp").bit_length() - 1):
        x = x + swapped(x, (bit, bit))
    return x


def level_from_predictions(coefs, mean, dosage, traits, nvars):
    coef = coefs.transpose(0, 2, 1)
    ntraits = traits.shape[1]
    offset = jnp.einsum("rmt,m->rt", coef.astype(jnp.float32), mean, precision=HI)
    pred = jnp.einsum("rmt,nm->trn", coef, dosage, preferred_element_type=jnp.float32)
    pred = (pred - offset.T[:, :, None]).astype(jnp.bfloat16)
    local_traits = ntraits // lax.axis_size("blk")
    parts = lax.all_to_all(pred[None], "blk", split_axis=1, concat_axis=0, tiled=True)
    mine = lax.dynamic_slice_in_dim(traits, lax.axis_index("blk") * local_traits, local_traits, 1)
    gram = jnp.einsum("btrn,ctsn->tbrcs", parts, parts, preferred_element_type=jnp.float32)
    cross = jnp.einsum("btrn,nt->tbr", parts, mine, preferred_element_type=jnp.float32)
    count, stack = parts.shape[1], parts.shape[0] * parts.shape[2]
    gram, cross = lax.psum((gram.reshape(count, stack, stack), cross.reshape(count, stack)), "samp")
    return gram / nvars, cross / nvars


def local(genotypes, traits, penalty_index):
    count, nvars = genotypes.shape
    ntraits = traits.shape[1]
    npen = penalty_index.shape[0]
    nblk = lax.axis_size("blk")
    members = lax.axis_size("samp")
    nsamp = float(count * members)
    samp_rank = lax.axis_index("samp")
    blk_rank = lax.axis_index("blk")
    paired = nblk == 2
    place = jnp.stack([blk_rank if paired else jnp.int32(0), place_bit((0, 0))])
    turned = traits.T
    near, away, kept, *sent = gram(genotypes, turned, place, members)
    others = [lax.ppermute(piece, "blk", [(0, 1), (1, 0)]) for piece in sent] if paired else []
    pieces = all_sums(near, away)
    lam = nsamp * jnp.exp2((penalty_index.astype(jnp.float32) - 8.0) / 2.0)
    mine = lax.dynamic_index_in_dim(lam, (samp_rank % GROUP) % npen, 0, keepdims=True).reshape(1, 1)
    coef, mean = solve(pieces, mine, others[:1], nsamp, nvars, ntraits)
    groups = [list(range(g, g + GROUP)) for g in range(0, members, GROUP)]
    if not paired:
        coefs = lax.all_gather(coef, "samp", axis_index_groups=groups)[:npen]
        dosage = genotypes.astype(jnp.bfloat16)
        return level_from_predictions(coefs, mean[0], dosage, traits, nvars)
    coef_far = lax.ppermute(coef, "blk", [(0, 1), (1, 0)])
    mean_far = lax.ppermute(mean, "blk", [(0, 1), (1, 0)])
    both = stacked(coef, coef_far, others[1])
    coefs = lax.all_gather(both, "samp", axis_index_groups=groups)
    rows = lax.dynamic_slice_in_dim(turned, blk_rank * (count // 2), count // 2, 1)
    found = level_sums(kept, others, coefs, mean, mean_far, rows, npen)
    stack = nblk * npen
    each = ntraits // nblk
    found = small_sum(found + lax.ppermute(found, "blk", [(0, 1), (1, 0)]))
    found = lax.dynamic_slice_in_dim(found, blk_rank * each, each, 0) / nvars
    return found[:, :stack * stack].reshape(each, stack, stack), found[:, stack * stack:stack * stack + stack]


def solution(mesh):
    placed = (P("samp", "blk"), P("samp", None), P())
    return jax.shard_map(
        local,
        mesh=mesh,
        in_specs=placed,
        out_specs=(P("blk", None, None), P("blk", None)),
        check_vma=False,
    )
```

```python
import functools

import jax
import jax.numpy as jnp
from jax import lax
from jax.experimental import pallas as pl
from jax.experimental.pallas import tpu as pltpu
from jax.sharding import PartitionSpec as P

BLK = 128
SUB = 8
GROUP = 8
HI = lax.Precision.HIGHEST
NT = (((1,), (1,)), ((), ()))
TN = (((0,), (0,)), ((), ()))


def dot_hi(a, b):
    return jnp.dot(a, b, precision=HI, preferred_element_type=jnp.float32)


def dot_nt(a, b):
    return lax.dot_general(a, b, NT, precision=HI, preferred_element_type=jnp.float32)


def panel_rows(nvars):
    starts = [0]
    for j in range(nvars // BLK):
        starts.append(starts[-1] + nvars - BLK * j)
    return starts[:-1], starts[-1]


def side_rows(ntraits):
    return ntraits + SUB


def down(row):
    return jnp.transpose(jnp.broadcast_to(row, (BLK, BLK)))


def inverse_of(x):
    near = pl.reciprocal(x, approx=True)
    return near * (2.0 - x * near)


def split(x):
    first = x.astype(jnp.bfloat16)
    rest = x - first.astype(jnp.float32)
    second = rest.astype(jnp.bfloat16)
    return first, second, (rest - second.astype(jnp.float32)).astype(jnp.bfloat16)


def as_left(x):
    a, b, c = split(x)
    return jnp.concatenate([a, a, b, a, b, c], axis=1)


def as_right(x, axis):
    a, b, c = split(x)
    return jnp.concatenate([a, b, a, c, b, a], axis=axis)


def stack_left(x):
    a, b, c = [part.astype(jnp.float32) for part in split(x)]
    return jnp.concatenate([a, a, b, a, b, c], axis=0).astype(jnp.bfloat16)


def stack_right(x):
    a, b, c = [part.astype(jnp.float32) for part in split(x)]
    return jnp.concatenate([a, b, a, c, b, a], axis=0).astype(jnp.bfloat16)


def invert_tile(tile):
    strips = [tile[SUB * i:SUB * (i + 1), :] for i in range(BLK // SUB)]
    lane = lax.broadcasted_iota(jnp.int32, (SUB, BLK), 1)
    sub = lax.broadcasted_iota(jnp.int32, (SUB, BLK), 0)
    rows_at = [sub == j for j in range(SUB)]
    for k in range(BLK // SUB):
        at = SUB * k
        inside = (lane >= at) & (lane < at + SUB)
        eye = (lane - at == sub).astype(jnp.float32)
        cols = [jnp.broadcast_to(strips[k][:, at + j:at + j + 1], (SUB, BLK)) for j in range(SUB)]
        right = jnp.where(inside, eye, strips[k])
        for j in range(SUB):
            pivot = inverse_of(jnp.broadcast_to(cols[j][j:j + 1, :], (SUB, BLK)))
            step = jnp.where(rows_at[j], -1.0, cols[j])

            def move(x):
                return jnp.where(rows_at[j], 0.0, x) - (step * jnp.broadcast_to(x[j:j + 1, :], (SUB, BLK))) * pivot

            cols = cols[:j + 1] + [move(c) for c in cols[j + 1:]]
            right = move(right)
        mirror = jnp.where(lane < at, -strips[k], jnp.where(inside, 0.0, strips[k]))
        change = lax.dot_general(stack_left(mirror), stack_right(right), TN, preferred_element_type=jnp.float32)
        fresh = []
        for i in range(BLK // SUB):
            rest = jnp.where(inside, 0.0, strips[i])
            if i == k:
                rest = right
            elif i == k + 1:
                for j in range(SUB):
                    factor = jnp.broadcast_to(strips[i][:, at + j:at + j + 1], (SUB, BLK))
                    rest = rest - factor * jnp.broadcast_to(right[j:j + 1, :], (SUB, BLK))
            else:
                rest = rest - change[SUB * i:SUB * (i + 1), :]
            fresh.append(rest)
        strips = fresh
    return jnp.concatenate(strips, axis=0)


def piece_starts(rows):
    return [0, rows * 17 // 32, rows]


def gram_kernel(ntraits, rank_ref, geno_ref, traits_ref, near_ref, away_ref, kept_ref, *refs):
    nvars = geno_ref.shape[1]
    step = pl.program_id(0)
    half = pl.num_programs(0) // 2
    wide = 2 * BLK
    pieces, side, ysum, panels = refs[:2], refs[2], refs[3], refs[4:]

    @pl.when(step == 0)
    def _():
        side[...] = jnp.zeros_like(side)
        ysum[...] = jnp.zeros_like(ysum)
        for panel in panels:
            panel[...] = jnp.zeros_like(panel)

    dosage = geno_ref[...].astype(jnp.float32).astype(jnp.bfloat16)

    count = dosage.shape[0]
    for j, panel in enumerate(panels):
        left, right = dosage[:, wide * j:], dosage[:, wide * j:wide * (j + 1)]
        panel[...] += lax.dot_general(left, right, TN, preferred_element_type=jnp.float32)
    traits = traits_ref[...]
    rows = jnp.concatenate([traits, jnp.ones((2 * SUB, count), jnp.bfloat16)], axis=0)
    sums = jnp.dot(rows, dosage, preferred_element_type=jnp.float32)
    side[...] += sums[0:side.shape[0], :]
    ysum[...] += jnp.sum(traits.astype(jnp.float32), axis=1, keepdims=True)

    for tile in range(piece_starts(geno_ref.shape[0] * 2)[-1] // count):
        @pl.when(step == tile)
        def _(tile=tile):
            starts = piece_starts(count * 2)
            for piece, first, end in zip(pieces, starts, starts[1:]):
                low, high = max(first, tile * count), min(end, (tile + 1) * count)
                if low < high:
                    piece[low - first:high - first, :] = dosage[low - tile * count:high - tile * count, :]

    @pl.when(step >= half)
    def _():
        kept_ref[...] = dosage

    def hand_out(even, odd):
        rows = even.shape[0]

        def store(row, value):
            while value.shape[0] > 0:
                place, at = divmod(row, rows)
                size = min(value.shape[0], rows - at)
                (odd if place else even)[at:at + size, :] = value[:size, :]
                row, value = row + size, value[size:, :]

        starts, low = panel_rows(nvars)
        for j, start in enumerate(starts):
            skip = BLK * (j % 2)
            store(start, panels[j // 2][skip:, skip:skip + BLK])
        tall = side_rows(ntraits)
        for j in range(nvars // BLK):
            store(low + tall * j, side[:, BLK * j:BLK * (j + 1)])
        used = low + tall * (nvars // BLK) + ntraits
        store(used - ntraits, ysum[...])
        if used < 2 * rows:
            store(used, jnp.zeros((2 * rows - used, BLK), jnp.float32))

    last = step == pl.num_programs(0) - 1

    @pl.when(last & (rank_ref[1] == 0))
    def _():
        hand_out(near_ref, away_ref)

    @pl.when(last & (rank_ref[1] == 1))
    def _():
        hand_out(away_ref, near_ref)


def gram(genotypes, traits, place, members):
    count, nvars = genotypes.shape
    ntraits = traits.shape[0]
    steps = 4
    tile = count // steps
    half = steps // 2
    low = panel_rows(nvars)[1]
    share = 2 * SUB * members
    total = -(-(low + side_rows(ntraits) * (nvars // BLK) + ntraits) // share) * share

    def source(i, place_ref):
        return (lax.rem(i + half * (1 - place_ref[0]), steps), 0)

    def traits_source(i, place_ref):
        return (0, lax.rem(i + half * (1 - place_ref[0]), steps))

    starts = piece_starts(count // 2)
    sizes = [end - first for first, end in zip(starts, starts[1:])]
    return pl.pallas_call(
        functools.partial(gram_kernel, ntraits),
        grid_spec=pltpu.PrefetchScalarGridSpec(
            num_scalar_prefetch=1,
            grid=(steps,),
            in_specs=[pl.BlockSpec((tile, nvars), source), pl.BlockSpec((ntraits, tile), traits_source)],
            out_specs=[
                pl.BlockSpec((total // 2, BLK), lambda i, rank_ref: (0, 0)),
                pl.BlockSpec((total // 2, BLK), lambda i, rank_ref: (0, 0)),
                pl.BlockSpec((tile, nvars), lambda i, rank_ref: (jnp.maximum(i - half, 0), 0)),
            ]
            + [pl.BlockSpec((size, nvars), lambda i, rank_ref: (0, 0)) for size in sizes],
            scratch_shapes=[pltpu.VMEM((side_rows(ntraits), nvars), jnp.float32), pltpu.VMEM((ntraits, BLK), jnp.float32)]
            + [pltpu.VMEM((nvars - 2 * BLK * j, 2 * BLK), jnp.float32) for j in range(nvars // (2 * BLK))],
        ),
        out_shape=[jax.ShapeDtypeStruct((total // 2, BLK), jnp.float32)] * 2
        + [jax.ShapeDtypeStruct((size, nvars), jnp.bfloat16) for size in [count // 2] + sizes],
        compiler_params=pltpu.CompilerParams(vmem_limit_bytes=48 * 1024 * 1024),
        name="gram_sums",
    )(place, genotypes, traits)


def solve_kernel(nsamp, ntraits, lam_ref, near_a, near_b, far_a, far_b, *refs):
    coef_ref, mean_ref, aug, wide = refs[-4:]
    nvars = coef_ref.shape[1]
    nblocks = nvars // BLK
    starts, low = panel_rows(nvars)
    tall = side_rows(ntraits)
    lam = lam_ref[0, 0]
    lower = lax.rem(lax.axis_index("samp"), 2) == 0
    quarter = near_a.shape[0]
    pairs = [(near_a, far_a), (near_b, far_b), (far_a, near_a), (far_b, near_b)]

    def read(row, count):
        found = []
        while count > 0:
            place, at = divmod(row, quarter)
            size = min(count, quarter - at)
            even, odd = pairs[place]
            found.append(jnp.where(lower, even[at:at + size, :], odd[at:at + size, :]))
            row, count = row + size, count - size
        return found[0] if len(found) == 1 else jnp.concatenate(found, axis=0)

    eye = lax.broadcasted_iota(jnp.int32, (BLK, BLK), 0) == lax.broadcasted_iota(jnp.int32, (BLK, BLK), 1)
    sides = [read(low + tall * j, tall) for j in range(nblocks)]
    means = [side[ntraits:ntraits + 1, :] / nsamp for side in sides]
    means_down = [down(mean) for mean in means]
    ysum = read(low + tall * nblocks, ntraits)
    for j in range(nblocks):
        span = slice(BLK * j, BLK * (j + 1))
        mean_ref[:, span] = jnp.broadcast_to(means[j], (SUB, BLK))
        for i in range(j, nblocks):
            value = read(starts[j] + BLK * (i - j), BLK) - nsamp * means_down[i] * means[j]
            if i == j:
                value = value + jnp.where(eye, lam * (value / nsamp + 1e-05), 0.0)
            aug[BLK * i:BLK * (i + 1), span] = value
        aug[nvars:nvars + ntraits, span] = sides[j][0:ntraits, :] - ysum * means[j]
    end = nvars + ntraits
    inverse = invert_tile(aug[0:BLK, 0:BLK])
    for k in range(nblocks):
        span = slice(BLK * k, BLK * (k + 1))
        first = BLK * (k + 1)
        panel = aug[first:end, span]
        mult = jnp.dot(as_left(panel), as_right(inverse, 0), preferred_element_type=jnp.float32)
        wide[first:end, span] = mult
        if k == nblocks - 1:
            break
        left, right = as_left(mult), as_right(panel, 1)
        j = k + 1
        while j < nblocks:
            top = BLK * j
            size = BLK if j == k + 1 or j == nblocks - 1 else 2 * BLK
            at = top - first
            aug[top:end, top:top + size] -= lax.dot_general(left[at:, :], right[at:at + size, :], NT, preferred_element_type=jnp.float32)
            if j == k + 1:
                inverse = invert_tile(aug[top:top + BLK, top:top + BLK])
            j += size // BLK
    left_over = wide[nvars:end, :]
    for k in range(nblocks - 1, -1, -1):
        low_k = BLK * k
        found = left_over[:, low_k:]
        coef_ref[:, low_k:low_k + BLK] = found.astype(jnp.bfloat16)
        if k > 0:
            rows = as_right(wide[low_k:low_k + BLK, 0:low_k], 0)
            left_over = left_over[:, 0:low_k] - jnp.dot(as_left(found), rows, preferred_element_type=jnp.float32)


def solve(pieces, lam, arrived, nsamp, nvars, ntraits):
    return pl.pallas_call(
        functools.partial(solve_kernel, nsamp, ntraits),
        out_shape=[jax.ShapeDtypeStruct((ntraits, nvars), jnp.bfloat16), jax.ShapeDtypeStruct((SUB, nvars), jnp.float32)],
        in_specs=[pl.BlockSpec(memory_space=pltpu.SMEM)]
        + [pl.BlockSpec(memory_space=pltpu.VMEM)] * 4
        + [pl.BlockSpec(memory_space=pl.ANY)] * len(arrived),
        out_specs=[pl.BlockSpec(memory_space=pltpu.VMEM)] * 2,
        scratch_shapes=[
            pltpu.VMEM((nvars + ntraits, nvars), jnp.float32),
            pltpu.VMEM((nvars + ntraits, nvars), jnp.float32),
        ],
        compiler_params=pltpu.CompilerParams(vmem_limit_bytes=48 * 1024 * 1024),
        cost_estimate=pl.CostEstimate(flops=46 * 10**9, bytes_accessed=10**6, transcendentals=0),
        name="ridge_solve",
    )(lam, *pieces, *arrived)


def level_kernel(npen, own_ref, coef_ref, mean_ref, far_mean_ref, traits_ref, *refs):
    rank = lax.axis_index("blk")
    ntraits = coef_ref.shape[2]
    nvars = own_ref.shape[1]
    count = own_ref.shape[0]
    stack = 2 * npen
    tile = 512
    pieces, (out_ref, pred, other_ref) = refs[:-3], refs[-3:]
    low = 0
    for piece in pieces:
        other_ref[low:low + piece.shape[0], :] = piece[...]
        low += piece.shape[0]
    for place in range(2):
        block = rank if place == 0 else 1 - rank
        source = own_ref if place == 0 else other_ref
        mean = (mean_ref if place == 0 else far_mean_ref)[0:1, :]
        coef = jnp.concatenate([coef_ref[r, block] for r in range(npen)], axis=0)
        offset = jnp.sum(coef.astype(jnp.float32) * mean, axis=1, keepdims=True)
        low = pl.multiple_of(block * (npen * ntraits), npen * ntraits)
        for n in range(0, count, tile):
            value = lax.dot_general(coef, source[n:n + tile, :], NT, preferred_element_type=jnp.float32)
            pred[pl.ds(low, npen * ntraits), n:n + tile] = value - offset
    pred[stack * ntraits:(stack + 1) * ntraits, :] = traits_ref[...].astype(jnp.float32)
    lane = lax.broadcasted_iota(jnp.int32, (SUB, BLK), 1)
    for t in range(0, ntraits, SUB):
        acc = jnp.zeros((SUB, BLK), jnp.float32)
        for i in range(stack):
            left = pred[i * ntraits + t:i * ntraits + t + SUB, :]
            for j in range(i, stack + 1):
                term = jnp.sum(left * pred[j * ntraits + t:j * ntraits + t + SUB, :], axis=1, keepdims=True)
                if j < stack:
                    acc = jnp.where((lane == i * stack + j) | (lane == j * stack + i), term, acc)
                else:
                    acc = jnp.where(lane == stack * stack + i, term, acc)
        out_ref[t:t + SUB, :] = acc


def level_sums(own, others, coefs, mean, far_mean, traits, npen):
    ntraits = traits.shape[0]
    count = own.shape[0]
    vmem = pl.BlockSpec(memory_space=pltpu.VMEM)
    return pl.pallas_call(
        functools.partial(level_kernel, npen),
        out_shape=jax.ShapeDtypeStruct((ntraits, BLK), jnp.float32),
        in_specs=[vmem] * (5 + len(others)),
        out_specs=pl.BlockSpec(memory_space=pltpu.VMEM),
        scratch_shapes=[
            pltpu.VMEM(((2 * npen + 1) * ntraits, count), jnp.float32),
            pltpu.VMEM(own.shape, own.dtype),
        ],
        compiler_params=pltpu.CompilerParams(vmem_limit_bytes=56 * 1024 * 1024),
        name="level_sums",
    )(own, coefs, mean, far_mean, traits, *others)


def swapped(x, bit):
    return lax.ppermute(x, "samp", [(i, i ^ (1 << bit)) for i in range(lax.axis_size("samp"))])


def place_bit(bit):
    return lax.rem(lax.div(lax.axis_index("samp"), 1 << bit), 2)


def stack_kernel(near_ref, far_ref, piece_ref, out_ref):
    rank = lax.axis_index("blk")
    out_ref[rank] = near_ref[...]
    out_ref[1 - rank] = far_ref[...]


def stacked(near, far, piece):
    return pl.pallas_call(
        stack_kernel,
        out_shape=jax.ShapeDtypeStruct((2,) + near.shape, near.dtype),
        in_specs=[pl.BlockSpec(memory_space=pltpu.VMEM)] * 2 + [pl.BlockSpec(memory_space=pl.ANY)],
        out_specs=pl.BlockSpec(memory_space=pltpu.VMEM),
        cost_estimate=pl.CostEstimate(flops=10**6, bytes_accessed=10**5, transcendentals=0),
        name="stack_blocks",
    )(near, far, piece)


def halved(x, bit):
    rows = x.shape[0] // 2
    mine = place_bit(bit)
    far = swapped(lax.dynamic_slice_in_dim(x, (1 - mine) * rows, rows, 0), bit)
    return lax.dynamic_slice_in_dim(x, mine * rows, rows, 0) + far


def doubled(x, bit):
    far = swapped(x, bit)
    even = place_bit(bit) == 0
    return jnp.concatenate([jnp.where(even, x, far), jnp.where(even, far, x)], axis=0)


def all_sums(x, away):
    bits = list(range(1, lax.axis_size("samp").bit_length() - 1))
    x = x + swapped(away, 0)
    rows = x.shape[0] // 2
    near = []
    for part, order in ((x[:rows], bits), (x[rows:], bits[1:] + bits[:1])):
        for bit in order:
            part = halved(part, bit)
        for bit in reversed(order):
            part = doubled(part, bit)
        near.append(part)
    return near + [swapped(part, 0) for part in near]


def small_sum(x):
    for bit in range(lax.axis_size("samp").bit_length() - 1):
        x = x + swapped(x, bit)
    return x


def level_from_predictions(coefs, mean, dosage, traits, nvars):
    coef = coefs.transpose(0, 2, 1)
    ntraits = traits.shape[1]
    offset = jnp.einsum("rmt,m->rt", coef.astype(jnp.float32), mean, precision=HI)
    pred = jnp.einsum("rmt,nm->trn", coef, dosage, preferred_element_type=jnp.float32)
    pred = (pred - offset.T[:, :, None]).astype(jnp.bfloat16)
    local_traits = ntraits // lax.axis_size("blk")
    parts = lax.all_to_all(pred[None], "blk", split_axis=1, concat_axis=0, tiled=True)
    mine = lax.dynamic_slice_in_dim(traits, lax.axis_index("blk") * local_traits, local_traits, 1)
    gram = jnp.einsum("btrn,ctsn->tbrcs", parts, parts, preferred_element_type=jnp.float32)
    cross = jnp.einsum("btrn,nt->tbr", parts, mine, preferred_element_type=jnp.float32)
    count, stack = parts.shape[1], parts.shape[0] * parts.shape[2]
    gram, cross = lax.psum((gram.reshape(count, stack, stack), cross.reshape(count, stack)), "samp")
    return gram / nvars, cross / nvars


def local(genotypes, traits, penalty_index):
    count, nvars = genotypes.shape
    ntraits = traits.shape[1]
    npen = penalty_index.shape[0]
    nblk = lax.axis_size("blk")
    members = lax.axis_size("samp")
    nsamp = float(count * members)
    samp_rank = lax.axis_index("samp")
    blk_rank = lax.axis_index("blk")
    paired = nblk == 2
    place = jnp.stack([blk_rank if paired else jnp.int32(0), place_bit(0)])
    turned = traits.T
    near, away, kept, *sent = gram(genotypes, turned, place, members)
    others = [lax.ppermute(piece, "blk", [(0, 1), (1, 0)]) for piece in sent] if paired else []
    pieces = all_sums(near, away)
    lam = nsamp * jnp.exp2((penalty_index.astype(jnp.float32) - 8.0) / 2.0)
    mine = lax.dynamic_index_in_dim(lam, (samp_rank % GROUP) % npen, 0, keepdims=True).reshape(1, 1)
    coef, mean = solve(pieces, mine, others[:1], nsamp, nvars, ntraits)
    groups = [list(range(g, g + GROUP)) for g in range(0, members, GROUP)]
    if not paired:
        coefs = lax.all_gather(coef, "samp", axis_index_groups=groups)[:npen]
        dosage = genotypes.astype(jnp.bfloat16)
        return level_from_predictions(coefs, mean[0], dosage, traits, nvars)
    coef_far = lax.ppermute(coef, "blk", [(0, 1), (1, 0)])
    mean_far = lax.ppermute(mean, "blk", [(0, 1), (1, 0)])
    both = stacked(coef, coef_far, others[1])
    coefs = lax.all_gather(both, "samp", axis_index_groups=groups)
    rows = lax.dynamic_slice_in_dim(turned, blk_rank * (count // 2), count // 2, 1)
    found = level_sums(kept, others, coefs, mean, mean_far, rows, npen)
    stack = nblk * npen
    each = ntraits // nblk
    found = small_sum(found + lax.ppermute(found, "blk", [(0, 1), (1, 0)]))
    found = lax.dynamic_slice_in_dim(found, blk_rank * each, each, 0) / nvars
    return found[:, :stack * stack].reshape(each, stack, stack), found[:, stack * stack:stack * stack + stack]


def solution(mesh):
    placed = (P("samp", "blk"), P("samp", None), P())
    return jax.shard_map(
        local,
        mesh=mesh,
        in_specs=placed,
        out_specs=(P("blk", None, None), P("blk", None)),
        check_vma=False,
    )
```
